128 devices in a mesh: seq: 16 (over x, z), head: 8 (over y, core).
Axes of the slice: x: 4, y: 4, z: 4, core: 2. Of those that a mesh axis runs over, the one named last changes fastest.
Arguments:
- queries: bfloat16 [65536, 16, 128], P(('seq', 'head'))
- keys: bfloat16 [65536, 4, 128], P('seq')
- values: bfloat16 [65536, 4, 128], P('seq')
- refine_owner: int32 [512, 4], P('seq'), may hold values from 0 to 15, all different within a row; in each aligned block of 32 rows (0 to 31, 32 to 63, ...) at most 16 rows name the same one
- refine_local: int32 [512, 4], P('seq'), may hold values from 0 to 31
Outputs:
- attended: bfloat16 [65536, 16, 128], P('seq', 'head')
The draws below stay inside these ranges and needn't reach their ends.
Inputs may be any that keep to these rules, and one draw needn't show every extreme that they name: `refine_owner`: in each row the 4 entries differ. In the rows of one device (aligned blocks of 32 rows) no value is named more than 16 times.
All inputs are finite; a program needn't handle non-finite values.
Results may differ from the reference program's by a relative error of at most 0.008.
Values may be sent and summed in bfloat16 or wider, within the bound.
A program may use at most 128 MiB of HBM per device.

```python
import math
import jax
import jax.numpy as jnp
import numpy as np
from jax import lax

QHEADS = 16
KVH = 4
HD = 128
BLK = 128
REFINE = 4
TOKENS = 65536
QB_DEV = 32
NBLK = 512
CAP = 16
N_SEQ = 16


def key_base(key):
    first_key, second_key = jax.random.split(jax.random.fold_in(key, 101))
    block_part = jax.random.normal(first_key, (NBLK, KVH, HD), jnp.float32)
    token_part = jax.random.normal(second_key, (TOKENS, KVH, HD), jnp.float32)
    return jnp.repeat(block_part, BLK, axis=0) + token_part


def draw_keys(key, part):
    base = key_base(key)
    return base.astype(jnp.bfloat16)


def draw_queries(key, part):
    key = jax.random.fold_in(key, 5)
    first_key, second_key = jax.random.split(key)
    block_part = jax.random.normal(first_key, (NBLK, QHEADS, HD), jnp.float32)
    token_part = 2.0 * jax.random.normal(second_key, (TOKENS, QHEADS, HD), jnp.float32)
    result = jnp.repeat(block_part, BLK, axis=0) + token_part
    return result.astype(jnp.bfloat16)


def draw_values(key, part):
    key = jax.random.fold_in(key, 7)
    first_key, second_key = jax.random.split(key, 2)
    block_part = jax.random.normal(first_key, (NBLK, KVH, HD), jnp.float32)
    token_part = jax.random.normal(second_key, (TOKENS, KVH, HD), jnp.float32)
    result = jnp.repeat(block_part, BLK, axis=0) + token_part
    return result.astype(jnp.bfloat16)


def touch_ends(drawn, rng, smallest, top_value):
    longest = drawn.shape.index(max(drawn.shape))
    spots = []
    for shift in (0, 1):
        where = [jax.random.randint(jax.random.fold_in(rng, axis), (), 0, length) for axis, length in enumerate(drawn.shape)]
        where[longest] = (where[longest] + shift) % drawn.shape[longest]
        spots.append(tuple(where))
    return drawn.at[spots[0]].set(smallest).at[spots[1]].set(top_value)


def deal_out(rng, own, number, rows, count, top, bound, slope):
    order = jax.random.permutation(rng, count)
    crowded, common = portions_of(count, rows * top, bound, slope, True), portions_of(count, rows * top, bound, slope, False)
    places = jnp.arange(count)

    def named(sizes, turn):
        used = int((sizes > 0).sum())
        fixed = max(1, used // 4)
        shifted = fixed + (places - fixed + turn * (used - fixed)) % max(1, count - fixed)
        return jnp.zeros((count,), jnp.int32).at[order[jnp.where(places < fixed, places, shifted)]].set(jnp.asarray(sizes, jnp.int32))

    sizes = jnp.where(number % 4 == 0, named(crowded, number // 4), named(common, number - number // 4 - 1))
    mixed = jax.random.permutation(jax.random.fold_in(own, 3), count)
    donor, sink = mixed[0:count // 2 * 2:2], mixed[1:count // 2 * 2:2]
    room = jnp.minimum(sizes[donor] - 1, bound - sizes[sink]) // 2
    room = jnp.where((donor == order[0]) | (sink == order[0]) | (sizes[sink] == 0), 0, jnp.maximum(room, 0))
    shifted = jax.random.randint(jax.random.fold_in(own, 4), (count // 2,), 0, 1 << 20) % (room + 1)
    sizes = sizes.at[donor].add(-shifted).at[sink].add(shifted)
    members = jnp.searchsorted(jnp.cumsum(sizes), jnp.arange(rows * top), side="right").astype(jnp.int32)
    table = members.reshape(top, rows).T
    table = table[jax.random.permutation(jax.random.fold_in(own, 1), rows)]
    turn = jax.random.randint(jax.random.fold_in(own, 2), (rows, 1), 0, top)
    return jnp.take_along_axis(table, (jnp.arange(top)[None, :] + turn) % top, axis=1)


def portions_of(count, total, reach, skew, full):
    weights = [(1 << 20) // math.isqrt(grade ** skew) + 1 for grade in range(1, count + 1)]
    largest = reach if full else min(reach, max(-(-total // count), total * weights[0] // sum(weights)))
    least = 1 if total - largest >= count - 1 else 0
    holding, rest = [largest] + [least] * (count - 1), total - largest - least * (count - 1)
    while rest > 0:
        free = [i for i in range(1, count) if holding[i] < largest] or [i for i in range(1, count) if holding[i] < reach]
        pool, remaining = sum([weights[i] for i in free]), rest
        for i in free:
            addition = min(reach - holding[i], max(1, remaining * weights[i] // pool), rest)
            holding[i] = holding[i] + addition
            rest = rest - addition
    return np.array(holding)


def setup_inputs(seed: int = 0) -> dict:
    key_list = jax.random.split(jax.random.key(seed), 6)
    queries = draw_queries(jax.random.fold_in(key_list[5], 71), 0)
    keys = draw_keys(jax.random.fold_in(key_list[5], 71), 0)
    values = draw_values(jax.random.fold_in(key_list[5], 71), 0)
    refine_owner_keys = jax.random.split(jax.random.fold_in(key_list[3], 1), NBLK // QB_DEV)
    refine_owner_turns = jax.random.permutation(jax.random.fold_in(key_list[3], 3), NBLK // QB_DEV)
    refine_owner = jax.vmap(lambda own, number: deal_out(jax.random.fold_in(key_list[3], 2), own, number, QB_DEV, N_SEQ, REFINE, CAP, 2))(refine_owner_keys, refine_owner_turns).reshape((NBLK, REFINE))
    refine_local = touch_ends(jax.random.randint(key_list[4], (NBLK, REFINE), 0, QB_DEV), jax.random.fold_in(key_list[4], 1), 0, QB_DEV - 1).astype(jnp.int32)
    return dict(queries=queries, keys=keys, values=values, refine_owner=refine_owner, refine_local=refine_local)


def reference(queries, keys, values, refine_owner, refine_local):
    score_scale = HD ** -0.5
    group_size = QHEADS // KVH
    key_blocks = keys.reshape(NBLK, BLK, KVH, HD)
    value_blocks = values.reshape(NBLK, BLK, KVH, HD)
    key_means = jnp.mean(key_blocks, axis=1, dtype=jnp.float32).astype(jnp.bfloat16)
    value_means = jnp.mean(value_blocks, axis=1, dtype=jnp.float32).astype(jnp.bfloat16)
    key_means_f = key_means.astype(jnp.float32)
    value_means_f = value_means.astype(jnp.float32)
    own_block = jnp.arange(NBLK, dtype=jnp.int32)[:, None]
    listed = (refine_owner * QB_DEV + refine_local).astype(jnp.int32)
    refined = jnp.concatenate([own_block, listed], axis=1)
    block_iota = jnp.arange(NBLK, dtype=jnp.int32)

    def per_block(packed):
        query_block, block_ids = packed
        query_f = query_block.astype(jnp.float32).reshape(BLK, KVH, group_size, HD)
        query_means = jnp.mean(query_f, axis=0)
        coarse = jnp.einsum("kgd,jkd->kgj", query_means, key_means_f, precision=lax.Precision.HIGHEST) * score_scale + math.log(BLK)
        excluded = jnp.any(block_ids[:, None] == block_iota[None, :], axis=0)
        coarse = jnp.where(excluded[None, None, :], -1e30, coarse)
        fine_keys = key_blocks[block_ids].reshape((REFINE + 1) * BLK, KVH, HD).astype(jnp.float32)
        fine_values = value_blocks[block_ids].reshape((REFINE + 1) * BLK, KVH, HD).astype(jnp.float32)
        fine = jnp.einsum("tkgd,ukd->tkgu", query_f, fine_keys) * score_scale
        row_max = jnp.maximum(jnp.max(coarse, axis=-1)[None], jnp.max(fine, axis=-1))
        coarse_weights = jnp.where(excluded[None, None, None, :], 0.0, jnp.exp(coarse[None] - row_max[..., None]))
        fine_weights = jnp.exp(fine - row_max[..., None])
        normaliser = jnp.sum(coarse_weights, axis=-1) + jnp.sum(fine_weights, axis=-1)
        coarse_rounded = coarse_weights.astype(jnp.bfloat16).astype(jnp.float32)
        fine_rounded = fine_weights.astype(jnp.bfloat16).astype(jnp.float32)
        weighted = jnp.einsum("tkgj,jkd->tkgd", coarse_rounded, value_means_f)
        weighted = weighted + jnp.einsum("tkgu,ukd->tkgd", fine_rounded, fine_values)
        result = weighted / normaliser[..., None]
        return result.reshape(BLK, QHEADS, HD).astype(jnp.bfloat16)

    attended = lax.map(per_block, (queries.reshape(NBLK, BLK, QHEADS, HD), refined))
    return attended.reshape(TOKENS, QHEADS, HD)
```

```python
import functools
import math

import jax
import jax.numpy as jnp
from jax import lax
from jax.experimental import pallas as pl
from jax.experimental.pallas import tpu as pltpu
from jax.sharding import PartitionSpec as P

MESH = pl.DeviceIdType.MESH
BLK = 128
HD = 128
SIDE = 4
BLOCKS = 32
LISTED = 128
CAP = 64
HEADS = 8


def move_kernel(
    own, q_in, owner_r, local_r, owner_c, local_c,
    far, ownkv, means, q_out,
    row, sendbuf, recv, sel, tab_out, tab_in, tab_s, pos_v, pos_s, mrow, mall, nat,
    a_send, a_recv, t_send, t_recv, s_send, s_recv, m_send, m_recv,
    q_send, q_recv, x_send, x_recv, l_sem,
):
    seq, head = lax.axis_index("seq"), lax.axis_index("head")
    core = head % 2
    x, z = seq // SIDE, seq % SIDE
    a, b = x + core * (z - x), z + core * (x - z)
    stride_a, stride_b = SIDE - 3 * core, 1 + 3 * core
    sibling = head + 1 - 2 * core

    def on_a(k):
        return (a + k) % SIDE

    def on_b(k):
        return (b + k) % SIDE

    def dev_a(k):
        return (on_a(k) * stride_a + b * stride_b, head)

    def dev_b(k):
        return (a * stride_a + on_b(k) * stride_b, head)

    def remote(src, dst, send, recv_, dev):
        return pltpu.make_async_remote_copy(
            src_ref=src, dst_ref=dst, send_sem=send, recv_sem=recv_,
            device_id=dev, device_id_type=MESH,
        )

    barrier = pltpu.get_barrier_semaphore()
    peers = [dev_a(1), dev_a(3), dev_b(1), dev_b(2), dev_b(3)]
    peers += [(seq, (head + k) % HEADS) for k in range(1, HEADS)]
    for dev in peers:
        pl.semaphore_signal(barrier, inc=1, device_id=dev, device_id_type=MESH)
    pl.semaphore_wait(barrier, len(peers))

    half = BLOCKS // 2
    lo, hi = pl.ds(0, half), pl.ds(half, half)
    gather = [
        remote(own.at[lo], row.at[a, lo], a_send.at[0], a_recv.at[0], dev_a(1)),
        remote(own.at[hi], row.at[a, hi], a_send.at[2], a_recv.at[2], dev_a(3)),
        remote(own.at[hi], row.at[a, hi], a_send.at[1], a_recv.at[1], dev_a(1)),
        remote(own.at[lo], row.at[a, lo], a_send.at[3], a_recv.at[3], dev_a(3)),
    ]
    for copy in gather:
        copy.start()
    queries = [
        remote(
            q_in.at[(head + k) % HEADS], q_out.at[head], q_send.at[k - 1], q_recv.at[k - 1],
            (seq, (head + k) % HEADS),
        )
        for k in range(1, HEADS)
    ]
    for copy in queries:
        copy.start()
    own_row = pltpu.make_async_copy(own, row.at[a], l_sem.at[0])
    own_q = pltpu.make_async_copy(q_in.at[head], q_out.at[head], l_sem.at[1])
    own_out = pltpu.make_async_copy(own, ownkv.at[core], l_sem.at[2])
    own_x = remote(own, ownkv.at[core], x_send.at[0], x_recv.at[0], (seq, sibling))
    for copy in (own_row, own_q, own_out, own_x):
        copy.start()

    ow_r, ow_c = owner_r[...], owner_c[...]
    ar, br = ow_r // SIDE, ow_r % SIDE
    ac, bc = ow_c // SIDE, ow_c % SIDE
    ar, br = ar + core * (br - ar), br + core * (ar - br)
    ac, bc = ac + core * (bc - ac), bc + core * (ac - bc)
    lane = lax.broadcasted_iota(jnp.int32, (LISTED, LISTED), 1)
    sub = lax.broadcasted_iota(jnp.int32, (LISTED, LISTED), 0)
    same = bc == br
    rank_r = jnp.sum(jnp.where(same & (sub < lane), 1, 0), axis=0, keepdims=True)
    rank_c = jnp.sum(
        jnp.where(same & (lane < sub), 1.0, 0.0).astype(jnp.float32), axis=1, keepdims=True
    ).astype(jnp.int32)
    idx_c = ac * BLOCKS + local_c[...]
    place_c = bc * LISTED + rank_c
    for g in range(SIDE):
        table = jnp.sum(
            jnp.where(place_c == lane + g * LISTED, idx_c, 0), axis=0, keepdims=True
        )
        tab_out[g] = jnp.broadcast_to(table, (8, LISTED))
    pos_v[...] = jnp.broadcast_to(br * CAP + rank_r, (8, LISTED))
    tables = [
        remote(tab_out.at[on_b(k)], tab_in.at[k - 1], t_send.at[k - 1], t_recv.at[k - 1], dev_b(k))
        for k in range(1, SIDE)
    ]
    for copy in tables:
        copy.start()
    own_tab = pltpu.make_async_copy(tab_out.at[b], tab_s.at[0], l_sem.at[3])
    pos_copy = pltpu.make_async_copy(pos_v, pos_s, l_sem.at[4])
    own_tab.start()
    pos_copy.start()

    gather[0].wait_recv()
    pass_r = remote(row.at[on_a(3), lo], row.at[on_a(3), lo], a_send.at[4], a_recv.at[4], dev_a(1))
    pass_r.start()
    gather[1].wait_recv()
    pass_l = remote(row.at[on_a(1), hi], row.at[on_a(1), hi], a_send.at[5], a_recv.at[5], dev_a(3))
    pass_l.start()
    gather[2].wait_recv()
    gather[3].wait_recv()
    pass_r.wait_recv()
    pass_l.wait_recv()
    own_row.wait()

    tab_copies = []
    for k in range(1, SIDE):
        tables[k - 1].wait_recv()
        copy = pltpu.make_async_copy(tab_in.at[k - 1], tab_s.at[k], l_sem.at[4 + k])
        copy.start()
        tab_copies.append(copy)
    own_tab.wait()
    for copy in tab_copies:
        copy.wait()

    rows = row.reshape(SIDE * BLOCKS, BLK, HD)
    part = CAP // 2
    picks = []
    for n, k in enumerate((2, 1, 3)):
        for p in range(2):

            @pl.loop(0, part)
            def _(i, k=k, p=p):
                sendbuf[k - 1, p * part + i] = rows[tab_s[k, 0, p * part + i]]

            copy = remote(
                sendbuf.at[k - 1, pl.ds(p * part, part)], recv.at[b, pl.ds(p * part, part)],
                s_send.at[2 * n + p], s_recv.at[2 * n + p], dev_b(-k % SIDE),
            )
            copy.start()
            picks.append(copy)

    @pl.loop(0, CAP)
    def _(i):
        recv[b, i] = rows[tab_s[0, 0, i]]

    take = 16
    pick_r = lax.broadcasted_iota(jnp.int32, (take, take * BLK), 0)
    pick_c = lax.broadcasted_iota(jnp.int32, (take, take * BLK), 1) // BLK
    averager = jnp.where(pick_r == pick_c, 1.0 / BLK, 0.0).astype(jnp.bfloat16)

    @pl.loop(0, SIDE * BLOCKS // take)
    def _(i):
        start = pl.multiple_of(i * take, take)
        tokens = rows[pl.ds(start, take)].reshape(take * BLK, HD)
        mean = jnp.dot(averager, tokens, preferred_element_type=jnp.float32)
        mrow[pl.ds(start, take)] = mean.astype(jnp.bfloat16)

    mean_sends = [
        remote(mrow, mall.at[b], m_send.at[k - 1], m_recv.at[k - 1], dev_b(k))
        for k in range(1, SIDE)
    ]
    for copy in mean_sends:
        copy.start()
    mall[b] = mrow[...]
    for copy in mean_sends:
        copy.wait_recv()
    for bb in range(SIDE):
        for aa in range(SIDE):
            nat[aa * stride_a + bb * stride_b] = mall[bb, pl.ds(aa * BLOCKS, BLOCKS)]
    mean_x = remote(nat, means.at[core], x_send.at[1], x_recv.at[1], (seq, sibling))
    mean_out = pltpu.make_async_copy(nat, means.at[core], l_sem.at[8])
    mean_x.start()
    mean_out.start()

    for copy in picks:
        copy.wait_recv()
    pos_copy.wait()
    slots = recv.reshape(SIDE * CAP, BLK, HD)
    chunk = LISTED // 4
    outs = []
    for p in range(4):

        @pl.loop(0, chunk)
        def _(i, p=p):
            sel[p * chunk + i] = slots[pos_s[0, p * chunk + i]]

        where = pl.ds(p * chunk, chunk)
        to_x = remote(
            sel.at[where], far.at[core, where], x_send.at[2 + p], x_recv.at[2 + p], (seq, sibling)
        )
        to_out = pltpu.make_async_copy(sel.at[where], far.at[core, where], l_sem.at[9 + p])
        to_x.start()
        to_out.start()
        outs += [to_x, to_out]

    for copy in outs + [own_q, own_out, own_x, mean_x, mean_out]:
        copy.wait()
    for copy in queries:
        copy.wait()
    for copy in gather + [pass_r, pass_l] + tables + picks + mean_sends:
        copy.wait_send()


def move(own, q_in, owner, local):
    dma = pltpu.SemaphoreType.DMA
    bf16, i32 = jnp.bfloat16, jnp.int32
    vmem, hbm = pl.BlockSpec(memory_space=pltpu.VMEM), pl.BlockSpec(memory_space=pl.ANY)
    return pl.pallas_call(
        move_kernel,
        out_shape=(
            jax.ShapeDtypeStruct((2, LISTED, BLK, HD), bf16),
            jax.ShapeDtypeStruct((2, BLOCKS, BLK, HD), bf16),
            jax.ShapeDtypeStruct((2, SIDE * SIDE, BLOCKS, HD), bf16),
            jax.ShapeDtypeStruct(q_in.shape, bf16),
        ),
        in_specs=[vmem, hbm, vmem, vmem, vmem, vmem],
        out_specs=(hbm, hbm, hbm, hbm),
        scratch_shapes=[
            pltpu.VMEM((SIDE, BLOCKS, BLK, HD), bf16),
            pltpu.VMEM((SIDE - 1, CAP, BLK, HD), bf16),
            pltpu.VMEM((SIDE, CAP, BLK, HD), bf16),
            pltpu.VMEM((LISTED, BLK, HD), bf16),
            pltpu.VMEM((SIDE, 8, LISTED), i32),
            pltpu.VMEM((SIDE - 1, 8, LISTED), i32),
            pltpu.SMEM((SIDE, 8, LISTED), i32),
            pltpu.VMEM((8, LISTED), i32),
            pltpu.SMEM((8, LISTED), i32),
            pltpu.VMEM((SIDE * BLOCKS, HD), bf16),
            pltpu.VMEM((SIDE, SIDE * BLOCKS, HD), bf16),
            pltpu.VMEM((SIDE * SIDE, BLOCKS, HD), bf16),
            dma((6,)), dma((6,)), dma((3,)), dma((3,)), dma((6,)), dma((6,)), dma((3,)), dma((3,)),
            dma((HEADS - 1,)), dma((HEADS - 1,)), dma((6,)), dma((6,)), dma((13,)),
        ],
        compiler_params=pltpu.CompilerParams(
            collective_id=0, has_side_effects=True, vmem_limit_bytes=48 * 2**20
        ),
        cost_estimate=pl.CostEstimate(flops=0, bytes_accessed=32 * 2**20, transcendentals=0),
        name="move",
    )(
        own, q_in, owner.reshape(1, LISTED), local.reshape(1, LISTED),
        owner.reshape(LISTED, 1), local.reshape(LISTED, 1),
    )


def attend_kernel(ids, q_ref, ko_ref, vo_ref, kf_ref, vf_ref, km_ref, vm_ref, o_ref):
    block = pl.program_id(0)
    f32, bf16 = jnp.float32, jnp.bfloat16
    rows = 2 * BLK
    to_log2 = math.log2(math.e)
    scale = HD**-0.5 * to_log2
    q = q_ref[...].reshape(rows, HD)

    def scores(left, right):
        return lax.dot_general(left, right, (((1,), (1,)), ((), ())), preferred_element_type=f32)

    which = lax.broadcasted_iota(jnp.int32, (8, rows), 0)
    column = lax.broadcasted_iota(jnp.int32, (8, rows), 1)
    parity = jnp.where(which == column % 2, 1.0 / BLK, 0.0).astype(bf16)
    q_mean = jnp.dot(parity, q, preferred_element_type=f32)
    high = q_mean.astype(bf16)
    rest = q_mean - high.astype(f32)
    mid = rest.astype(bf16)
    low = (rest - mid.astype(f32)).astype(bf16)
    km = km_ref[0]
    coarse = (scores(high, km) + scores(mid, km) + scores(low, km)) * scale + math.log2(BLK)
    number = lax.broadcasted_iota(jnp.int32, coarse.shape, 1)
    gone = number == ids[block * 5]
    for r in range(1, 5):
        gone = gone | (number == ids[block * 5 + r])
    coarse = jnp.where(gone, -1e30, coarse)
    c_max = jnp.max(coarse, axis=1, keepdims=True)
    c_w = jnp.where(gone, 0.0, jnp.exp2(coarse - c_max))
    c_sum = jnp.sum(c_w, axis=1, keepdims=True)
    c_val = jnp.dot(c_w.astype(bf16), vm_ref[0], preferred_element_type=f32)

    odd = lax.broadcasted_iota(jnp.int32, (rows, 1), 0) % 2 == 1

    def per_row(stat):
        return jnp.where(odd, stat[1:2], stat[0:1])

    keys = [ko_ref[0, 0]] + [kf_ref[0, r] for r in range(4)]
    values = [vo_ref[0, 0]] + [vf_ref[0, r] for r in range(4)]
    fine = scores(q, jnp.concatenate(keys, axis=0)) * scale
    cm = per_row(c_max)
    top = jnp.maximum(cm, jnp.max(fine, axis=1, keepdims=True))
    weights = jnp.exp2(fine - top)
    alpha = jnp.exp2(cm - top)
    total = alpha * per_row(c_sum) + jnp.sum(weights, axis=1, keepdims=True)
    out = jnp.dot(
        weights.astype(bf16), jnp.concatenate(values, axis=0), preferred_element_type=f32
    )
    out = (out + alpha * per_row(c_val)) / total
    o_ref[...] = out.astype(bf16).reshape(BLK, 2, HD)


def attend(ids, q, ownkv, far, means):
    per = 512 // BLK
    one = (1, 1, BLK, HD)
    four = (1, 4, BLK, HD)
    whole = (1, means.shape[1], HD)
    return pl.pallas_call(
        attend_kernel,
        out_shape=jax.ShapeDtypeStruct((BLOCKS * BLK, 2, HD), jnp.bfloat16),
        grid_spec=pltpu.PrefetchScalarGridSpec(
            num_scalar_prefetch=1,
            grid=(BLOCKS,),
            in_specs=[
                pl.BlockSpec((1, BLK, 2, HD), lambda i, ids: (i // per, i % per, 0, 0)),
                pl.BlockSpec(one, lambda i, ids: (0, i, 0, 0)),
                pl.BlockSpec(one, lambda i, ids: (1, i, 0, 0)),
                pl.BlockSpec(four, lambda i, ids: (0, i, 0, 0)),
                pl.BlockSpec(four, lambda i, ids: (1, i, 0, 0)),
                pl.BlockSpec(whole, lambda i, ids: (0, 0, 0)),
                pl.BlockSpec(whole, lambda i, ids: (1, 0, 0)),
            ],
            out_specs=pl.BlockSpec((BLK, 2, HD), lambda i, ids: (i, 0, 0)),
        ),
        compiler_params=pltpu.CompilerParams(vmem_limit_bytes=32 * 2**20),
        name="attend",
    )(ids, q, ownkv, ownkv, far, far, means, means)


def on_device(queries, keys, values, refine_owner, refine_local):
    head = lax.axis_index("head")
    kv = head // 2
    q_in = queries.reshape(512, HEADS, 2, HD).transpose(1, 0, 2, 3)
    own = lax.cond(
        head % 2 == 0,
        lambda: lax.dynamic_index_in_dim(keys, kv, 1, keepdims=False),
        lambda: lax.dynamic_index_in_dim(values, kv, 1, keepdims=False),
    ).reshape(BLOCKS, BLK, HD)
    far, ownkv, means, q = move(own, q_in, refine_owner, refine_local)
    first = lax.axis_index("seq") * BLOCKS
    own_ids = (first + jnp.arange(BLOCKS, dtype=jnp.int32))[:, None]
    ids = jnp.concatenate([own_ids, refine_owner * BLOCKS + refine_local], axis=1).reshape(-1)
    return attend(ids, q, ownkv, far, means.reshape(2, -1, HD))


def solution(mesh):
    return jax.shard_map(
        on_device,
        mesh=mesh,
        in_specs=(
            P(("seq", "head"), None, None),
            P("seq", None, None),
            P("seq", None, None),
            P("seq", None),
            P("seq", None),
        ),
        out_specs=P("seq", "head", None),
        check_vma=False,
    )
```

```python
import functools
import math

import jax
import jax.numpy as jnp
from jax import lax
from jax.experimental import pallas as pl
from jax.experimental.pallas import tpu as pltpu
from jax.sharding import PartitionSpec as P

MESH = pl.DeviceIdType.MESH
BLK = 128
HD = 128
KVH = 4
SIDE = 4
BLOCKS = 32
LISTED = 128
REFINE = 4
HEADS = 8
HALF = BLK // 2
ROWS = 2 * BLK
MIB = 2**20
F32, BF16, I32 = jnp.float32, jnp.bfloat16, jnp.int32
DMA = pltpu.SemaphoreType.DMA


class Place:
    def __init__(self):
        self.seq, self.head = lax.axis_index("seq"), lax.axis_index("head")
        self.core = self.head % 2
        x, z = self.seq // SIDE, self.seq % SIDE
        self.a, self.b = x + self.core * (z - x), z + self.core * (x - z)
        self.stride_a, self.stride_b = SIDE - 3 * self.core, 1 + 3 * self.core
        self.sibling = (self.seq, self.head + 1 - 2 * self.core)

    def on_a(self, k):
        return (self.a + k) % SIDE

    def on_b(self, k):
        return (self.b + k) % SIDE

    def dev_a(self, k):
        return (self.on_a(k) * self.stride_a + self.b * self.stride_b, self.head)

    def dev_b(self, k):
        return (self.a * self.stride_a + self.on_b(k) * self.stride_b, self.head)

    def dev_head(self, k):
        return (self.seq, (self.head + k) % HEADS)


def remote(src, dst, send, recv, dev):
    return pltpu.make_async_remote_copy(
        src_ref=src, dst_ref=dst, send_sem=send, recv_sem=recv, device_id=dev, device_id_type=MESH
    )


def greet(peers):
    barrier = pltpu.get_barrier_semaphore()
    for dev in peers:
        pl.semaphore_signal(barrier, inc=1, device_id=dev, device_id_type=MESH)
    pl.semaphore_wait(barrier, len(peers))


def start(copies):
    for copy in copies:
        copy.start()


def spread_kernel(
    keys, values, queries, owner_r, local_r, owner_c, local_c,
    rows, own, means, q_out, tabs, pos,
    kv_in, q_in, half, row, both, q_st, tab_out, tab_in, pos_v, mean_a, mean_b,
    in_sem, a_send, a_recv, q_send, q_recv, t_send, t_recv, m_send, m_recv, x_send, x_recv, l_sem,
):
    at = Place()
    kv = at.head // 2
    parts = 2
    per = BLOCKS // parts
    loads = []
    for t, src in enumerate((keys, values)):
        for p in range(parts):
            where = pl.ds(p * per, per)
            loads.append(
                pltpu.make_async_copy(
                    src.at[where, pl.ds(at.core * (HALF * KVH), HALF * KVH)],
                    kv_in.at[t, where],
                    in_sem.at[t * parts + p],
                )
            )
    loads.append(pltpu.make_async_copy(queries, q_in, in_sem.at[2 * parts]))
    start(loads)

    greet(
        [at.dev_a(k) for k in range(1, SIDE)]
        + [at.dev_b(k) for k in range(1, SIDE)]
        + [at.dev_head(k) for k in range(1, HEADS)]
    )

    out_row = lax.broadcasted_iota(I32, (HALF, HALF * KVH), 0)
    in_row = lax.broadcasted_iota(I32, (HALF, HALF * KVH), 1)
    chooser = jnp.where(in_row == out_row * KVH + kv, 1.0, 0.0).astype(BF16)
    my_half = pl.ds(at.core * HALF, HALF)
    gather, to_x = [], []
    for t in range(2):
        for p in range(parts):
            loads[t * parts + p].wait()

            @pl.loop(p * per // 4, (p + 1) * per // 4)
            def _(i, t=t):
                for u in range(4):
                    picked = jnp.dot(chooser, kv_in[t, i * 4 + u], preferred_element_type=F32)
                    picked = picked.astype(BF16)
                    half[t, i * 4 + u] = picked
                    both[t, i * 4 + u, my_half] = picked

            if p == 1:
                order = ((0, 1, 0), (1, 3, 2), (1, 1, 1), (0, 3, 3))
                for part, k, n in order:
                    where = pl.ds(part * per, per)
                    gather.append(
                        remote(
                            half.at[t, where], row.at[t, at.a, where],
                            a_send.at[t, n], a_recv.at[t, n], at.dev_a(k),
                        )
                    )
                start(gather[-4:])
        to_x.append(
            remote(
                both.at[t, :, my_half], both.at[t, :, my_half],
                x_send.at[t], x_recv.at[t], at.sibling,
            )
        )
        to_x[-1].start()
    own_row = [pltpu.make_async_copy(half.at[t], row.at[t, at.a], l_sem.at[t]) for t in range(2)]
    start(own_row)

    loads[-1].wait()
    step = 16
    out_row = lax.broadcasted_iota(I32, (16 * step, 16 * step), 0)
    in_row = lax.broadcasted_iota(I32, (16 * step, 16 * step), 1)
    pair, rest = out_row // (2 * step), out_row % (2 * step)
    order = jnp.where(in_row == (rest // 2) * 16 + pair * 2 + rest % 2, 1.0, 0.0).astype(BF16)
    chunks = q_in.shape[0] // (16 * step)

    @pl.loop(0, chunks // 2)
    def _(i):
        for u in range(2):
            first = pl.multiple_of((i * 2 + u) * 16 * step, 16 * step)
            turned = jnp.dot(order, q_in[pl.ds(first, 16 * step)], preferred_element_type=F32)
            turned = turned.astype(BF16)
            place = pl.multiple_of((i * 2 + u) * 2 * step, 2 * step)
            for h in range(HEADS):
                q_st[h, pl.ds(place, 2 * step)] = turned[h * 2 * step : (h + 1) * 2 * step]

    asked = [
        remote(
            q_st.at[(at.head + k) % HEADS], q_out.at[at.head],
            q_send.at[k - 1], q_recv.at[k - 1], at.dev_head(k),
        )
        for k in range(1, HEADS)
    ]
    start(asked)
    own_q = pltpu.make_async_copy(q_st.at[at.head], q_out.at[at.head], l_sem.at[2])
    own_q.start()

    ow_r, ow_c = owner_r[...], owner_c[...]
    ar, br = ow_r // SIDE, ow_r % SIDE
    ac, bc = ow_c // SIDE, ow_c % SIDE
    br, bc = br + at.core * (ar - br), bc + at.core * (ac - bc)
    ac = ac + at.core * (ow_c % SIDE - ac)
    id_r, id_c = ow_r * BLOCKS + local_r[...], ow_c * BLOCKS + local_c[...]
    lane = lax.broadcasted_iota(I32, (LISTED, LISTED), 1)
    sub = lax.broadcasted_iota(I32, (LISTED, LISTED), 0)
    twin = id_r == id_c

    def count(mask, axis):
        ones = jnp.where(mask, 1.0, 0.0).astype(F32)
        return jnp.sum(ones, axis=axis, keepdims=True).astype(I32)

    first_r = count(twin & (sub < lane), 0) == 0
    first_c = count(twin & (lane < sub), 1) == 0
    rank_c = count((bc == br) & (lane < sub) & first_r, 1)
    pos_r = jnp.sum(jnp.where(twin & first_c, rank_c, 0), axis=0, keepdims=True)
    idx_c = ac * BLOCKS + local_c[...]
    for g in range(SIDE):
        wanted = first_c & (bc == g) & (rank_c == lane)
        table = jnp.sum(jnp.where(wanted, idx_c, 0), axis=0, keepdims=True)
        tab_out[g] = jnp.broadcast_to(table, (8, LISTED))
    pos_v[...] = jnp.broadcast_to(br * LISTED + pos_r, (8, LISTED))
    tables = [
        remote(
            tab_out.at[at.on_b(k)], tab_in.at[k], t_send.at[k - 1], t_recv.at[k - 1], at.dev_b(k)
        )
        for k in range(1, SIDE)
    ]
    start(tables)
    tab_in[0] = tab_out[at.b]
    pos_copy = pltpu.make_async_copy(pos_v, pos, l_sem.at[3])
    pos_copy.start()

    passed = []
    lower, upper = pl.ds(0, per), pl.ds(per, per)
    for t in range(2):
        gather[4 * t].wait_recv()
        ref = row.at[t, at.on_a(3), lower]
        passed.append(remote(ref, ref, a_send.at[t, 4], a_recv.at[t, 4], at.dev_a(1)))
        passed[-1].start()
        gather[4 * t + 1].wait_recv()
        ref = row.at[t, at.on_a(1), upper]
        passed.append(remote(ref, ref, a_send.at[t, 5], a_recv.at[t, 5], at.dev_a(3)))
        passed[-1].start()

    take = 16
    pick_r = lax.broadcasted_iota(I32, (take, take * BLK), 0)
    pick_c = lax.broadcasted_iota(I32, (take, take * BLK), 1) // BLK
    averager = jnp.where(pick_r == pick_c, 1.0 / BLK, 0.0).astype(BF16)
    for t in range(2):
        to_x[t].wait_recv()
    for t in range(2):
        for i in range(BLOCKS // take):
            where = pl.ds(i * take, take)
            tokens = both[t, where].reshape(take * BLK, HD)
            mean = jnp.dot(averager, tokens, preferred_element_type=F32)
            mean_a[at.a, t, where] = mean.astype(BF16)
    own_out = pltpu.make_async_copy(both, own, l_sem.at[4])
    own_out.start()
    along_a = [
        remote(
            mean_a.at[at.a], mean_a.at[at.a], m_send.at[k - 1], m_recv.at[k - 1], at.dev_a(k)
        )
        for k in range(1, SIDE)
    ]
    start(along_a)
    for copy in along_a:
        copy.wait_recv()
    for k in range(SIDE):
        mean_b[at.b, k] = mean_a[k]
    along_b = [
        remote(
            mean_b.at[at.b], mean_b.at[at.b], m_send.at[k + 2], m_recv.at[k + 2], at.dev_b(k)
        )
        for k in range(1, SIDE)
    ]
    start(along_b)
    for copy in along_b:
        copy.wait_recv()
    mean_out = [
        pltpu.make_async_copy(
            mean_b.at[n, m], means.at[m * at.stride_a + n * at.stride_b], l_sem.at[7 + n * SIDE + m]
        )
        for n in range(SIDE)
        for m in range(SIDE)
    ]
    start(mean_out)
    for copy in tables:
        copy.wait_recv()
    tab_copy = pltpu.make_async_copy(tab_in, tabs, l_sem.at[23])
    tab_copy.start()

    rows_out = []
    for t in range(2):
        gather[4 * t + 2].wait_recv()
        gather[4 * t + 3].wait_recv()
        passed[2 * t].wait_recv()
        passed[2 * t + 1].wait_recv()
        own_row[t].wait()
        rows_out.append(pltpu.make_async_copy(row.at[t], rows.at[t], l_sem.at[5 + t]))
        rows_out[-1].start()
    for copy in asked:
        copy.wait()
    for copy in rows_out + mean_out + [own_q, pos_copy, own_out, tab_copy]:
        copy.wait()
    for copy in gather + passed + to_x + tables + along_a + along_b:
        copy.wait_send()


def spread(keys, values, queries, owner, local):
    vmem, hbm = pl.BlockSpec(memory_space=pltpu.VMEM), pl.BlockSpec(memory_space=pl.ANY)
    q_rows = queries.shape[0] // HEADS
    row_shape = (2, SIDE, BLOCKS, HALF, HD)
    own_shape = (2, BLOCKS, BLK, HD)
    mean_shape = (2, BLOCKS, HD)
    return pl.pallas_call(
        spread_kernel,
        out_shape=(
            jax.ShapeDtypeStruct(row_shape, BF16),
            jax.ShapeDtypeStruct(own_shape, BF16),
            jax.ShapeDtypeStruct((SIDE * SIDE,) + mean_shape, BF16),
            jax.ShapeDtypeStruct((HEADS, q_rows, HD), BF16),
            jax.ShapeDtypeStruct((SIDE, 8, LISTED), I32),
            jax.ShapeDtypeStruct((8, LISTED), I32),
        ),
        in_specs=[hbm, hbm, hbm, vmem, vmem, vmem, vmem],
        out_specs=(hbm,) * 6,
        scratch_shapes=[
            pltpu.VMEM((2, BLOCKS, HALF * KVH, HD), BF16),
            pltpu.VMEM(queries.shape, BF16),
            pltpu.VMEM((2, BLOCKS, HALF, HD), BF16),
            pltpu.VMEM(row_shape, BF16),
            pltpu.VMEM(own_shape, BF16),
            pltpu.VMEM((HEADS, q_rows, HD), BF16),
            pltpu.VMEM((SIDE, 8, LISTED), I32),
            pltpu.VMEM((SIDE, 8, LISTED), I32),
            pltpu.VMEM((8, LISTED), I32),
            pltpu.VMEM((SIDE,) + mean_shape, BF16),
            pltpu.VMEM((SIDE, SIDE) + mean_shape, BF16),
            DMA((5,)), DMA((2, 6)), DMA((2, 6)), DMA((HEADS - 1,)), DMA((HEADS - 1,)),
            DMA((3,)), DMA((3,)), DMA((6,)), DMA((6,)), DMA((2,)), DMA((2,)), DMA((24,)),
        ],
        compiler_params=pltpu.CompilerParams(
            collective_id=0, has_side_effects=True, vmem_limit_bytes=60 * MIB
        ),
        name="spread",
    )(
        keys, values, queries, owner.reshape(1, LISTED), local.reshape(1, LISTED),
        owner.reshape(LISTED, 1), local.reshape(LISTED, 1),
    )


def scores(left, right):
    return lax.dot_general(left, right, (((1,), (1,)), ((), ())), preferred_element_type=F32)


def pick_kernel(
    cap, tabs, pos, ids, rows, own, means, q_hbm, out,
    row_k, row_v, both, mean, q, sendbuf, recv_k, recv_v, far, weights, base, q_mean, c_max, c_sum, c_val, o_st,
    in_sem, s_send, s_recv, x_send, x_recv, o_sem,
):
    at = Place()
    row, recv = (row_k, row_v), (recv_k, recv_v)
    loads = [pltpu.make_async_copy(rows.at[t], row[t], in_sem.at[t]) for t in range(2)]
    loads += [
        pltpu.make_async_copy(q_hbm, q, in_sem.at[2]),
        pltpu.make_async_copy(means, mean, in_sem.at[3]),
        pltpu.make_async_copy(own, both, in_sem.at[4]),
    ]
    start(loads)
    greet([at.dev_b(k) for k in range(1, SIDE)] + [at.sibling])

    picks = [[], []]
    offsets = (2, 1, 3)

    def collect(t):
        blocks = row[t].reshape(SIDE * BLOCKS, HALF, HD)
        loads[t].wait()
        for n, k in enumerate(offsets):

            @pl.loop(0, cap // 8)
            def _(i, k=k):
                for u in range(8):
                    sendbuf[t, k - 1, i * 8 + u] = blocks[tabs[k, 0, i * 8 + u]]

            picks[t].append(
                remote(
                    sendbuf.at[t, k - 1], recv[t].at[at.b],
                    s_send.at[t, n], s_recv.at[t, n], at.dev_b(-k % SIDE),
                )
            )
            if t == 0:
                picks[t][-1].start()

        @pl.loop(0, cap // 8)
        def _(i):
            for u in range(8):
                recv[t][at.b, i * 8 + u] = blocks[tabs[0, 0, i * 8 + u]]

    collect(0)
    collect(1)

    to_log2 = math.log2(math.e)
    scale = HD**-0.5 * to_log2
    which = lax.broadcasted_iota(I32, (8, ROWS), 0)
    column = lax.broadcasted_iota(I32, (8, ROWS), 1)
    parity = jnp.where(which == column % 2, 1.0 / BLK, 0.0).astype(BF16)
    loads[2].wait()
    loads[3].wait()
    per_owner = q.shape[1] // ROWS

    def q_rows(i):
        first = pl.multiple_of((i % per_owner) * ROWS, ROWS)
        return q[i // per_owner, pl.ds(first, ROWS)]

    @pl.loop(0, BLOCKS // 4)
    def _(i):
        for u in range(4):
            q_mean[i * 4 + u] = jnp.dot(parity, q_rows(i * 4 + u), preferred_element_type=F32)

    group = 8
    total_blocks = SIDE * SIDE * BLOCKS
    key_means = mean[:, 0].reshape(total_blocks, HD)
    value_means = mean[:, 1].reshape(total_blocks, HD)

    @pl.loop(0, BLOCKS // group)
    def _(i):
        where = pl.ds(i * group, group)
        means_f = q_mean[where].reshape(group * 8, HD)
        high = means_f.astype(BF16)
        rest = means_f - high.astype(F32)
        mid = rest.astype(BF16)
        low = (rest - mid.astype(F32)).astype(BF16)
        coarse = scores(high, key_means) + scores(mid, key_means) + scores(low, key_means)
        coarse = coarse * scale + math.log2(BLK)
        number = lax.broadcasted_iota(I32, coarse.shape, 1)
        listed = ids[pl.ds(pl.multiple_of(i * group * 8, group * 8), group * 8)]
        gone = number == listed[:, 0:1]
        for r in range(1, REFINE + 1):
            gone = gone | (number == listed[:, r : r + 1])
        coarse = jnp.where(gone, -1e30, coarse)
        top = jnp.max(coarse, axis=1, keepdims=True)
        part = jnp.where(gone, 0.0, jnp.exp2(coarse - top))
        c_max[where] = jnp.broadcast_to(top, (group * 8, HD)).reshape(group, 8, HD)
        total = jnp.sum(part, axis=1, keepdims=True)
        c_sum[where] = jnp.broadcast_to(total, (group * 8, HD)).reshape(group, 8, HD)
        value = jnp.dot(part.astype(BF16), value_means, preferred_element_type=F32)
        c_val[where] = value.reshape(group, 8, HD)

    for copy in picks[0]:
        copy.wait_send()
    start(picks[1])
    loads[4].wait()

    my_half = pl.ds(at.core * HALF, HALF)
    pieces = 4
    piece = LISTED // pieces

    def listed_blocks(t):
        for copy in picks[t]:
            copy.wait_recv()
        copies = []
        for p in range(pieces):

            @pl.loop(0, piece // 8)
            def _(i, p=p):
                for u in range(8):
                    e = p * piece + i * 8 + u
                    place = pos[0, e]
                    far[t, e, my_half] = recv[t][place // LISTED, place % LISTED]

            ref = far.at[t, pl.ds(p * piece, piece), my_half]
            copies.append(
                remote(ref, ref, x_send.at[t, p], x_recv.at[t, p], at.sibling)
            )
            copies[-1].start()
        return copies

    odd = lax.broadcasted_iota(I32, (ROWS, 1), 0) % 2 == 1

    def per_row(ref, i, width):
        return jnp.where(odd, ref[i, 1:2, :width], ref[i, 0:1, :width])

    key_copies = listed_blocks(0)
    blocks_piece = BLOCKS // pieces
    for p in range(pieces):
        key_copies[p].wait_recv()

        @pl.loop(p * blocks_piece // 2, (p + 1) * blocks_piece // 2)
        def _(j):
            for u in range(2):
                i = j * 2 + u
                block_keys = jnp.concatenate(
                    [both[0, i], far[0, pl.ds(i * REFINE, REFINE)].reshape(REFINE * BLK, HD)], axis=0
                )
                fine = scores(q_rows(i), block_keys) * scale
                coarse_top = per_row(c_max, i, 1)
                top = jnp.maximum(coarse_top, jnp.max(fine, axis=1, keepdims=True))
                fine = jnp.exp2(fine - top)
                alpha = jnp.exp2(coarse_top - top)
                total = alpha * per_row(c_sum, i, 1) + jnp.sum(fine, axis=1, keepdims=True)
                share = 1.0 / total
                weights[i] = (fine * share).astype(BF16)
                base[i] = (alpha * share) * per_row(c_val, i, HD)

    value_copies = listed_blocks(1)
    outs = []
    for p in range(pieces):
        value_copies[p].wait_recv()

        @pl.loop(p * blocks_piece // 2, (p + 1) * blocks_piece // 2)
        def _(j):
            for u in range(2):
                i = j * 2 + u
                block_values = jnp.concatenate(
                    [both[1, i], far[1, pl.ds(i * REFINE, REFINE)].reshape(REFINE * BLK, HD)], axis=0
                )
                result = jnp.dot(weights[i], block_values, preferred_element_type=F32) + base[i]
                o_st[i] = result.astype(BF16)

        where = pl.ds(p * blocks_piece, blocks_piece)
        outs.append(pltpu.make_async_copy(o_st.at[where], out.at[where], o_sem.at[p]))
        outs[-1].start()

    for copy in outs:
        copy.wait()
    for copy in key_copies + value_copies + picks[1]:
        copy.wait_send()


def pick(cap, collective_id, rows, own, means, q, tabs, pos, ids):
    smem, vmem = pl.BlockSpec(memory_space=pltpu.SMEM), pl.BlockSpec(memory_space=pltpu.VMEM)
    hbm = pl.BlockSpec(memory_space=pl.ANY)
    return pl.pallas_call(
        functools.partial(pick_kernel, cap),
        out_shape=jax.ShapeDtypeStruct((BLOCKS, ROWS, HD), BF16),
        in_specs=[smem, smem, vmem, hbm, hbm, hbm, hbm],
        out_specs=hbm,
        scratch_shapes=[
            pltpu.VMEM(rows.shape[1:], BF16),
            pltpu.VMEM(rows.shape[1:], BF16),
            pltpu.VMEM(own.shape, BF16),
            pltpu.VMEM(means.shape, BF16),
            pltpu.VMEM(q.shape, BF16),
            pltpu.VMEM((2, SIDE - 1, cap, HALF, HD), BF16),
            pltpu.VMEM((SIDE, cap, HALF, HD), BF16),
            pltpu.VMEM((SIDE, cap, HALF, HD), BF16),
            pltpu.VMEM((2, LISTED, BLK, HD), BF16),
            pltpu.VMEM((BLOCKS, ROWS, (REFINE + 1) * BLK), BF16),
            pltpu.VMEM((BLOCKS, ROWS, HD), F32),
            pltpu.VMEM((BLOCKS, 8, HD), F32),
            pltpu.VMEM((BLOCKS, 8, HD), F32),
            pltpu.VMEM((BLOCKS, 8, HD), F32),
            pltpu.VMEM((BLOCKS, 8, HD), F32),
            pltpu.VMEM((BLOCKS, ROWS, HD), BF16),
            DMA((5,)), DMA((2, 3)), DMA((2, 3)), DMA((2, 4)), DMA((2, 4)), DMA((4,)),
        ],
        compiler_params=pltpu.CompilerParams(
            collective_id=collective_id, has_side_effects=True, vmem_limit_bytes=60 * MIB
        ),
        name="pick",
    )(tabs, pos, ids, rows, own, means, q)


def on_device(queries, keys, values, refine_owner, refine_local):
    first = lax.axis_index("seq") * BLOCKS
    own_ids = (first + jnp.arange(BLOCKS, dtype=I32))[:, None]
    ids = jnp.concatenate([own_ids, refine_owner * BLOCKS + refine_local], axis=1)
    ids = jnp.repeat(ids, 8, axis=0)
    rows, own, means, q, tabs, pos = spread(
        keys.reshape(BLOCKS, BLK * KVH, HD),
        values.reshape(BLOCKS, BLK * KVH, HD),
        queries.reshape(-1, HD),
        refine_owner,
        refine_local,
    )
    out = pick(64, 1, rows, own, means, q, tabs, pos, ids)
    return out.reshape(BLOCKS * BLK, 2, HD)


def solution(mesh):
    return jax.shard_map(
        on_device,
        mesh=mesh,
        in_specs=(
            P(("seq", "head"), None, None),
            P("seq", None, None),
            P("seq", None, None),
            P("seq", None),
            P("seq", None),
        ),
        out_specs=P("seq", "head", None),
        check_vma=False,
    )
```

```python
import functools
import math

import jax
import jax.numpy as jnp
from jax import lax
from jax.experimental import pallas as pl
from jax.experimental.pallas import tpu as pltpu
from jax.sharding import PartitionSpec as P

MESH = pl.DeviceIdType.MESH
BLK = 128
HD = 128
KVH = 4
SIDE = 4
BLOCKS = 32
LISTED = 128
REFINE = 4
HEADS = 8
HALF = BLK // 2
ROWS = 2 * BLK
MIB = 2**20
F32, BF16, I32 = jnp.float32, jnp.bfloat16, jnp.int32
DMA = pltpu.SemaphoreType.DMA


class Place:
    def __init__(self):
        self.seq, self.head = lax.axis_index("seq"), lax.axis_index("head")
        self.core = self.head % 2
        x, z = self.seq // SIDE, self.seq % SIDE
        self.a, self.b = x + self.core * (z - x), z + self.core * (x - z)
        self.stride_a, self.stride_b = SIDE - 3 * self.core, 1 + 3 * self.core
        self.sibling = (self.seq, self.head + 1 - 2 * self.core)

    def on_a(self, k):
        return (self.a + k) % SIDE

    def on_b(self, k):
        return (self.b + k) % SIDE

    def dev_a(self, k):
        return (self.on_a(k) * self.stride_a + self.b * self.stride_b, self.head)

    def dev_b(self, k):
        return (self.a * self.stride_a + self.on_b(k) * self.stride_b, self.head)

    def dev_head(self, k):
        return (self.seq, (self.head + k) % HEADS)


def remote(src, dst, send, recv, dev):
    return pltpu.make_async_remote_copy(
        src_ref=src, dst_ref=dst, send_sem=send, recv_sem=recv, device_id=dev, device_id_type=MESH
    )


def greet(peers):
    barrier = pltpu.get_barrier_semaphore()
    for dev in peers:
        pl.semaphore_signal(barrier, inc=1, device_id=dev, device_id_type=MESH)
    pl.semaphore_wait(barrier, len(peers))


def start(copies):
    for copy in copies:
        copy.start()


def spread_kernel(
    keys, values, queries, owner, local,
    rows, own, means, q_out, q_later, tabs, pos,
    kv_in, q_in, half, row, both, q_st, tab_out, tab_in, pos_v, mean_a, mean_b,
    in_sem, a_send, a_recv, q_send, q_recv, t_send, t_recv, m_send, m_recv, x_send, x_recv, l_sem,
):
    at = Place()
    kv = at.head // 2
    parts = 2
    per = BLOCKS // parts
    loads = []
    for t, src in enumerate((keys, values)):
        for p in range(parts):
            where = pl.ds(p * per, per)
            loads.append(
                pltpu.make_async_copy(
                    src.at[where, pl.ds(at.core * (HALF * KVH), HALF * KVH)],
                    kv_in.at[t, where],
                    in_sem.at[t * parts + p],
                )
            )
    loads.append(pltpu.make_async_copy(queries, q_in, in_sem.at[2 * parts]))
    start(loads)

    greet(
        [at.dev_a(k) for k in range(1, SIDE)]
        + [at.dev_b(k) for k in range(1, SIDE)]
        + [at.dev_head(k) for k in range(1, HEADS)]
    )

    out_row = lax.broadcasted_iota(I32, (HALF, HALF * KVH), 0)
    in_row = lax.broadcasted_iota(I32, (HALF, HALF * KVH), 1)
    chooser = jnp.where(in_row == out_row * KVH + kv, 1.0, 0.0).astype(BF16)
    my_half = pl.ds(at.core * HALF, HALF)
    gather, to_x = [], []
    order = ((0, 1, 0), (1, 3, 2), (1, 1, 1), (0, 3, 3))
    for t in range(2):
        for p in range(parts):
            loads[t * parts + p].wait()

            @pl.loop(p * per // 8, (p + 1) * per // 8)
            def _(i, t=t):
                for u in range(8):
                    picked = jnp.dot(chooser, kv_in[t, i * 8 + u], preferred_element_type=F32)
                    picked = picked.astype(BF16)
                    half[t, i * 8 + u] = picked
                    both[t, i * 8 + u, my_half] = picked

            for part, k, n in order[:1] if p == 0 else order[1:]:
                where = pl.ds(part * per, per)
                gather.append(
                    remote(
                        half.at[t, where], row.at[t, at.a, where],
                        a_send.at[t, n], a_recv.at[t, n], at.dev_a(k),
                    )
                )
                gather[-1].start()
        to_x.append(
            remote(
                both.at[t, :, my_half], both.at[t, :, my_half],
                x_send.at[t], x_recv.at[t], at.sibling,
            )
        )
        to_x[-1].start()
    own_row = [pltpu.make_async_copy(half.at[t], row.at[t, at.a], l_sem.at[t]) for t in range(2)]
    start(own_row)

    loads[-1].wait()
    step = 16
    out_row = lax.broadcasted_iota(I32, (16 * step, 16 * step), 0)
    in_row = lax.broadcasted_iota(I32, (16 * step, 16 * step), 1)
    pair, rest = out_row // (2 * step), out_row % (2 * step)
    order = jnp.where(in_row == (rest // 2) * 16 + pair * 2 + rest % 2, 1.0, 0.0).astype(BF16)
    chunks = q_in.shape[0] // (16 * step)

    def turn(low, high):
        @pl.loop(low // 4, high // 4)
        def _(i):
            for u in range(4):
                first = pl.multiple_of((i * 4 + u) * 16 * step, 16 * step)
                turned = jnp.dot(order, q_in[pl.ds(first, 16 * step)], preferred_element_type=F32)
                turned = turned.astype(BF16)
                place = pl.multiple_of((i * 4 + u) * 2 * step, 2 * step)
                for h in range(HEADS):
                    q_st[h, pl.ds(place, 2 * step)] = turned[h * 2 * step : (h + 1) * 2 * step]

    turn(0, chunks // 2)
    now = pl.ds(0, q_st.shape[1] // 2)
    asked = [
        remote(
            q_st.at[(at.head + k) % HEADS, now], q_out.at[at.head],
            q_send.at[k - 1], q_recv.at[k - 1], at.dev_head(k),
        )
        for k in range(1, HEADS)
    ]
    start(asked)
    own_q = pltpu.make_async_copy(q_st.at[at.head, now], q_out.at[at.head], l_sem.at[2])
    own_q.start()
    turn(chunks // 2, chunks)
    later = pl.ds(q_st.shape[1] // 2, q_st.shape[1] // 2)
    later_q = pltpu.make_async_copy(q_st.at[:, later], q_later, l_sem.at[24])
    later_q.start()

    lane = lax.broadcasted_iota(I32, (LISTED, LISTED), 1)
    sub = lax.broadcasted_iota(I32, (LISTED, LISTED), 0)

    def as_row(ref):
        return jnp.concatenate([ref[r : r + 1] for r in range(REFINE)], axis=1)

    def as_column(line):
        spot = jnp.where(lane == sub, line.astype(F32), 0.0)
        return jnp.sum(spot, axis=1, keepdims=True).astype(I32)

    ow_r, lo_r = as_row(owner), as_row(local)
    ow_c, lo_c = as_column(ow_r), as_column(lo_r)
    ar, br = ow_r // SIDE, ow_r % SIDE
    ac, bc = ow_c // SIDE, ow_c % SIDE
    br, bc = br + at.core * (ar - br), bc + at.core * (ac - bc)
    ac = ac + at.core * (ow_c % SIDE - ac)
    id_r, id_c = ow_r * BLOCKS + lo_r, ow_c * BLOCKS + lo_c
    twin = id_r == id_c

    def count(mask, axis):
        ones = jnp.where(mask, 1.0, 0.0).astype(F32)
        return jnp.sum(ones, axis=axis, keepdims=True).astype(I32)

    first_r = count(twin & (sub < lane), 0) == 0
    first_c = count(twin & (lane < sub), 1) == 0
    rank_c = count((bc == br) & (lane < sub) & first_r, 1)
    pos_r = jnp.sum(jnp.where(twin & first_c, rank_c, 0), axis=0, keepdims=True)
    idx_c = ac * BLOCKS + lo_c
    for g in range(SIDE):
        wanted = first_c & (bc == g) & (rank_c == lane)
        table = jnp.sum(jnp.where(wanted, idx_c, 0), axis=0, keepdims=True)
        tab_out[g] = jnp.broadcast_to(table, (8, LISTED))
    line = lax.broadcasted_iota(I32, (8, LISTED), 0)
    pos_v[...] = jnp.where(line == 0, br * LISTED + pos_r, id_r)
    tables = [
        remote(
            tab_out.at[at.on_b(k)], tab_in.at[k], t_send.at[k - 1], t_recv.at[k - 1], at.dev_b(k)
        )
        for k in range(1, SIDE)
    ]
    start(tables)
    tab_in[0] = tab_out[at.b]
    pos_copy = pltpu.make_async_copy(pos_v, pos, l_sem.at[3])
    pos_copy.start()

    passed = []
    lower, upper = pl.ds(0, per), pl.ds(per, per)
    for t in range(2):
        gather[4 * t].wait_recv()
        ref = row.at[t, at.on_a(3), lower]
        passed.append(remote(ref, ref, a_send.at[t, 4], a_recv.at[t, 4], at.dev_a(1)))
        passed[-1].start()
        gather[4 * t + 1].wait_recv()
        ref = row.at[t, at.on_a(1), upper]
        passed.append(remote(ref, ref, a_send.at[t, 5], a_recv.at[t, 5], at.dev_a(3)))
        passed[-1].start()

    take = 16
    pick_r = lax.broadcasted_iota(I32, (take, take * BLK), 0)
    pick_c = lax.broadcasted_iota(I32, (take, take * BLK), 1) // BLK
    averager = jnp.where(pick_r == pick_c, 1.0 / BLK, 0.0).astype(BF16)
    for t in range(2):
        to_x[t].wait_recv()
    for t in range(2):
        for i in range(BLOCKS // take):
            where = pl.ds(i * take, take)
            tokens = both[t, where].reshape(take * BLK, HD)
            mean = jnp.dot(averager, tokens, preferred_element_type=F32)
            mean_a[at.a, t, where] = mean.astype(BF16)
    own_out = pltpu.make_async_copy(both, own, l_sem.at[4])
    own_out.start()
    along_a = [
        remote(
            mean_a.at[at.a], mean_a.at[at.a], m_send.at[k - 1], m_recv.at[k - 1], at.dev_a(k)
        )
        for k in range(1, SIDE)
    ]
    start(along_a)
    for copy in along_a:
        copy.wait_recv()
    for k in range(SIDE):
        mean_b[at.b, k] = mean_a[k]
    along_b = [
        remote(
            mean_b.at[at.b], mean_b.at[at.b], m_send.at[k + 2], m_recv.at[k + 2], at.dev_b(k)
        )
        for k in range(1, SIDE)
    ]
    start(along_b)
    for copy in along_b:
        copy.wait_recv()
    mean_out = [
        pltpu.make_async_copy(
            mean_b.at[n, m], means.at[m * at.stride_a + n * at.stride_b], l_sem.at[7 + n * SIDE + m]
        )
        for n in range(SIDE)
        for m in range(SIDE)
    ]
    start(mean_out)
    for copy in tables:
        copy.wait_recv()
    tab_copy = pltpu.make_async_copy(tab_in, tabs, l_sem.at[23])
    tab_copy.start()

    rows_out = []
    for t in range(2):
        gather[4 * t + 2].wait_recv()
        gather[4 * t + 3].wait_recv()
        passed[2 * t].wait_recv()
        passed[2 * t + 1].wait_recv()
        own_row[t].wait()
        rows_out.append(pltpu.make_async_copy(row.at[t], rows.at[t], l_sem.at[5 + t]))
        rows_out[-1].start()
    for copy in asked:
        copy.wait()
    for copy in rows_out + mean_out + [own_q, later_q, pos_copy, own_out, tab_copy]:
        copy.wait()
    for copy in gather + passed + to_x + tables + along_a + along_b:
        copy.wait_send()


def spread(keys, values, queries, owner, local):
    vmem, hbm = pl.BlockSpec(memory_space=pltpu.VMEM), pl.BlockSpec(memory_space=pl.ANY)
    q_rows = queries.shape[0] // HEADS
    row_shape = (2, SIDE, BLOCKS, HALF, HD)
    own_shape = (2, BLOCKS, BLK, HD)
    mean_shape = (2, BLOCKS, HD)
    return pl.pallas_call(
        spread_kernel,
        out_shape=(
            jax.ShapeDtypeStruct(row_shape, BF16),
            jax.ShapeDtypeStruct(own_shape, BF16),
            jax.ShapeDtypeStruct((SIDE * SIDE,) + mean_shape, BF16),
            jax.ShapeDtypeStruct((HEADS, q_rows // 2, HD), BF16),
            jax.ShapeDtypeStruct((HEADS, q_rows // 2, HD), BF16),
            jax.ShapeDtypeStruct((SIDE, 8, LISTED), I32),
            jax.ShapeDtypeStruct((8, LISTED), I32),
        ),
        in_specs=[hbm, hbm, hbm, vmem, vmem],
        out_specs=(hbm,) * 7,
        scratch_shapes=[
            pltpu.VMEM((2, BLOCKS, HALF * KVH, HD), BF16),
            pltpu.VMEM(queries.shape, BF16),
            pltpu.VMEM((2, BLOCKS, HALF, HD), BF16),
            pltpu.VMEM(row_shape, BF16),
            pltpu.VMEM(own_shape, BF16),
            pltpu.VMEM((HEADS, q_rows, HD), BF16),
            pltpu.VMEM((SIDE, 8, LISTED), I32),
            pltpu.VMEM((SIDE, 8, LISTED), I32),
            pltpu.VMEM((8, LISTED), I32),
            pltpu.VMEM((SIDE,) + mean_shape, BF16),
            pltpu.VMEM((SIDE, SIDE) + mean_shape, BF16),
            DMA((5,)), DMA((2, 6)), DMA((2, 6)), DMA((HEADS - 1,)), DMA((HEADS - 1,)),
            DMA((3,)), DMA((3,)), DMA((6,)), DMA((6,)), DMA((2,)), DMA((2,)), DMA((25,)),
        ],
        compiler_params=pltpu.CompilerParams(
            collective_id=0, has_side_effects=True, vmem_limit_bytes=60 * MIB
        ),
        name="spread",
    )(keys, values, queries, owner, local)


def scores(left, right):
    return lax.dot_general(left, right, (((1,), (1,)), ((), ())), preferred_element_type=F32)


def pick_kernel(
    cap, tabs, pos, rows, own, means, q_first, q_later, out,
    row_k, row_v, both, mean, q, sendbuf, recv_k, recv_v, far, weights, base, q_mean, c_max, c_sum, c_val, o_st,
    in_sem, s_send, s_recv, x_send, x_recv, q_send, q_recv, o_sem,
):
    at = Place()
    row, recv = (row_k, row_v), (recv_k, recv_v)
    early, late = pl.ds(0, q.shape[1] // 2), pl.ds(q.shape[1] // 2, q.shape[1] // 2)
    loads = [pltpu.make_async_copy(rows.at[t], row[t], in_sem.at[t]) for t in range(2)]
    loads += [
        pltpu.make_async_copy(q_first, q.at[:, early], in_sem.at[2]),
        pltpu.make_async_copy(means, mean, in_sem.at[3]),
        pltpu.make_async_copy(own, both, in_sem.at[4]),
        pltpu.make_async_copy(q_later.at[at.head], q.at[at.head, late], in_sem.at[5]),
    ]
    start(loads)
    greet([at.dev_b(k) for k in range(1, SIDE)] + [at.dev_head(k) for k in range(1, HEADS)])

    picks = [[], []]
    offsets = (2, 1, 3)

    def collect(t):
        blocks = row[t].reshape(SIDE * BLOCKS, HALF, HD)
        loads[t].wait()
        for n, k in enumerate(offsets):

            @pl.loop(0, cap // 8)
            def _(i, k=k):
                for u in range(8):
                    sendbuf[t, k - 1, i * 8 + u] = blocks[tabs[k, 0, i * 8 + u]]

            picks[t].append(
                remote(
                    sendbuf.at[t, k - 1], recv[t].at[at.b],
                    s_send.at[t, n], s_recv.at[t, n], at.dev_b(-k % SIDE),
                )
            )
            if t == 0:
                picks[t][-1].start()

        @pl.loop(0, cap // 8)
        def _(i):
            for u in range(8):
                recv[t][at.b, i * 8 + u] = blocks[tabs[0, 0, i * 8 + u]]

    collect(0)
    asked = [
        remote(
            q_later.at[(at.head + k) % HEADS], q.at[at.head, late],
            q_send.at[k - 1], q_recv.at[k - 1], at.dev_head(k),
        )
        for k in range(1, HEADS)
    ]
    start(asked)
    collect(1)

    to_log2 = math.log2(math.e)
    scale = HD**-0.5 * to_log2
    which = lax.broadcasted_iota(I32, (8, ROWS), 0)
    column = lax.broadcasted_iota(I32, (8, ROWS), 1)
    parity = jnp.where(which == column % 2, 1.0 / BLK, 0.0).astype(BF16)
    for n in (2, 3, 5):
        loads[n].wait()
    for copy in asked:
        copy.wait_recv()
    per_owner = q.shape[1] // ROWS

    def q_rows(i):
        first = pl.multiple_of((i % per_owner) * ROWS, ROWS)
        return q[i // per_owner, pl.ds(first, ROWS)]

    @pl.loop(0, BLOCKS // 4)
    def _(i):
        for u in range(4):
            q_mean[i * 4 + u] = jnp.dot(parity, q_rows(i * 4 + u), preferred_element_type=F32)

    group = 8
    total_blocks = SIDE * SIDE * BLOCKS
    key_means = mean[:, 0].reshape(total_blocks, HD)
    value_means = mean[:, 1].reshape(total_blocks, HD)

    @pl.loop(0, BLOCKS // group)
    def _(i):
        where = pl.ds(i * group, group)
        means_f = q_mean[where].reshape(group * 8, HD)
        high = means_f.astype(BF16)
        rest = means_f - high.astype(F32)
        mid = rest.astype(BF16)
        low = (rest - mid.astype(F32)).astype(BF16)
        coarse = scores(high, key_means) + scores(mid, key_means) + scores(low, key_means)
        coarse = coarse * scale + math.log2(BLK)
        number = lax.broadcasted_iota(I32, (8, total_blocks), 1)
        kept = []
        for u in range(group):
            block = i * group + u
            gone = number == at.seq * BLOCKS + block
            for r in range(REFINE):
                gone = gone | (number == pos[1, r * BLOCKS + block])
            kept.append(jnp.where(gone, 0.0, 1.0))
        kept = jnp.concatenate(kept, axis=0) > 0.0
        coarse = jnp.where(kept, coarse, -1e30)
        top = jnp.max(coarse, axis=1, keepdims=True)
        part = jnp.where(kept, jnp.exp2(coarse - top), 0.0)
        c_max[where] = jnp.broadcast_to(top, (group * 8, HD)).reshape(group, 8, HD)
        total = jnp.sum(part, axis=1, keepdims=True)
        c_sum[where] = jnp.broadcast_to(total, (group * 8, HD)).reshape(group, 8, HD)
        value = jnp.dot(part.astype(BF16), value_means, preferred_element_type=F32)
        c_val[where] = value.reshape(group, 8, HD)

    for copy in picks[0]:
        copy.wait_send()
    start(picks[1])
    loads[4].wait()

    my_half = pl.ds(at.core * HALF, HALF)
    pieces = 4
    piece, blocks_piece = LISTED // pieces, BLOCKS // pieces

    def listed_blocks(t):
        for copy in picks[t]:
            copy.wait_recv()
        copies = []
        for p in range(pieces):

            @pl.loop(p * blocks_piece // 2, (p + 1) * blocks_piece // 2)
            def _(j):
                for u in range(2):
                    for r in range(REFINE):
                        i = j * 2 + u
                        place = pos[0, r * BLOCKS + i]
                        far[t, i * REFINE + r, my_half] = recv[t][place // LISTED, place % LISTED]

            ref = far.at[t, pl.ds(p * piece, piece), my_half]
            copies.append(
                remote(ref, ref, x_send.at[t, p], x_recv.at[t, p], at.sibling)
            )
            copies[-1].start()
        return copies

    odd = lax.broadcasted_iota(I32, (ROWS, 1), 0) % 2 == 1

    def per_row(ref, i, width):
        return jnp.where(odd, ref[i, 1:2, :width], ref[i, 0:1, :width])

    key_copies = listed_blocks(0)
    for p in range(pieces):
        key_copies[p].wait_recv()

        @pl.loop(p * blocks_piece // 4, (p + 1) * blocks_piece // 4)
        def _(j):
            for u in range(4):
                i = j * 4 + u
                block_keys = jnp.concatenate(
                    [both[0, i], far[0, pl.ds(i * REFINE, REFINE)].reshape(REFINE * BLK, HD)], axis=0
                )
                fine = scores(q_rows(i), block_keys) * scale
                coarse_top = per_row(c_max, i, 1)
                top = jnp.maximum(coarse_top, jnp.max(fine, axis=1, keepdims=True))
                fine = jnp.exp2(fine - top)
                alpha = jnp.exp2(coarse_top - top)
                total = alpha * per_row(c_sum, i, 1) + jnp.sum(fine, axis=1, keepdims=True)
                share = 1.0 / total
                weights[i] = (fine * share).astype(BF16)
                base[i] = (alpha * share) * per_row(c_val, i, HD)

    value_copies = listed_blocks(1)
    outs = []
    for p in range(pieces):
        value_copies[p].wait_recv()

        @pl.loop(p * blocks_piece // 4, (p + 1) * blocks_piece // 4)
        def _(j):
            for u in range(4):
                i = j * 4 + u
                block_values = jnp.concatenate(
                    [both[1, i], far[1, pl.ds(i * REFINE, REFINE)].reshape(REFINE * BLK, HD)], axis=0
                )
                result = jnp.dot(weights[i], block_values, preferred_element_type=F32) + base[i]
                o_st[i] = result.astype(BF16)

        where = pl.ds(p * blocks_piece, blocks_piece)
        outs.append(pltpu.make_async_copy(o_st.at[where], out.at[where], o_sem.at[p]))
        outs[-1].start()

    for copy in outs:
        copy.wait()
    for copy in key_copies + value_copies + picks[1] + asked:
        copy.wait_send()


def pick(cap, collective_id, rows, own, means, q_first, q_later, tabs, pos):
    smem, hbm = pl.BlockSpec(memory_space=pltpu.SMEM), pl.BlockSpec(memory_space=pl.ANY)
    q_shape = (HEADS, 2 * q_first.shape[1], HD)
    return pl.pallas_call(
        functools.partial(pick_kernel, cap),
        out_shape=jax.ShapeDtypeStruct((BLOCKS, ROWS, HD), BF16),
        in_specs=[smem, smem, hbm, hbm, hbm, hbm, hbm],
        out_specs=hbm,
        scratch_shapes=[
            pltpu.VMEM(rows.shape[1:], BF16),
            pltpu.VMEM(rows.shape[1:], BF16),
            pltpu.VMEM(own.shape, BF16),
            pltpu.VMEM(means.shape, BF16),
            pltpu.VMEM(q_shape, BF16),
            pltpu.VMEM((2, SIDE - 1, cap, HALF, HD), BF16),
            pltpu.VMEM((SIDE, cap, HALF, HD), BF16),
            pltpu.VMEM((SIDE, cap, HALF, HD), BF16),
            pltpu.VMEM((2, LISTED, BLK, HD), BF16),
            pltpu.VMEM((BLOCKS, ROWS, (REFINE + 1) * BLK), BF16),
            pltpu.VMEM((BLOCKS, ROWS, HD), F32),
            pltpu.VMEM((BLOCKS, 8, HD), F32),
            pltpu.VMEM((BLOCKS, 8, HD), F32),
            pltpu.VMEM((BLOCKS, 8, HD), F32),
            pltpu.VMEM((BLOCKS, 8, HD), F32),
            pltpu.VMEM((BLOCKS, ROWS, HD), BF16),
            DMA((6,)), DMA((2, 3)), DMA((2, 3)), DMA((2, 4)), DMA((2, 4)),
            DMA((HEADS - 1,)), DMA((HEADS - 1,)), DMA((4,)),
        ],
        compiler_params=pltpu.CompilerParams(
            collective_id=collective_id, has_side_effects=True, vmem_limit_bytes=60 * MIB
        ),
        name="pick",
    )(tabs, pos, rows, own, means, q_first, q_later)


def hand_on_kernel(src, dst, held, in_sem, out_sem):
    parts = in_sem.shape[0]
    per = BLOCKS // parts
    where = [pl.ds(p * per, per) for p in range(parts)]
    inward = [
        pltpu.make_async_copy(src.at[w], held.at[w], in_sem.at[p]) for p, w in enumerate(where)
    ]
    outward = [
        pltpu.make_async_copy(held.at[w], dst.at[w], out_sem.at[p]) for p, w in enumerate(where)
    ]
    start(inward)
    for before, after in zip(inward, outward):
        before.wait()
        after.start()
    for copy in outward:
        copy.wait()


def hand_on(result):
    hbm = pl.BlockSpec(memory_space=pl.ANY)
    return pl.pallas_call(
        hand_on_kernel,
        out_shape=jax.ShapeDtypeStruct(result.shape, result.dtype),
        in_specs=[hbm],
        out_specs=hbm,
        scratch_shapes=[pltpu.VMEM(result.shape, result.dtype), DMA((8,)), DMA((8,))],
        compiler_params=pltpu.CompilerParams(vmem_limit_bytes=60 * MIB),
        name="hand_on",
    )(result)


def on_device(queries, keys, values, refine_owner, refine_local):
    rows, own, means, q_first, q_later, tabs, pos = spread(
        keys.reshape(BLOCKS, BLK * KVH, HD),
        values.reshape(BLOCKS, BLK * KVH, HD),
        queries.reshape(-1, HD),
        refine_owner.T,
        refine_local.T,
    )
    out = pick(64, 1, rows, own, means, q_first, q_later, tabs, pos)
    return hand_on(out).reshape(BLOCKS * BLK, 2, HD)


def solution(mesh):
    return jax.shard_map(
        on_device,
        mesh=mesh,
        in_specs=(
            P(("seq", "head"), None, None),
            P("seq", None, None),
            P("seq", None, None),
            P("seq", None),
            P("seq", None),
        ),
        out_specs=P("seq", "head", None),
        check_vma=False,
    )
```

```python
import functools
import math

import jax
import jax.numpy as jnp
from jax import lax
from jax.experimental import pallas as pl
from jax.experimental.pallas import tpu as pltpu
from jax.sharding import PartitionSpec as P

MESH = pl.DeviceIdType.MESH
BLK = 128
HD = 128
KVH = 4
SIDE = 4
BLOCKS = 32
LISTED = 128
REFINE = 4
HEADS = 8
HALF = BLK // 2
MOST = 64
ROWS = 2 * BLK
MIB = 2**20
F32, BF16, I32 = jnp.float32, jnp.bfloat16, jnp.int32
DMA = pltpu.SemaphoreType.DMA


class Place:
    def __init__(self):
        self.seq, self.head = lax.axis_index("seq"), lax.axis_index("head")
        self.core = self.head % 2
        x, z = self.seq // SIDE, self.seq % SIDE
        self.a, self.b = x + self.core * (z - x), z + self.core * (x - z)
        self.stride_a, self.stride_b = SIDE - 3 * self.core, 1 + 3 * self.core
        self.sibling = (self.seq, self.head + 1 - 2 * self.core)

    def on_a(self, k):
        return (self.a + k) % SIDE

    def on_b(self, k):
        return (self.b + k) % SIDE

    def dev_a(self, k):
        return (self.on_a(k) * self.stride_a + self.b * self.stride_b, self.head)

    def dev_b(self, k):
        return (self.a * self.stride_a + self.on_b(k) * self.stride_b, self.head)

    def dev_head(self, k):
        return (self.seq, (self.head + k) % HEADS)


def remote(src, dst, send, recv, dev):
    return pltpu.make_async_remote_copy(
        src_ref=src, dst_ref=dst, send_sem=send, recv_sem=recv, device_id=dev, device_id_type=MESH
    )


def greet(peers):
    barrier = pltpu.get_barrier_semaphore()
    for dev in peers:
        pl.semaphore_signal(barrier, inc=1, device_id=dev, device_id_type=MESH)
    pl.semaphore_wait(barrier, len(peers))


def start(copies):
    for copy in copies:
        copy.start()


def spread_kernel(
    keys, values, queries, owner, local,
    rows, own, means, q_out, q_later, tabs, pos, need,
    kv_in, q_in, half, row, both, q_st, tab_out, tab_in, pos_v, need_a, need_b, mean_a, mean_b,
    in_sem, a_send, a_recv, q_send, q_recv, t_send, t_recv, n_send, n_recv, m_send, m_recv, x_send, x_recv, l_sem,
):
    at = Place()
    kv = at.head // 2
    parts = 2
    per = BLOCKS // parts
    loads = []
    for t, src in enumerate((keys, values)):
        for p in range(parts):
            where = pl.ds(p * per, per)
            loads.append(
                pltpu.make_async_copy(
                    src.at[where, pl.ds(at.core * (HALF * KVH), HALF * KVH)],
                    kv_in.at[t, where],
                    in_sem.at[t * parts + p],
                )
            )
    loads.append(pltpu.make_async_copy(queries, q_in, in_sem.at[2 * parts]))
    start(loads)

    greet(
        [at.dev_a(k) for k in range(1, SIDE)]
        + [at.dev_b(k) for k in range(1, SIDE)]
        + [at.dev_head(k) for k in range(1, HEADS)]
    )

    out_row = lax.broadcasted_iota(I32, (HALF, HALF * KVH), 0)
    in_row = lax.broadcasted_iota(I32, (HALF, HALF * KVH), 1)
    chooser = jnp.where(in_row == out_row * KVH + kv, 1.0, 0.0).astype(BF16)
    my_half = pl.ds(at.core * HALF, HALF)
    gather, to_x = [], []
    order = ((0, 1, 0), (1, 3, 2), (1, 1, 1), (0, 3, 3))
    for t in range(2):
        for p in range(parts):
            loads[t * parts + p].wait()

            @pl.loop(p * per // 8, (p + 1) * per // 8)
            def _(i, t=t):
                for u in range(8):
                    picked = jnp.dot(chooser, kv_in[t, i * 8 + u], preferred_element_type=F32)
                    picked = picked.astype(BF16)
                    half[t, i * 8 + u] = picked
                    both[t, i * 8 + u, my_half] = picked

            for part, k, n in order[:1] if p == 0 else order[1:]:
                where = pl.ds(part * per, per)
                gather.append(
                    remote(
                        half.at[t, where], row.at[t, at.a, where],
                        a_send.at[t, n], a_recv.at[t, n], at.dev_a(k),
                    )
                )
                gather[-1].start()
        to_x.append(
            remote(
                both.at[t, :, my_half], both.at[t, :, my_half],
                x_send.at[t], x_recv.at[t], at.sibling,
            )
        )
        to_x[-1].start()
    own_row = [pltpu.make_async_copy(half.at[t], row.at[t, at.a], l_sem.at[t]) for t in range(2)]
    start(own_row)

    loads[-1].wait()
    step = 16
    out_row = lax.broadcasted_iota(I32, (16 * step, 16 * step), 0)
    in_row = lax.broadcasted_iota(I32, (16 * step, 16 * step), 1)
    pair, rest = out_row // (2 * step), out_row % (2 * step)
    order = jnp.where(in_row == (rest // 2) * 16 + pair * 2 + rest % 2, 1.0, 0.0).astype(BF16)
    chunks = q_in.shape[0] // (16 * step)

    def turn(low, high):
        @pl.loop(low // 4, high // 4)
        def _(i):
            for u in range(4):
                first = pl.multiple_of((i * 4 + u) * 16 * step, 16 * step)
                turned = jnp.dot(order, q_in[pl.ds(first, 16 * step)], preferred_element_type=F32)
                turned = turned.astype(BF16)
                place = pl.multiple_of((i * 4 + u) * 2 * step, 2 * step)
                for h in range(HEADS):
                    q_st[h, pl.ds(place, 2 * step)] = turned[h * 2 * step : (h + 1) * 2 * step]

    turn(0, chunks // 2)
    now = pl.ds(0, q_st.shape[1] // 2)
    asked = [
        remote(
            q_st.at[(at.head + k) % HEADS, now], q_out.at[at.head],
            q_send.at[k - 1], q_recv.at[k - 1], at.dev_head(k),
        )
        for k in range(1, HEADS)
    ]
    start(asked)
    own_q = pltpu.make_async_copy(q_st.at[at.head, now], q_out.at[at.head], l_sem.at[2])
    own_q.start()
    turn(chunks // 2, chunks)
    later = pl.ds(q_st.shape[1] // 2, q_st.shape[1] // 2)
    later_q = pltpu.make_async_copy(q_st.at[:, later], q_later, l_sem.at[24])
    later_q.start()

    lane = lax.broadcasted_iota(I32, (LISTED, LISTED), 1)
    sub = lax.broadcasted_iota(I32, (LISTED, LISTED), 0)

    def as_row(ref):
        return jnp.concatenate([ref[r : r + 1] for r in range(REFINE)], axis=1)

    def as_column(line):
        spot = jnp.where(lane == sub, line.astype(F32), 0.0)
        return jnp.sum(spot, axis=1, keepdims=True).astype(I32)

    ow_r, lo_r = as_row(owner), as_row(local)
    ow_c, lo_c = as_column(ow_r), as_column(lo_r)
    ar, br = ow_r // SIDE, ow_r % SIDE
    ac, bc = ow_c // SIDE, ow_c % SIDE
    br, bc = br + at.core * (ar - br), bc + at.core * (ac - bc)
    ac = ac + at.core * (ow_c % SIDE - ac)
    id_r, id_c = ow_r * BLOCKS + lo_r, ow_c * BLOCKS + lo_c
    twin = id_r == id_c

    def count(mask, axis):
        ones = jnp.where(mask, 1.0, 0.0).astype(F32)
        return jnp.sum(ones, axis=axis, keepdims=True).astype(I32)

    first_r = count(twin & (sub < lane), 0) == 0
    first_c = count(twin & (lane < sub), 1) == 0
    rank_c = count((bc == br) & (lane < sub) & first_r, 1)
    pos_r = jnp.sum(jnp.where(twin & first_c, rank_c, 0), axis=0, keepdims=True)
    idx_c = ac * BLOCKS + lo_c
    for g in range(SIDE):
        wanted = first_c & (bc == g) & (rank_c == lane)
        table = jnp.sum(jnp.where(wanted, idx_c, 0), axis=0, keepdims=True)
        tab_out[g] = jnp.broadcast_to(table, (8, LISTED))
    line = lax.broadcasted_iota(I32, (8, LISTED), 0)
    pos_v[...] = jnp.where(line == 0, br * LISTED + pos_r, id_r)
    tables = [
        remote(
            tab_out.at[at.on_b(k)], tab_in.at[k], t_send.at[k - 1], t_recv.at[k - 1], at.dev_b(k)
        )
        for k in range(1, SIDE)
    ]
    start(tables)

    x_c, z_c = ow_c // SIDE, ow_c % SIDE
    x_r, z_r = ow_r // SIDE, ow_r % SIDE
    most = jnp.zeros((1, 1), F32)
    for mine_c, mine_r, here in ((x_c, x_r, at.seq // SIDE), (z_c, z_r, at.seq % SIDE)):
        rank = count((mine_c == mine_r) & (lane < sub) & first_r, 1)
        wanted = jnp.where(first_c & (mine_c != here), rank + 1, 0).astype(F32)
        most = jnp.maximum(most, jnp.max(wanted, axis=0, keepdims=True))
    need_a[at.a] = jnp.broadcast_to(most, (8, LISTED)).astype(I32)
    need_along_a = [
        remote(
            need_a.at[at.a], need_a.at[at.a], n_send.at[k - 1], n_recv.at[k - 1], at.dev_a(k)
        )
        for k in range(1, SIDE)
    ]
    start(need_along_a)
    tab_in[0] = tab_out[at.b]
    pos_copy = pltpu.make_async_copy(pos_v, pos, l_sem.at[3])
    pos_copy.start()

    passed = []
    lower, upper = pl.ds(0, per), pl.ds(per, per)
    for t in range(2):
        gather[4 * t].wait_recv()
        ref = row.at[t, at.on_a(3), lower]
        passed.append(remote(ref, ref, a_send.at[t, 4], a_recv.at[t, 4], at.dev_a(1)))
        passed[-1].start()
        gather[4 * t + 1].wait_recv()
        ref = row.at[t, at.on_a(1), upper]
        passed.append(remote(ref, ref, a_send.at[t, 5], a_recv.at[t, 5], at.dev_a(3)))
        passed[-1].start()

    take = 16
    pick_r = lax.broadcasted_iota(I32, (take, take * BLK), 0)
    pick_c = lax.broadcasted_iota(I32, (take, take * BLK), 1) // BLK
    averager = jnp.where(pick_r == pick_c, 1.0 / BLK, 0.0).astype(BF16)
    for t in range(2):
        to_x[t].wait_recv()
    for t in range(2):
        for i in range(BLOCKS // take):
            where = pl.ds(i * take, take)
            tokens = both[t, where].reshape(take * BLK, HD)
            mean = jnp.dot(averager, tokens, preferred_element_type=F32)
            mean_a[at.a, t, where] = mean.astype(BF16)
    own_out = pltpu.make_async_copy(both, own, l_sem.at[4])
    own_out.start()
    along_a = [
        remote(
            mean_a.at[at.a], mean_a.at[at.a], m_send.at[k - 1], m_recv.at[k - 1], at.dev_a(k)
        )
        for k in range(1, SIDE)
    ]
    start(along_a)
    for copy in along_a + need_along_a:
        copy.wait_recv()
    need_b[at.b] = jnp.max(need_a[...], axis=0)
    need_along_b = [
        remote(
            need_b.at[at.b], need_b.at[at.b], n_send.at[k + 2], n_recv.at[k + 2], at.dev_b(k)
        )
        for k in range(1, SIDE)
    ]
    start(need_along_b)
    for k in range(SIDE):
        mean_b[at.b, k] = mean_a[k]
    along_b = [
        remote(
            mean_b.at[at.b], mean_b.at[at.b], m_send.at[k + 2], m_recv.at[k + 2], at.dev_b(k)
        )
        for k in range(1, SIDE)
    ]
    start(along_b)
    for copy in along_b + need_along_b:
        copy.wait_recv()
    need[...] = jnp.max(need_b[...], axis=0)
    mean_out = [
        pltpu.make_async_copy(
            mean_b.at[n, m], means.at[m * at.stride_a + n * at.stride_b], l_sem.at[7 + n * SIDE + m]
        )
        for n in range(SIDE)
        for m in range(SIDE)
    ]
    start(mean_out)
    for copy in tables:
        copy.wait_recv()
    tab_copy = pltpu.make_async_copy(tab_in, tabs, l_sem.at[23])
    tab_copy.start()

    rows_out = []
    for t in range(2):
        gather[4 * t + 2].wait_recv()
        gather[4 * t + 3].wait_recv()
        passed[2 * t].wait_recv()
        passed[2 * t + 1].wait_recv()
        own_row[t].wait()
        rows_out.append(pltpu.make_async_copy(row.at[t], rows.at[t], l_sem.at[5 + t]))
        rows_out[-1].start()
    for copy in asked:
        copy.wait()
    for copy in rows_out + mean_out + [own_q, later_q, pos_copy, own_out, tab_copy]:
        copy.wait()
    for copy in gather + passed + to_x + tables + along_a + along_b + need_along_a + need_along_b:
        copy.wait_send()


def spread(keys, values, queries, owner, local):
    vmem, hbm = pl.BlockSpec(memory_space=pltpu.VMEM), pl.BlockSpec(memory_space=pl.ANY)
    q_rows = queries.shape[0] // HEADS
    row_shape = (2, SIDE, BLOCKS, HALF, HD)
    own_shape = (2, BLOCKS, BLK, HD)
    mean_shape = (2, BLOCKS, HD)
    return pl.pallas_call(
        spread_kernel,
        out_shape=(
            jax.ShapeDtypeStruct(row_shape, BF16),
            jax.ShapeDtypeStruct(own_shape, BF16),
            jax.ShapeDtypeStruct((SIDE * SIDE,) + mean_shape, BF16),
            jax.ShapeDtypeStruct((HEADS, q_rows // 2, HD), BF16),
            jax.ShapeDtypeStruct((HEADS, q_rows // 2, HD), BF16),
            jax.ShapeDtypeStruct((SIDE, 8, LISTED), I32),
            jax.ShapeDtypeStruct((8, LISTED), I32),
            jax.ShapeDtypeStruct((8, LISTED), I32),
        ),
        in_specs=[hbm, hbm, hbm, vmem, vmem],
        out_specs=(hbm,) * 7 + (vmem,),
        scratch_shapes=[
            pltpu.VMEM((2, BLOCKS, HALF * KVH, HD), BF16),
            pltpu.VMEM(queries.shape, BF16),
            pltpu.VMEM((2, BLOCKS, HALF, HD), BF16),
            pltpu.VMEM(row_shape, BF16),
            pltpu.VMEM(own_shape, BF16),
            pltpu.VMEM((HEADS, q_rows, HD), BF16),
            pltpu.VMEM((SIDE, 8, LISTED), I32),
            pltpu.VMEM((SIDE, 8, LISTED), I32),
            pltpu.VMEM((8, LISTED), I32),
            pltpu.VMEM((SIDE, 8, LISTED), I32),
            pltpu.VMEM((SIDE, 8, LISTED), I32),
            pltpu.VMEM((SIDE,) + mean_shape, BF16),
            pltpu.VMEM((SIDE, SIDE) + mean_shape, BF16),
            DMA((5,)), DMA((2, 6)), DMA((2, 6)), DMA((HEADS - 1,)), DMA((HEADS - 1,)),
            DMA((3,)), DMA((3,)), DMA((6,)), DMA((6,)), DMA((6,)), DMA((6,)),
            DMA((2,)), DMA((2,)), DMA((25,)),
        ],
        compiler_params=pltpu.CompilerParams(
            collective_id=0, has_side_effects=True, vmem_limit_bytes=60 * MIB
        ),
        name="spread",
    )(keys, values, queries, owner, local)


def scores(left, right):
    return lax.dot_general(left, right, (((1,), (1,)), ((), ())), preferred_element_type=F32)


def pick_kernel(
    cap, tabs, pos, rows, own, means, q_first, q_later, out,
    row_k, row_v, both, mean, q, sendbuf, recv_k, recv_v, far, weights, base, q_mean, c_max, c_sum, c_val, o_st,
    in_sem, s_send, s_recv, x_send, x_recv, q_send, q_recv, o_sem,
):
    at = Place()
    row, recv = (row_k, row_v), (recv_k, recv_v)
    early, late = pl.ds(0, q.shape[1] // 2), pl.ds(q.shape[1] // 2, q.shape[1] // 2)
    loads = [pltpu.make_async_copy(rows.at[t], row[t], in_sem.at[t]) for t in range(2)]
    loads += [
        pltpu.make_async_copy(q_first, q.at[:, early], in_sem.at[2]),
        pltpu.make_async_copy(means, mean, in_sem.at[3]),
        pltpu.make_async_copy(own, both, in_sem.at[4]),
        pltpu.make_async_copy(q_later.at[at.head], q.at[at.head, late], in_sem.at[5]),
    ]
    start(loads)
    greet([at.dev_b(k) for k in range(1, SIDE)] + [at.dev_head(k) for k in range(1, HEADS)])

    picks = [[], []]
    offsets = (2, 1, 3)

    def collect(t):
        blocks = row[t].reshape(SIDE * BLOCKS, HALF, HD)
        loads[t].wait()
        for n, k in enumerate(offsets):

            @pl.loop(0, cap // 4)
            def _(i, k=k):
                for u in range(4):
                    sendbuf[t, k - 1, i * 4 + u] = blocks[tabs[k, 0, i * 4 + u]]

            picks[t].append(
                remote(
                    sendbuf.at[t, k - 1], recv[t].at[at.b, pl.ds(0, cap)],
                    s_send.at[t, n], s_recv.at[t, n], at.dev_b(-k % SIDE),
                )
            )
            if t == 0:
                picks[t][-1].start()

        @pl.loop(0, MOST // 8)
        def _(i):
            for u in range(8):
                recv[t][at.b, i * 8 + u] = blocks[tabs[0, 0, i * 8 + u]]

    collect(0)
    asked = [
        remote(
            q_later.at[(at.head + k) % HEADS], q.at[at.head, late],
            q_send.at[k - 1], q_recv.at[k - 1], at.dev_head(k),
        )
        for k in range(1, HEADS)
    ]
    start(asked)
    collect(1)

    to_log2 = math.log2(math.e)
    scale = HD**-0.5 * to_log2
    which = lax.broadcasted_iota(I32, (8, ROWS), 0)
    column = lax.broadcasted_iota(I32, (8, ROWS), 1)
    parity = jnp.where(which == column % 2, 1.0 / BLK, 0.0).astype(BF16)
    for n in (2, 3, 5):
        loads[n].wait()
    for copy in asked:
        copy.wait_recv()
    per_owner = q.shape[1] // ROWS

    def q_rows(i):
        first = pl.multiple_of((i % per_owner) * ROWS, ROWS)
        return q[i // per_owner, pl.ds(first, ROWS)]

    @pl.loop(0, BLOCKS // 4)
    def _(i):
        for u in range(4):
            q_mean[i * 4 + u] = jnp.dot(parity, q_rows(i * 4 + u), preferred_element_type=F32)

    group = 8
    total_blocks = SIDE * SIDE * BLOCKS
    key_means = mean[:, 0].reshape(total_blocks, HD)
    value_means = mean[:, 1].reshape(total_blocks, HD)

    @pl.loop(0, BLOCKS // group)
    def _(i):
        where = pl.ds(i * group, group)
        means_f = q_mean[where].reshape(group * 8, HD)
        high = means_f.astype(BF16)
        rest = means_f - high.astype(F32)
        mid = rest.astype(BF16)
        low = (rest - mid.astype(F32)).astype(BF16)
        coarse = scores(high, key_means) + scores(mid, key_means) + scores(low, key_means)
        coarse = coarse * scale + math.log2(BLK)
        number = lax.broadcasted_iota(I32, (8, total_blocks), 1)
        kept = []
        for u in range(group):
            block = i * group + u
            gone = number == at.seq * BLOCKS + block
            for r in range(REFINE):
                gone = gone | (number == pos[1, r * BLOCKS + block])
            kept.append(jnp.where(gone, 0.0, 1.0))
        kept = jnp.concatenate(kept, axis=0) > 0.0
        coarse = jnp.where(kept, coarse, -1e30)
        top = jnp.max(coarse, axis=1, keepdims=True)
        part = jnp.where(kept, jnp.exp2(coarse - top), 0.0)
        c_max[where] = jnp.broadcast_to(top, (group * 8, HD)).reshape(group, 8, HD)
        total = jnp.sum(part, axis=1, keepdims=True)
        c_sum[where] = jnp.broadcast_to(total, (group * 8, HD)).reshape(group, 8, HD)
        value = jnp.dot(part.astype(BF16), value_means, preferred_element_type=F32)
        c_val[where] = value.reshape(group, 8, HD)

    for copy in picks[0]:
        copy.wait_send()
    start(picks[1])
    loads[4].wait()

    my_half = pl.ds(at.core * HALF, HALF)
    pieces = 4
    piece, blocks_piece = LISTED // pieces, BLOCKS // pieces

    def listed_blocks(t):
        for copy in picks[t]:
            copy.wait_recv()
        copies = []
        for p in range(pieces):

            @pl.loop(p * blocks_piece // 2, (p + 1) * blocks_piece // 2)
            def _(j):
                for u in range(2):
                    for r in range(REFINE):
                        i = j * 2 + u
                        place = pos[0, r * BLOCKS + i]
                        far[t, i * REFINE + r, my_half] = recv[t][place // LISTED, place % LISTED]

            ref = far.at[t, pl.ds(p * piece, piece), my_half]
            copies.append(
                remote(ref, ref, x_send.at[t, p], x_recv.at[t, p], at.sibling)
            )
            copies[-1].start()
        return copies

    odd = lax.broadcasted_iota(I32, (ROWS, 1), 0) % 2 == 1

    def per_row(ref, i, width):
        return jnp.where(odd, ref[i, 1:2, :width], ref[i, 0:1, :width])

    key_copies = listed_blocks(0)
    for p in range(pieces):
        key_copies[p].wait_recv()

        @pl.loop(p * blocks_piece // 4, (p + 1) * blocks_piece // 4)
        def _(j):
            for u in range(4):
                i = j * 4 + u
                block_keys = jnp.concatenate(
                    [both[0, i], far[0, pl.ds(i * REFINE, REFINE)].reshape(REFINE * BLK, HD)], axis=0
                )
                fine = scores(q_rows(i), block_keys) * scale
                coarse_top = per_row(c_max, i, 1)
                top = jnp.maximum(coarse_top, jnp.max(fine, axis=1, keepdims=True))
                fine = jnp.exp2(fine - top)
                alpha = jnp.exp2(coarse_top - top)
                total = alpha * per_row(c_sum, i, 1) + jnp.sum(fine, axis=1, keepdims=True)
                share = 1.0 / total
                weights[i] = (fine * share).astype(BF16)
                base[i] = (alpha * share) * per_row(c_val, i, HD)

    value_copies = listed_blocks(1)
    outs = []
    for p in range(pieces):
        value_copies[p].wait_recv()

        @pl.loop(p * blocks_piece // 4, (p + 1) * blocks_piece // 4)
        def _(j):
            for u in range(4):
                i = j * 4 + u
                block_values = jnp.concatenate(
                    [both[1, i], far[1, pl.ds(i * REFINE, REFINE)].reshape(REFINE * BLK, HD)], axis=0
                )
                result = jnp.dot(weights[i], block_values, preferred_element_type=F32) + base[i]
                o_st[i] = result.astype(BF16)

        where = pl.ds(p * blocks_piece, blocks_piece)
        outs.append(pltpu.make_async_copy(o_st.at[where], out.at[where], o_sem.at[p]))
        outs[-1].start()

    for copy in outs:
        copy.wait()
    for copy in key_copies + value_copies + picks[1] + asked:
        copy.wait_send()


def pick(collective_id, cap, rows, own, means, q_first, q_later, tabs, pos):
    smem, hbm = pl.BlockSpec(memory_space=pltpu.SMEM), pl.BlockSpec(memory_space=pl.ANY)
    q_shape = (HEADS, 2 * q_first.shape[1], HD)
    return pl.pallas_call(
        functools.partial(pick_kernel, cap),
        out_shape=jax.ShapeDtypeStruct((BLOCKS, ROWS, HD), BF16),
        in_specs=[smem, smem, hbm, hbm, hbm, hbm, hbm],
        out_specs=hbm,
        scratch_shapes=[
            pltpu.VMEM(rows.shape[1:], BF16),
            pltpu.VMEM(rows.shape[1:], BF16),
            pltpu.VMEM(own.shape, BF16),
            pltpu.VMEM(means.shape, BF16),
            pltpu.VMEM(q_shape, BF16),
            pltpu.VMEM((2, SIDE - 1, cap, HALF, HD), BF16),
            pltpu.VMEM((SIDE, MOST, HALF, HD), BF16),
            pltpu.VMEM((SIDE, MOST, HALF, HD), BF16),
            pltpu.VMEM((2, LISTED, BLK, HD), BF16),
            pltpu.VMEM((BLOCKS, ROWS, (REFINE + 1) * BLK), BF16),
            pltpu.VMEM((BLOCKS, ROWS, HD), F32),
            pltpu.VMEM((BLOCKS, 8, HD), F32),
            pltpu.VMEM((BLOCKS, 8, HD), F32),
            pltpu.VMEM((BLOCKS, 8, HD), F32),
            pltpu.VMEM((BLOCKS, 8, HD), F32),
            pltpu.VMEM((BLOCKS, ROWS, HD), BF16),
            DMA((6,)), DMA((2, 3)), DMA((2, 3)), DMA((2, 4)), DMA((2, 4)),
            DMA((HEADS - 1,)), DMA((HEADS - 1,)), DMA((4,)),
        ],
        compiler_params=pltpu.CompilerParams(
            collective_id=collective_id, has_side_effects=True, vmem_limit_bytes=60 * MIB
        ),
        name="pick",
    )(tabs, pos, rows, own, means, q_first, q_later)


def hand_on_kernel(src, dst, held, in_sem, out_sem):
    parts = in_sem.shape[0]
    per = BLOCKS // parts
    where = [pl.ds(p * per, per) for p in range(parts)]
    inward = [
        pltpu.make_async_copy(src.at[w], held.at[w], in_sem.at[p]) for p, w in enumerate(where)
    ]
    outward = [
        pltpu.make_async_copy(held.at[w], dst.at[w], out_sem.at[p]) for p, w in enumerate(where)
    ]
    start(inward)
    for before, after in zip(inward, outward):
        before.wait()
        after.start()
    for copy in outward:
        copy.wait()


def hand_on(result):
    hbm = pl.BlockSpec(memory_space=pl.ANY)
    return pl.pallas_call(
        hand_on_kernel,
        out_shape=jax.ShapeDtypeStruct(result.shape, result.dtype),
        in_specs=[hbm],
        out_specs=hbm,
        scratch_shapes=[pltpu.VMEM(result.shape, result.dtype), DMA((8,)), DMA((8,))],
        compiler_params=pltpu.CompilerParams(vmem_limit_bytes=60 * MIB),
        name="hand_on",
    )(result)


def on_device(queries, keys, values, refine_owner, refine_local):
    *moved, need = spread(
        keys.reshape(BLOCKS, BLK * KVH, HD),
        values.reshape(BLOCKS, BLK * KVH, HD),
        queries.reshape(-1, HD),
        refine_owner.T,
        refine_local.T,
    )
    caps = (40, 44, 52, MOST)
    most = need[0, 0]
    level = sum((most > cap).astype(I32) for cap in caps[:-1])

    def branch(n):
        return lambda *operands: hand_on(pick(n + 1, caps[n], *operands))

    out = lax.switch(level, [branch(n) for n in range(len(caps))], *moved)
    return out.reshape(BLOCKS * BLK, 2, HD)


def solution(mesh):
    return jax.shard_map(
        on_device,
        mesh=mesh,
        in_specs=(
            P(("seq", "head"), None, None),
            P("seq", None, None),
            P("seq", None, None),
            P("seq", None),
            P("seq", None),
        ),
        out_specs=P("seq", "head", None),
        check_vma=False,
    )
```

```python
import functools
import math

import jax
import jax.numpy as jnp
from jax import lax
from jax.experimental import pallas as pl
from jax.experimental.pallas import tpu as pltpu
from jax.sharding import PartitionSpec as P

MESH = pl.DeviceIdType.MESH
BLK = 128
HD = 128
KVH = 4
SIDE = 4
BLOCKS = 32
LISTED = 128
REFINE = 4
HEADS = 8
HALF = BLK // 2
MOST = 64
ROWS = 2 * BLK
MIB = 2**20
F32, BF16, I32 = jnp.float32, jnp.bfloat16, jnp.int32
DMA = pltpu.SemaphoreType.DMA


class Place:
    def __init__(self):
        self.seq, self.head = lax.axis_index("seq"), lax.axis_index("head")
        self.core = self.head % 2
        x, z = self.seq // SIDE, self.seq % SIDE
        self.a, self.b = x + self.core * (z - x), z + self.core * (x - z)
        self.stride_a, self.stride_b = SIDE - 3 * self.core, 1 + 3 * self.core
        self.sibling = (self.seq, self.head + 1 - 2 * self.core)

    def on_a(self, k):
        return (self.a + k) % SIDE

    def on_b(self, k):
        return (self.b + k) % SIDE

    def dev_a(self, k):
        return (self.on_a(k) * self.stride_a + self.b * self.stride_b, self.head)

    def dev_b(self, k):
        return (self.a * self.stride_a + self.on_b(k) * self.stride_b, self.head)

    def dev_head(self, k):
        return (self.seq, (self.head + k) % HEADS)


def remote(src, dst, send, recv, dev):
    return pltpu.make_async_remote_copy(
        src_ref=src, dst_ref=dst, send_sem=send, recv_sem=recv, device_id=dev, device_id_type=MESH
    )


def greet(peers):
    barrier = pltpu.get_barrier_semaphore()
    for dev in peers:
        pl.semaphore_signal(barrier, inc=1, device_id=dev, device_id_type=MESH)
    pl.semaphore_wait(barrier, len(peers))


def start(copies):
    for copy in copies:
        copy.start()


def spread_kernel(
    keys, values, queries, owner, local,
    rows, own, means, q_out, q_later, tabs, pos, need,
    kv_in, q_in, half, row, both, q_st, tab_out, tab_in, pos_v, need_a, need_b, mean_a, mean_b,
    in_sem, a_send, a_recv, q_send, q_recv, t_send, t_recv, n_send, n_recv, m_send, m_recv, x_send, x_recv, l_sem,
):
    at = Place()
    kv = at.head // 2
    parts = 2
    per = BLOCKS // parts
    loads = []
    for t, src in enumerate((keys, values)):
        for p in range(parts):
            where = pl.ds(p * per, per)
            loads.append(
                pltpu.make_async_copy(
                    src.at[where, pl.ds(at.core * (HALF * KVH), HALF * KVH)],
                    kv_in.at[t, where],
                    in_sem.at[t * parts + p],
                )
            )
    loads.append(pltpu.make_async_copy(queries, q_in, in_sem.at[2 * parts]))
    start(loads)

    greet(
        [at.dev_a(k) for k in range(1, SIDE)]
        + [at.dev_b(k) for k in range(1, SIDE)]
        + [at.dev_head(k) for k in range(1, HEADS)]
    )

    out_row = lax.broadcasted_iota(I32, (HALF, HALF * KVH), 0)
    in_row = lax.broadcasted_iota(I32, (HALF, HALF * KVH), 1)
    chooser = jnp.where(in_row == out_row * KVH + kv, 1.0, 0.0).astype(BF16)
    my_half = pl.ds(at.core * HALF, HALF)
    gather, to_x = [], []
    order = ((0, 1, 0), (1, 3, 2), (1, 1, 1), (0, 3, 3))
    for t in range(2):
        for p in range(parts):
            loads[t * parts + p].wait()

            @pl.loop(p * per // 4, (p + 1) * per // 4)
            def _(i, t=t):
                for u in range(4):
                    picked = jnp.dot(chooser, kv_in[t, i * 4 + u], preferred_element_type=F32)
                    picked = picked.astype(BF16)
                    half[t, i * 4 + u] = picked
                    both[t, i * 4 + u, my_half] = picked

            for part, k, n in order[:1] if p == 0 else order[1:]:
                where = pl.ds(part * per, per)
                gather.append(
                    remote(
                        half.at[t, where], row.at[t, at.a, where],
                        a_send.at[t, n], a_recv.at[t, n], at.dev_a(k),
                    )
                )
                gather[-1].start()
        to_x.append(
            remote(
                both.at[t, :, my_half], both.at[t, :, my_half],
                x_send.at[t], x_recv.at[t], at.sibling,
            )
        )
        to_x[-1].start()
    own_row = [pltpu.make_async_copy(half.at[t], row.at[t, at.a], l_sem.at[t]) for t in range(2)]
    start(own_row)

    loads[-1].wait()
    step = 16
    out_row = lax.broadcasted_iota(I32, (16 * step, 16 * step), 0)
    in_row = lax.broadcasted_iota(I32, (16 * step, 16 * step), 1)
    pair, rest = out_row // (2 * step), out_row % (2 * step)
    order = jnp.where(in_row == (rest // 2) * 16 + pair * 2 + rest % 2, 1.0, 0.0).astype(BF16)
    chunks = q_in.shape[0] // (16 * step)

    def turn(low, high):
        @pl.loop(low // 2, high // 2)
        def _(i):
            for u in range(2):
                first = pl.multiple_of((i * 2 + u) * 16 * step, 16 * step)
                turned = jnp.dot(order, q_in[pl.ds(first, 16 * step)], preferred_element_type=F32)
                turned = turned.astype(BF16)
                place = pl.multiple_of((i * 2 + u) * 2 * step, 2 * step)
                for h in range(HEADS):
                    q_st[h, pl.ds(place, 2 * step)] = turned[h * 2 * step : (h + 1) * 2 * step]

    turn(0, chunks // 2)
    now = pl.ds(0, q_st.shape[1] // 2)
    asked = [
        remote(
            q_st.at[(at.head + k) % HEADS, now], q_out.at[at.head],
            q_send.at[k - 1], q_recv.at[k - 1], at.dev_head(k),
        )
        for k in range(1, HEADS)
    ]
    start(asked)
    own_q = pltpu.make_async_copy(q_st.at[at.head, now], q_out.at[at.head], l_sem.at[2])
    own_q.start()
    turn(chunks // 2, chunks)
    later = pl.ds(q_st.shape[1] // 2, q_st.shape[1] // 2)
    later_q = pltpu.make_async_copy(q_st.at[:, later], q_later, l_sem.at[24])
    later_q.start()

    lane = lax.broadcasted_iota(I32, (LISTED, LISTED), 1)
    sub = lax.broadcasted_iota(I32, (LISTED, LISTED), 0)

    def as_row(ref):
        return jnp.concatenate([ref[r : r + 1] for r in range(REFINE)], axis=1)

    def as_column(line):
        spot = jnp.where(lane == sub, line.astype(F32), 0.0)
        return jnp.sum(spot, axis=1, keepdims=True).astype(I32)

    ow_r, lo_r = as_row(owner), as_row(local)
    ow_c, lo_c = as_column(ow_r), as_column(lo_r)
    ar, br = ow_r // SIDE, ow_r % SIDE
    ac, bc = ow_c // SIDE, ow_c % SIDE
    br, bc = br + at.core * (ar - br), bc + at.core * (ac - bc)
    ac = ac + at.core * (ow_c % SIDE - ac)
    id_r, id_c = ow_r * BLOCKS + lo_r, ow_c * BLOCKS + lo_c
    twin = id_r == id_c

    def count(mask, axis):
        ones = jnp.where(mask, 1.0, 0.0).astype(F32)
        return jnp.sum(ones, axis=axis, keepdims=True).astype(I32)

    first_r = count(twin & (sub < lane), 0) == 0
    first_c = count(twin & (lane < sub), 1) == 0
    rank_c = count((bc == br) & (lane < sub) & first_r, 1)
    pos_r = jnp.sum(jnp.where(twin & first_c, rank_c, 0), axis=0, keepdims=True)
    idx_c = ac * BLOCKS + lo_c
    for g in range(SIDE):
        wanted = first_c & (bc == g) & (rank_c == lane)
        table = jnp.sum(jnp.where(wanted, idx_c, 0), axis=0, keepdims=True)
        tab_out[g] = jnp.broadcast_to(table, (8, LISTED))
    line = lax.broadcasted_iota(I32, (8, LISTED), 0)
    pos_v[...] = jnp.where(line == 0, br * LISTED + pos_r, id_r)
    tables = [
        remote(
            tab_out.at[at.on_b(k)], tab_in.at[k], t_send.at[k - 1], t_recv.at[k - 1], at.dev_b(k)
        )
        for k in range(1, SIDE)
    ]
    start(tables)

    x_c, z_c = ow_c // SIDE, ow_c % SIDE
    x_r, z_r = ow_r // SIDE, ow_r % SIDE
    most = jnp.zeros((1, 1), F32)
    for mine_c, mine_r, here in ((x_c, x_r, at.seq // SIDE), (z_c, z_r, at.seq % SIDE)):
        rank = count((mine_c == mine_r) & (lane < sub) & first_r, 1)
        wanted = jnp.where(first_c & (mine_c != here), rank + 1, 0).astype(F32)
        most = jnp.maximum(most, jnp.max(wanted, axis=0, keepdims=True))
    need_a[at.a] = jnp.broadcast_to(most, (8, LISTED)).astype(I32)
    need_along_a = [
        remote(
            need_a.at[at.a], need_a.at[at.a], n_send.at[k - 1], n_recv.at[k - 1], at.dev_a(k)
        )
        for k in range(1, SIDE)
    ]
    start(need_along_a)
    tab_in[0] = tab_out[at.b]
    pos_copy = pltpu.make_async_copy(pos_v, pos, l_sem.at[3])
    pos_copy.start()

    passed = []
    lower, upper = pl.ds(0, per), pl.ds(per, per)
    for t in range(2):
        gather[4 * t].wait_recv()
        ref = row.at[t, at.on_a(3), lower]
        passed.append(remote(ref, ref, a_send.at[t, 4], a_recv.at[t, 4], at.dev_a(1)))
        passed[-1].start()
        gather[4 * t + 1].wait_recv()
        ref = row.at[t, at.on_a(1), upper]
        passed.append(remote(ref, ref, a_send.at[t, 5], a_recv.at[t, 5], at.dev_a(3)))
        passed[-1].start()

    take = 16
    pick_r = lax.broadcasted_iota(I32, (take, take * BLK), 0)
    pick_c = lax.broadcasted_iota(I32, (take, take * BLK), 1) // BLK
    averager = jnp.where(pick_r == pick_c, 1.0 / BLK, 0.0).astype(BF16)
    for t in range(2):
        to_x[t].wait_recv()
    for t in range(2):
        for i in range(BLOCKS // take):
            where = pl.ds(i * take, take)
            tokens = both[t, where].reshape(take * BLK, HD)
            mean = jnp.dot(averager, tokens, preferred_element_type=F32)
            mean_a[at.a, t, where] = mean.astype(BF16)
    own_out = pltpu.make_async_copy(both, own, l_sem.at[4])
    own_out.start()
    along_a = [
        remote(
            mean_a.at[at.a], mean_a.at[at.a], m_send.at[k - 1], m_recv.at[k - 1], at.dev_a(k)
        )
        for k in range(1, SIDE)
    ]
    start(along_a)
    for copy in along_a + need_along_a:
        copy.wait_recv()
    need_b[at.b] = jnp.max(need_a[...], axis=0)
    need_along_b = [
        remote(
            need_b.at[at.b], need_b.at[at.b], n_send.at[k + 2], n_recv.at[k + 2], at.dev_b(k)
        )
        for k in range(1, SIDE)
    ]
    start(need_along_b)
    for k in range(SIDE):
        mean_b[at.b, k] = mean_a[k]
    along_b = [
        remote(
            mean_b.at[at.b], mean_b.at[at.b], m_send.at[k + 2], m_recv.at[k + 2], at.dev_b(k)
        )
        for k in range(1, SIDE)
    ]
    start(along_b)
    for copy in along_b + need_along_b:
        copy.wait_recv()
    need[0, 0] = jnp.max(jnp.max(need_b[...], axis=0).astype(F32)).astype(I32)
    mean_out = [
        pltpu.make_async_copy(
            mean_b.at[n, m], means.at[m * at.stride_a + n * at.stride_b], l_sem.at[7 + n * SIDE + m]
        )
        for n in range(SIDE)
        for m in range(SIDE)
    ]
    start(mean_out)
    for copy in tables:
        copy.wait_recv()
    tab_copy = pltpu.make_async_copy(tab_in, tabs, l_sem.at[23])
    tab_copy.start()

    rows_out = []
    for t in range(2):
        gather[4 * t + 2].wait_recv()
        gather[4 * t + 3].wait_recv()
        passed[2 * t].wait_recv()
        passed[2 * t + 1].wait_recv()
        own_row[t].wait()
        rows_out.append(pltpu.make_async_copy(row.at[t], rows.at[t], l_sem.at[5 + t]))
        rows_out[-1].start()
    for copy in asked:
        copy.wait()
    for copy in rows_out + mean_out + [own_q, later_q, pos_copy, own_out, tab_copy]:
        copy.wait()
    for copy in gather + passed + to_x + tables + along_a + along_b + need_along_a + need_along_b:
        copy.wait_send()


def spread(keys, values, queries, owner, local):
    vmem, hbm = pl.BlockSpec(memory_space=pltpu.VMEM), pl.BlockSpec(memory_space=pl.ANY)
    q_rows = queries.shape[0] // HEADS
    row_shape = (2, SIDE, BLOCKS, HALF, HD)
    own_shape = (2, BLOCKS, BLK, HD)
    mean_shape = (2, BLOCKS, HD)
    return pl.pallas_call(
        spread_kernel,
        out_shape=(
            jax.ShapeDtypeStruct(row_shape, BF16),
            jax.ShapeDtypeStruct(own_shape, BF16),
            jax.ShapeDtypeStruct((SIDE * SIDE,) + mean_shape, BF16),
            jax.ShapeDtypeStruct((HEADS, q_rows // 2, HD), BF16),
            jax.ShapeDtypeStruct((HEADS, q_rows // 2, HD), BF16),
            jax.ShapeDtypeStruct((SIDE, 8, LISTED), I32),
            jax.ShapeDtypeStruct((8, LISTED), I32),
            jax.ShapeDtypeStruct((1, 1), I32),
        ),
        in_specs=[hbm, hbm, hbm, vmem, vmem],
        out_specs=(hbm,) * 7 + (pl.BlockSpec(memory_space=pltpu.SMEM),),
        scratch_shapes=[
            pltpu.VMEM((2, BLOCKS, HALF * KVH, HD), BF16),
            pltpu.VMEM(queries.shape, BF16),
            pltpu.VMEM((2, BLOCKS, HALF, HD), BF16),
            pltpu.VMEM(row_shape, BF16),
            pltpu.VMEM(own_shape, BF16),
            pltpu.VMEM((HEADS, q_rows, HD), BF16),
            pltpu.VMEM((SIDE, 8, LISTED), I32),
            pltpu.VMEM((SIDE, 8, LISTED), I32),
            pltpu.VMEM((8, LISTED), I32),
            pltpu.VMEM((SIDE, 8, LISTED), I32),
            pltpu.VMEM((SIDE, 8, LISTED), I32),
            pltpu.VMEM((SIDE,) + mean_shape, BF16),
            pltpu.VMEM((SIDE, SIDE) + mean_shape, BF16),
            DMA((5,)), DMA((2, 6)), DMA((2, 6)), DMA((HEADS - 1,)), DMA((HEADS - 1,)),
            DMA((3,)), DMA((3,)), DMA((6,)), DMA((6,)), DMA((6,)), DMA((6,)),
            DMA((2,)), DMA((2,)), DMA((25,)),
        ],
        compiler_params=pltpu.CompilerParams(
            collective_id=0, has_side_effects=True, vmem_limit_bytes=60 * MIB
        ),
        name="spread",
    )(keys, values, queries, owner, local)


def scores(left, right):
    return lax.dot_general(left, right, (((1,), (1,)), ((), ())), preferred_element_type=F32)


def pick_kernel(
    cap, tabs, pos, rows, own, means, q_first, q_later, out,
    row_k, row_v, both, mean, q, sendbuf, recv_k, recv_v, far, weights, base, q_mean, c_max, c_sum, c_val, o_st,
    in_sem, s_send, s_recv, x_send, x_recv, q_send, q_recv, o_sem,
):
    at = Place()
    row, recv = (row_k, row_v), (recv_k, recv_v)
    early, late = pl.ds(0, q.shape[1] // 2), pl.ds(q.shape[1] // 2, q.shape[1] // 2)
    loads = [pltpu.make_async_copy(rows.at[t], row[t], in_sem.at[t]) for t in range(2)]
    loads += [
        pltpu.make_async_copy(q_first, q.at[:, early], in_sem.at[2]),
        pltpu.make_async_copy(means, mean, in_sem.at[3]),
        pltpu.make_async_copy(own, both, in_sem.at[4]),
        pltpu.make_async_copy(q_later.at[at.head], q.at[at.head, late], in_sem.at[5]),
    ]
    start(loads)
    greet([at.dev_b(k) for k in range(1, SIDE)] + [at.dev_head(k) for k in range(1, HEADS)])

    picks = [[], []]
    offsets = (2, 1, 3)

    def collect(t):
        blocks = row[t].reshape(SIDE * BLOCKS, HALF, HD)
        loads[t].wait()
        for n, k in enumerate(offsets):

            @pl.loop(0, cap // 4)
            def _(i, k=k):
                for u in range(4):
                    sendbuf[t, k - 1, i * 4 + u] = blocks[tabs[k, 0, i * 4 + u]]

            picks[t].append(
                remote(
                    sendbuf.at[t, k - 1], recv[t].at[at.b, pl.ds(0, cap)],
                    s_send.at[t, n], s_recv.at[t, n], at.dev_b(-k % SIDE),
                )
            )
            if t == 0:
                picks[t][-1].start()

        @pl.loop(0, MOST // 8)
        def _(i):
            for u in range(8):
                recv[t][at.b, i * 8 + u] = blocks[tabs[0, 0, i * 8 + u]]

    collect(0)
    asked = [
        remote(
            q_later.at[(at.head + k) % HEADS], q.at[at.head, late],
            q_send.at[k - 1], q_recv.at[k - 1], at.dev_head(k),
        )
        for k in range(1, HEADS)
    ]
    start(asked)
    collect(1)

    to_log2 = math.log2(math.e)
    scale = HD**-0.5 * to_log2
    which = lax.broadcasted_iota(I32, (8, ROWS), 0)
    column = lax.broadcasted_iota(I32, (8, ROWS), 1)
    parity = jnp.where(which == column % 2, 1.0 / BLK, 0.0).astype(BF16)
    for n in (2, 3, 5):
        loads[n].wait()
    for copy in asked:
        copy.wait_recv()
    per_owner = q.shape[1] // ROWS

    def q_rows(i):
        first = pl.multiple_of((i % per_owner) * ROWS, ROWS)
        return q[i // per_owner, pl.ds(first, ROWS)]

    @pl.loop(0, BLOCKS // 4)
    def _(i):
        for u in range(4):
            q_mean[i * 4 + u] = jnp.dot(parity, q_rows(i * 4 + u), preferred_element_type=F32)

    group = 8
    total_blocks = SIDE * SIDE * BLOCKS
    key_means = mean[:, 0].reshape(total_blocks, HD)
    value_means = mean[:, 1].reshape(total_blocks, HD)

    @pl.loop(0, BLOCKS // group)
    def _(i):
        where = pl.ds(i * group, group)
        means_f = q_mean[where].reshape(group * 8, HD)
        high = means_f.astype(BF16)
        rest = means_f - high.astype(F32)
        mid = rest.astype(BF16)
        low = (rest - mid.astype(F32)).astype(BF16)
        coarse = scores(high, key_means) + scores(mid, key_means) + scores(low, key_means)
        coarse = coarse * scale + math.log2(BLK)
        number = lax.broadcasted_iota(I32, (8, total_blocks), 1)
        kept = []
        for u in range(group):
            block = i * group + u
            gone = number == at.seq * BLOCKS + block
            for r in range(REFINE):
                gone = gone | (number == pos[1, r * BLOCKS + block])
            kept.append(jnp.where(gone, 0.0, 1.0))
        kept = jnp.concatenate(kept, axis=0) > 0.0
        coarse = jnp.where(kept, coarse, -1e30)
        top = jnp.max(coarse, axis=1, keepdims=True)
        part = jnp.where(kept, jnp.exp2(coarse - top), 0.0)
        c_max[where] = jnp.broadcast_to(top, (group * 8, HD)).reshape(group, 8, HD)
        total = jnp.sum(part, axis=1, keepdims=True)
        c_sum[where] = jnp.broadcast_to(total, (group * 8, HD)).reshape(group, 8, HD)
        value = jnp.dot(part.astype(BF16), value_means, preferred_element_type=F32)
        c_val[where] = value.reshape(group, 8, HD)

    for copy in picks[0]:
        copy.wait_send()
    start(picks[1])
    loads[4].wait()

    my_half = pl.ds(at.core * HALF, HALF)
    pieces, unroll = x_send.shape[1], 4
    piece, blocks_piece = LISTED // pieces, BLOCKS // pieces

    def to_sibling(t, p):
        ref = far.at[t, pl.ds(p * piece, piece), my_half]
        return remote(ref, ref, x_send.at[t, p], x_recv.at[t, p], at.sibling)

    def line_up(t):
        for copy in picks[t]:
            copy.wait_recv()

        @pl.loop(0, pieces)
        def _(p):
            @pl.loop(0, blocks_piece // 2)
            def _(j):
                for u in range(2):
                    for r in range(REFINE):
                        i = p * blocks_piece + j * 2 + u
                        place = pos[0, r * BLOCKS + i]
                        far[t, i * REFINE + r, my_half] = recv[t][place // LISTED, place % LISTED]

            to_sibling(t, p).start()

    def fine_blocks(t, i):
        listed = far[t, pl.ds(i * REFINE, REFINE)].reshape(REFINE * BLK, HD)
        return jnp.concatenate([both[t, i], listed], axis=0)

    odd = lax.broadcasted_iota(I32, (ROWS, 1), 0) % 2 == 1

    def per_row(ref, i, width):
        return jnp.where(odd, ref[i, 1:2, :width], ref[i, 0:1, :width])

    line_up(0)

    @pl.loop(0, pieces)
    def _(p):
        to_sibling(0, p).wait_recv()

        @pl.loop(0, blocks_piece // unroll)
        def _(j):
            for u in range(unroll):
                i = p * blocks_piece + j * unroll + u
                fine = scores(q_rows(i), fine_blocks(0, i)) * scale
                coarse_top = per_row(c_max, i, 1)
                top = jnp.maximum(coarse_top, jnp.max(fine, axis=1, keepdims=True))
                fine = jnp.exp2(fine - top)
                alpha = jnp.exp2(coarse_top - top)
                total = alpha * per_row(c_sum, i, 1) + jnp.sum(fine, axis=1, keepdims=True)
                share = 1.0 / total
                weights[i] = (fine * share).astype(BF16)
                base[i] = (alpha * share) * per_row(c_val, i, HD)

    line_up(1)

    def to_out(p):
        where = pl.ds(p * blocks_piece, blocks_piece)
        return pltpu.make_async_copy(o_st.at[where], out.at[where], o_sem.at[p])

    @pl.loop(0, pieces)
    def _(p):
        to_sibling(1, p).wait_recv()

        @pl.loop(0, blocks_piece // unroll)
        def _(j):
            for u in range(unroll):
                i = p * blocks_piece + j * unroll + u
                result = jnp.dot(weights[i], fine_blocks(1, i), preferred_element_type=F32)
                o_st[i] = (result + base[i]).astype(BF16)

        to_out(p).start()

    @pl.loop(0, pieces)
    def _(p):
        to_out(p).wait()
        for t in range(2):
            to_sibling(t, p).wait_send()

    for copy in picks[1] + asked:
        copy.wait_send()


def pick(collective_id, cap, rows, own, means, q_first, q_later, tabs, pos):
    smem, hbm = pl.BlockSpec(memory_space=pltpu.SMEM), pl.BlockSpec(memory_space=pl.ANY)
    q_shape = (HEADS, 2 * q_first.shape[1], HD)
    return pl.pallas_call(
        functools.partial(pick_kernel, cap),
        out_shape=jax.ShapeDtypeStruct((BLOCKS, ROWS, HD), BF16),
        in_specs=[smem, smem, hbm, hbm, hbm, hbm, hbm],
        out_specs=hbm,
        scratch_shapes=[
            pltpu.VMEM(rows.shape[1:], BF16),
            pltpu.VMEM(rows.shape[1:], BF16),
            pltpu.VMEM(own.shape, BF16),
            pltpu.VMEM(means.shape, BF16),
            pltpu.VMEM(q_shape, BF16),
            pltpu.VMEM((2, SIDE - 1, cap, HALF, HD), BF16),
            pltpu.VMEM((SIDE, MOST, HALF, HD), BF16),
            pltpu.VMEM((SIDE, MOST, HALF, HD), BF16),
            pltpu.VMEM((2, LISTED, BLK, HD), BF16),
            pltpu.VMEM((BLOCKS, ROWS, (REFINE + 1) * BLK), BF16),
            pltpu.VMEM((BLOCKS, ROWS, HD), F32),
            pltpu.VMEM((BLOCKS, 8, HD), F32),
            pltpu.VMEM((BLOCKS, 8, HD), F32),
            pltpu.VMEM((BLOCKS, 8, HD), F32),
            pltpu.VMEM((BLOCKS, 8, HD), F32),
            pltpu.VMEM((BLOCKS, ROWS, HD), BF16),
            DMA((6,)), DMA((2, 3)), DMA((2, 3)), DMA((2, 4)), DMA((2, 4)),
            DMA((HEADS - 1,)), DMA((HEADS - 1,)), DMA((4,)),
        ],
        compiler_params=pltpu.CompilerParams(
            collective_id=collective_id, has_side_effects=True, vmem_limit_bytes=60 * MIB
        ),
        name="pick",
    )(tabs, pos, rows, own, means, q_first, q_later)


def hand_on_kernel(src, dst, held, in_sem, out_sem):
    parts = in_sem.shape[0]
    per = BLOCKS // parts
    where = [pl.ds(p * per, per) for p in range(parts)]
    inward = [
        pltpu.make_async_copy(src.at[w], held.at[w], in_sem.at[p]) for p, w in enumerate(where)
    ]
    outward = [
        pltpu.make_async_copy(held.at[w], dst.at[w], out_sem.at[p]) for p, w in enumerate(where)
    ]
    start(inward)
    for before, after in zip(inward, outward):
        before.wait()
        after.start()
    for copy in outward:
        copy.wait()


def hand_on(result):
    hbm = pl.BlockSpec(memory_space=pl.ANY)
    return pl.pallas_call(
        hand_on_kernel,
        out_shape=jax.ShapeDtypeStruct(result.shape, result.dtype),
        in_specs=[hbm],
        out_specs=hbm,
        scratch_shapes=[pltpu.VMEM(result.shape, result.dtype), DMA((8,)), DMA((8,))],
        compiler_params=pltpu.CompilerParams(vmem_limit_bytes=60 * MIB),
        name="hand_on",
    )(result)


def blank():
    def kernel(out):
        del out

    return pl.pallas_call(
        kernel,
        out_shape=jax.ShapeDtypeStruct((BLOCKS, ROWS, HD), BF16),
        out_specs=pl.BlockSpec(memory_space=pl.ANY),
        name="blank",
    )()


def on_device(queries, keys, values, refine_owner, refine_local):
    *moved, need = spread(
        keys.reshape(BLOCKS, BLK * KVH, HD),
        values.reshape(BLOCKS, BLK * KVH, HD),
        queries.reshape(-1, HD),
        refine_owner.T,
        refine_local.T,
    )
    caps = (40, 44, 52, MOST)
    most = need[0, 0]
    level = sum((most > cap).astype(I32) for cap in caps[:-1])

    def branch(n):
        return lambda *operands: hand_on(pick(n + 1, caps[n], *operands))

    out = blank()
    for n in range(len(caps)):
        run = branch(n)
        out = lax.fori_loop(0, (level == n).astype(I32), lambda _, kept: run(*moved), out)
    return out.reshape(BLOCKS * BLK, 2, HD)


def solution(mesh):
    return jax.shard_map(
        on_device,
        mesh=mesh,
        in_specs=(
            P(("seq", "head"), None, None),
            P("seq", None, None),
            P("seq", None, None),
            P("seq", None),
            P("seq", None),
        ),
        out_specs=P("seq", "head", None),
        check_vma=False,
    )
```

```python
import functools
import math

import jax
import jax.numpy as jnp
from jax import lax
from jax.experimental import pallas as pl
from jax.experimental.pallas import tpu as pltpu
from jax.sharding import PartitionSpec as P

MESH = pl.DeviceIdType.MESH
BLK = 128
HD = 128
KVH = 4
SIDE = 4
BLOCKS = 32
LISTED = 128
REFINE = 4
HEADS = 8
HALF = BLK // 2
MOST = 64
ROWS = 2 * BLK
MIB = 2**20
F32, BF16, I32 = jnp.float32, jnp.bfloat16, jnp.int32
DMA = pltpu.SemaphoreType.DMA


class Place:
    def __init__(self):
        self.seq, self.head = lax.axis_index("seq"), lax.axis_index("head")
        self.core = self.head % 2
        x, z = self.seq // SIDE, self.seq % SIDE
        self.a, self.b = x + self.core * (z - x), z + self.core * (x - z)
        self.stride_a, self.stride_b = SIDE - 3 * self.core, 1 + 3 * self.core
        self.sibling = (self.seq, self.head + 1 - 2 * self.core)

    def on_a(self, k):
        return (self.a + k) % SIDE

    def on_b(self, k):
        return (self.b + k) % SIDE

    def dev_a(self, k):
        return (self.on_a(k) * self.stride_a + self.b * self.stride_b, self.head)

    def dev_b(self, k):
        return (self.a * self.stride_a + self.on_b(k) * self.stride_b, self.head)

    def dev_head(self, k):
        return (self.seq, (self.head + k) % HEADS)


def remote(src, dst, send, recv, dev):
    return pltpu.make_async_remote_copy(
        src_ref=src, dst_ref=dst, send_sem=send, recv_sem=recv, device_id=dev, device_id_type=MESH
    )


def greet(peers):
    barrier = pltpu.get_barrier_semaphore()
    for dev in peers:
        pl.semaphore_signal(barrier, inc=1, device_id=dev, device_id_type=MESH)


def wait_greeted(peers):
    pl.semaphore_wait(pltpu.get_barrier_semaphore(), len(peers))


def start(copies):
    for copy in copies:
        copy.start()


def spread_kernel(
    keys, values, queries, owner, local,
    rows, own, means, q_out, q_later, tabs, pos, need,
    kv_in, q_in, half, both, q_st, tab_out, tab_in, pos_v, need_a, need_b, mean_a, mean_b,
    in_sem, a_send, a_recv, q_send, q_recv, t_send, t_recv, n_send, n_recv, m_send, m_recv, x_send, x_recv, l_sem,
):
    at = Place()
    kv = at.head // 2
    parts = 2
    per = BLOCKS // parts
    loads = []
    for t, src in enumerate((keys, values)):
        for p in range(parts):
            where = pl.ds(p * per, per)
            loads.append(
                pltpu.make_async_copy(
                    src.at[where, pl.ds(at.core * (HALF * KVH), HALF * KVH)],
                    kv_in.at[t, where],
                    in_sem.at[t * parts + p],
                )
            )
    loads.append(pltpu.make_async_copy(queries, q_in, in_sem.at[2 * parts]))
    start(loads)
    peers = [at.dev_a(k) for k in range(1, SIDE)]
    peers += [at.dev_b(k) for k in range(1, SIDE)]
    peers += [at.dev_head(k) for k in range(1, HEADS)]
    greet(peers)

    out_row = lax.broadcasted_iota(I32, (HALF, HALF * KVH), 0)
    in_row = lax.broadcasted_iota(I32, (HALF, HALF * KVH), 1)
    chooser = jnp.where(in_row == out_row * KVH + kv, 1.0, 0.0).astype(BF16)
    my_half = pl.ds(at.core * HALF, HALF)
    gather, to_x = [], []
    order = ((0, 1, 0), (1, 3, 2), (1, 1, 1), (0, 3, 3))
    for t in range(2):
        for p in range(parts):
            loads[t * parts + p].wait()

            @pl.loop(p * per // 4, (p + 1) * per // 4)
            def _(i, t=t):
                for u in range(4):
                    picked = jnp.dot(chooser, kv_in[t, i * 4 + u], preferred_element_type=F32)
                    picked = picked.astype(BF16)
                    half[t, i * 4 + u] = picked
                    both[t, i * 4 + u, my_half] = picked

            if t + p == 0:
                wait_greeted(peers)
            for part, k, n in order[:1] if p == 0 else order[1:]:
                where = pl.ds(part * per, per)
                gather.append(
                    remote(
                        half.at[t, where], rows.at[t, at.a, where],
                        a_send.at[t, n], a_recv.at[t, n], at.dev_a(k),
                    )
                )
                gather[-1].start()
        to_x.append(
            remote(
                both.at[t, :, my_half], both.at[t, :, my_half],
                x_send.at[t], x_recv.at[t], at.sibling,
            )
        )
        to_x[-1].start()
    own_row = [pltpu.make_async_copy(half.at[t], rows.at[t, at.a], l_sem.at[t]) for t in range(2)]
    start(own_row)

    loads[-1].wait()
    step = 16
    out_row = lax.broadcasted_iota(I32, (16 * step, 16 * step), 0)
    in_row = lax.broadcasted_iota(I32, (16 * step, 16 * step), 1)
    pair, rest = out_row // (2 * step), out_row % (2 * step)
    order = jnp.where(in_row == (rest // 2) * 16 + pair * 2 + rest % 2, 1.0, 0.0).astype(BF16)
    chunks = q_in.shape[0] // (16 * step)

    def turn(low, high):
        @pl.loop(low // 2, high // 2)
        def _(i):
            for u in range(2):
                first = pl.multiple_of((i * 2 + u) * 16 * step, 16 * step)
                turned = jnp.dot(order, q_in[pl.ds(first, 16 * step)], preferred_element_type=F32)
                turned = turned.astype(BF16)
                place = pl.multiple_of((i * 2 + u) * 2 * step, 2 * step)
                for h in range(HEADS):
                    q_st[h, pl.ds(place, 2 * step)] = turned[h * 2 * step : (h + 1) * 2 * step]

    turn(0, chunks // 2)
    now = pl.ds(0, q_st.shape[1] // 2)
    asked = [
        remote(
            q_st.at[(at.head + k) % HEADS, now], q_out.at[at.head],
            q_send.at[k - 1], q_recv.at[k - 1], at.dev_head(k),
        )
        for k in range(1, HEADS)
    ]
    start(asked)
    own_q = pltpu.make_async_copy(q_st.at[at.head, now], q_out.at[at.head], l_sem.at[2])
    own_q.start()
    passed = []
    lower, upper = pl.ds(0, per), pl.ds(per, per)

    def forward(t):
        gather[4 * t].wait_recv()
        ref = rows.at[t, at.on_a(3), lower]
        passed.append(remote(ref, ref, a_send.at[t, 4], a_recv.at[t, 4], at.dev_a(1)))
        passed[-1].start()
        gather[4 * t + 1].wait_recv()
        ref = rows.at[t, at.on_a(1), upper]
        passed.append(remote(ref, ref, a_send.at[t, 5], a_recv.at[t, 5], at.dev_a(3)))
        passed[-1].start()

    forward(0)
    turn(chunks // 2, chunks)
    later = pl.ds(q_st.shape[1] // 2, q_st.shape[1] // 2)
    later_q = pltpu.make_async_copy(q_st.at[:, later], q_later, l_sem.at[24])
    later_q.start()

    lane = lax.broadcasted_iota(I32, (LISTED, LISTED), 1)
    sub = lax.broadcasted_iota(I32, (LISTED, LISTED), 0)

    def as_row(ref):
        return jnp.concatenate([ref[r : r + 1] for r in range(REFINE)], axis=1)

    def as_column(line):
        spot = jnp.where(lane == sub, line.astype(F32), 0.0)
        return jnp.sum(spot, axis=1, keepdims=True).astype(I32)

    ow_r, lo_r = as_row(owner), as_row(local)
    ow_c, lo_c = as_column(ow_r), as_column(lo_r)
    x_r, z_r = ow_r // SIDE, ow_r % SIDE
    x_c, z_c = ow_c // SIDE, ow_c % SIDE
    id_r, id_c = ow_r * BLOCKS + lo_r, ow_c * BLOCKS + lo_c
    twin = id_r == id_c

    def count(mask, axis):
        ones = jnp.where(mask, 1.0, 0.0).astype(F32)
        return jnp.sum(ones, axis=axis, keepdims=True).astype(I32)

    first_r = count(twin & (sub < lane), 0) == 0
    first_c = count(twin & (lane < sub), 1) == 0
    rank_z = count((z_c == z_r) & (lane < sub) & first_r, 1)
    rank_x = count((x_c == x_r) & (lane < sub) & first_r, 1)
    places = [
        group * LISTED
        + jnp.sum(jnp.where(twin & first_c, rank, 0), axis=0, keepdims=True)
        for group, rank in ((z_r, rank_z), (x_r, rank_x))
    ]
    rank_c = rank_z + at.core * (rank_x - rank_z)
    ac, bc = x_c + at.core * (z_c - x_c), z_c + at.core * (x_c - z_c)
    idx_c = ac * BLOCKS + lo_c
    for g in range(SIDE):
        wanted = first_c & (bc == g) & (rank_c == lane)
        table = jnp.sum(jnp.where(wanted, idx_c, 0), axis=0, keepdims=True)
        tab_out[g] = jnp.broadcast_to(table, (8, LISTED))
    line = lax.broadcasted_iota(I32, (8, LISTED), 0)
    pos_v[...] = jnp.where(line == 0, places[0], jnp.where(line == 1, places[1], id_r))
    tables = [
        remote(
            tab_out.at[at.on_b(k)], tab_in.at[k], t_send.at[k - 1], t_recv.at[k - 1], at.dev_b(k)
        )
        for k in range(1, SIDE)
    ]
    start(tables)

    most = jnp.zeros((1, 1), F32)
    for group, rank, here in ((x_c, rank_x, at.seq // SIDE), (z_c, rank_z, at.seq % SIDE)):
        wanted = jnp.where(first_c & (group != here), rank + 1, 0).astype(F32)
        most = jnp.maximum(most, jnp.max(wanted, axis=0, keepdims=True))
    need_a[at.a] = jnp.broadcast_to(most, (8, LISTED)).astype(I32)
    need_along_a = [
        remote(
            need_a.at[at.a], need_a.at[at.a], n_send.at[k - 1], n_recv.at[k - 1], at.dev_a(k)
        )
        for k in range(1, SIDE)
    ]
    start(need_along_a)
    tab_in[0] = tab_out[at.b]
    pos_copy = pltpu.make_async_copy(pos_v, pos, l_sem.at[3])
    pos_copy.start()

    forward(1)

    take = 16
    pick_r = lax.broadcasted_iota(I32, (take, take * BLK), 0)
    pick_c = lax.broadcasted_iota(I32, (take, take * BLK), 1) // BLK
    averager = jnp.where(pick_r == pick_c, 1.0 / BLK, 0.0).astype(BF16)
    for t in range(2):
        to_x[t].wait_recv()
    for t in range(2):
        for i in range(BLOCKS // take):
            where = pl.ds(i * take, take)
            tokens = both[t, where].reshape(take * BLK, HD)
            mean = jnp.dot(averager, tokens, preferred_element_type=F32)
            mean_a[at.a, t, where] = mean.astype(BF16)
    own_out = pltpu.make_async_copy(both, own, l_sem.at[4])
    own_out.start()
    along_a = [
        remote(
            mean_a.at[at.a], mean_a.at[at.a], m_send.at[k - 1], m_recv.at[k - 1], at.dev_a(k)
        )
        for k in range(1, SIDE)
    ]
    start(along_a)
    for copy in along_a + need_along_a:
        copy.wait_recv()
    need_b[at.b] = jnp.max(need_a[...], axis=0)
    need_along_b = [
        remote(
            need_b.at[at.b], need_b.at[at.b], n_send.at[k + 2], n_recv.at[k + 2], at.dev_b(k)
        )
        for k in range(1, SIDE)
    ]
    start(need_along_b)
    for k in range(SIDE):
        mean_b[at.b, k] = mean_a[k]
    along_b = [
        remote(
            mean_b.at[at.b], mean_b.at[at.b], m_send.at[k + 2], m_recv.at[k + 2], at.dev_b(k)
        )
        for k in range(1, SIDE)
    ]
    start(along_b)
    for copy in along_b + need_along_b:
        copy.wait_recv()
    need[0, 0] = jnp.max(jnp.max(need_b[...], axis=0).astype(F32)).astype(I32)
    mean_out = [
        pltpu.make_async_copy(
            mean_b.at[n, m], means.at[m * at.stride_a + n * at.stride_b], l_sem.at[7 + n * SIDE + m]
        )
        for n in range(SIDE)
        for m in range(SIDE)
    ]
    start(mean_out)
    for copy in tables:
        copy.wait_recv()
    tab_copy = pltpu.make_async_copy(tab_in, tabs, l_sem.at[23])
    tab_copy.start()

    for t in range(2):
        gather[4 * t + 2].wait_recv()
        gather[4 * t + 3].wait_recv()
        passed[2 * t].wait_recv()
        passed[2 * t + 1].wait_recv()
    for copy in asked:
        copy.wait()
    for copy in own_row + mean_out + [own_q, later_q, pos_copy, own_out, tab_copy]:
        copy.wait()
    for copy in gather + passed + to_x + tables + along_a + along_b + need_along_a + need_along_b:
        copy.wait_send()


def spread(keys, values, queries, owner, local):
    vmem, hbm = pl.BlockSpec(memory_space=pltpu.VMEM), pl.BlockSpec(memory_space=pl.ANY)
    q_rows = queries.shape[0] // HEADS
    row_shape = (2, SIDE, BLOCKS, HALF, HD)
    own_shape = (2, BLOCKS, BLK, HD)
    mean_shape = (2, BLOCKS, HD)
    return pl.pallas_call(
        spread_kernel,
        out_shape=(
            jax.ShapeDtypeStruct(row_shape, BF16),
            jax.ShapeDtypeStruct(own_shape, BF16),
            jax.ShapeDtypeStruct((SIDE * SIDE,) + mean_shape, BF16),
            jax.ShapeDtypeStruct((HEADS, q_rows // 2, HD), BF16),
            jax.ShapeDtypeStruct((HEADS, q_rows // 2, HD), BF16),
            jax.ShapeDtypeStruct((SIDE, 8, LISTED), I32),
            jax.ShapeDtypeStruct((8, LISTED), I32),
            jax.ShapeDtypeStruct((1, 1), I32),
        ),
        in_specs=[hbm, hbm, hbm, vmem, vmem],
        out_specs=(hbm,) * 7 + (pl.BlockSpec(memory_space=pltpu.SMEM),),
        scratch_shapes=[
            pltpu.VMEM((2, BLOCKS, HALF * KVH, HD), BF16),
            pltpu.VMEM(queries.shape, BF16),
            pltpu.VMEM((2, BLOCKS, HALF, HD), BF16),
            pltpu.VMEM(own_shape, BF16),
            pltpu.VMEM((HEADS, q_rows, HD), BF16),
            pltpu.VMEM((SIDE, 8, LISTED), I32),
            pltpu.VMEM((SIDE, 8, LISTED), I32),
            pltpu.VMEM((8, LISTED), I32),
            pltpu.VMEM((SIDE, 8, LISTED), I32),
            pltpu.VMEM((SIDE, 8, LISTED), I32),
            pltpu.VMEM((SIDE,) + mean_shape, BF16),
            pltpu.VMEM((SIDE, SIDE) + mean_shape, BF16),
            DMA((5,)), DMA((2, 6)), DMA((2, 6)), DMA((HEADS - 1,)), DMA((HEADS - 1,)),
            DMA((3,)), DMA((3,)), DMA((6,)), DMA((6,)), DMA((6,)), DMA((6,)),
            DMA((2,)), DMA((2,)), DMA((25,)),
        ],
        compiler_params=pltpu.CompilerParams(
            collective_id=0, has_side_effects=True, vmem_limit_bytes=60 * MIB
        ),
        name="spread",
    )(keys, values, queries, owner, local)


def scores(left, right):
    return lax.dot_general(left, right, (((1,), (1,)), ((), ())), preferred_element_type=F32)


def pick_kernel(
    cap, tabs, pos, rows, own, means, q_first, q_later, out,
    row_k, row_v, both, mean, q, sendbuf, recv_k, recv_v, far, weights, base, q_mean, c_max, c_sum, c_val, o_st,
    in_sem, s_send, s_recv, x_send, x_recv, q_send, q_recv, o_sem,
):
    at = Place()
    row, recv = (row_k, row_v), (recv_k, recv_v)
    early, late = pl.ds(0, q.shape[1] // 2), pl.ds(q.shape[1] // 2, q.shape[1] // 2)
    loads = [pltpu.make_async_copy(rows.at[t], row[t], in_sem.at[t]) for t in range(2)]
    loads += [
        pltpu.make_async_copy(q_first, q.at[:, early], in_sem.at[2]),
        pltpu.make_async_copy(means, mean, in_sem.at[3]),
        pltpu.make_async_copy(own, both, in_sem.at[4]),
        pltpu.make_async_copy(q_later.at[at.head], q.at[at.head, late], in_sem.at[5]),
    ]
    start(loads)
    peers = [at.dev_b(k) for k in range(1, SIDE)] + [at.dev_head(k) for k in range(1, HEADS)]
    greet(peers)
    wait_greeted(peers)

    picks = [[], []]
    offsets = (2, 1, 3)

    def collect(t):
        blocks = row[t].reshape(SIDE * BLOCKS, HALF, HD)
        loads[t].wait()
        for n, k in enumerate(offsets):

            @pl.loop(0, cap // 4)
            def _(i, k=k):
                for u in range(4):
                    sendbuf[t, k - 1, i * 4 + u] = blocks[tabs[k, 0, i * 4 + u]]

            picks[t].append(
                remote(
                    sendbuf.at[t, k - 1], recv[t].at[at.b, pl.ds(0, cap)],
                    s_send.at[t, n], s_recv.at[t, n], at.dev_b(-k % SIDE),
                )
            )
            if t == 0:
                picks[t][-1].start()

        @pl.loop(0, MOST // 8)
        def _(i):
            for u in range(8):
                recv[t][at.b, i * 8 + u] = blocks[tabs[0, 0, i * 8 + u]]

    collect(0)
    asked = [
        remote(
            q_later.at[(at.head + k) % HEADS], q.at[at.head, late],
            q_send.at[k - 1], q_recv.at[k - 1], at.dev_head(k),
        )
        for k in range(1, HEADS)
    ]
    start(asked)
    collect(1)

    to_log2 = math.log2(math.e)
    scale = HD**-0.5 * to_log2
    which = lax.broadcasted_iota(I32, (8, ROWS), 0)
    column = lax.broadcasted_iota(I32, (8, ROWS), 1)
    parity = jnp.where(which == column % 2, 1.0 / BLK, 0.0).astype(BF16)
    for n in (2, 3, 5):
        loads[n].wait()
    for copy in asked:
        copy.wait_recv()
    per_owner = q.shape[1] // ROWS

    def q_rows(i):
        first = pl.multiple_of((i % per_owner) * ROWS, ROWS)
        return q[i // per_owner, pl.ds(first, ROWS)]

    @pl.loop(0, BLOCKS // 4)
    def _(i):
        for u in range(4):
            q_mean[i * 4 + u] = jnp.dot(parity, q_rows(i * 4 + u), preferred_element_type=F32)

    group = 8
    total_blocks = SIDE * SIDE * BLOCKS
    key_means = mean[:, 0].reshape(total_blocks, HD)
    value_means = mean[:, 1].reshape(total_blocks, HD)

    @pl.loop(0, BLOCKS // group)
    def _(i):
        where = pl.ds(i * group, group)
        means_f = q_mean[where].reshape(group * 8, HD)
        high = means_f.astype(BF16)
        rest = means_f - high.astype(F32)
        mid = rest.astype(BF16)
        low = (rest - mid.astype(F32)).astype(BF16)
        coarse = scores(high, key_means) + scores(mid, key_means) + scores(low, key_means)
        coarse = coarse * scale + math.log2(BLK)
        number = lax.broadcasted_iota(I32, (8, total_blocks), 1)
        kept = []
        for u in range(group):
            block = i * group + u
            gone = number == at.seq * BLOCKS + block
            for r in range(REFINE):
                gone = gone | (number == pos[2, r * BLOCKS + block])
            kept.append(jnp.where(gone, 0.0, 1.0))
        kept = jnp.concatenate(kept, axis=0) > 0.0
        coarse = jnp.where(kept, coarse, -1e30)
        top = jnp.max(coarse, axis=1, keepdims=True)
        part = jnp.where(kept, jnp.exp2(coarse - top), 0.0)
        c_max[where] = jnp.broadcast_to(top, (group * 8, HD)).reshape(group, 8, HD)
        total = jnp.sum(part, axis=1, keepdims=True)
        c_sum[where] = jnp.broadcast_to(total, (group * 8, HD)).reshape(group, 8, HD)
        value = jnp.dot(part.astype(BF16), value_means, preferred_element_type=F32)
        c_val[where] = value.reshape(group, 8, HD)

    for before, after in zip(*picks):
        before.wait_send()
        after.start()
    loads[4].wait()

    my_half = pl.ds(at.core * HALF, HALF)
    pieces, unroll = x_send.shape[1], 4
    piece, blocks_piece = LISTED // pieces, BLOCKS // pieces

    def to_sibling(t, p):
        ref = far.at[t, pl.ds(p * piece, piece), my_half]
        return remote(ref, ref, x_send.at[t, p], x_recv.at[t, p], at.sibling)

    def line_up(t):
        for copy in picks[t]:
            copy.wait_recv()

        @pl.loop(0, pieces)
        def _(p):
            @pl.loop(0, blocks_piece // 2)
            def _(j):
                for u in range(2):
                    for r in range(REFINE):
                        i = p * blocks_piece + j * 2 + u
                        place = pos[at.core, r * BLOCKS + i]
                        far[t, i * REFINE + r, my_half] = recv[t][place // LISTED, place % LISTED]

            to_sibling(t, p).start()

    def fine_blocks(t, i):
        listed = far[t, pl.ds(i * REFINE, REFINE)].reshape(REFINE * BLK, HD)
        return jnp.concatenate([both[t, i], listed], axis=0)

    odd = lax.broadcasted_iota(I32, (ROWS, 1), 0) % 2 == 1

    def per_row(ref, i, width):
        return jnp.where(odd, ref[i, 1:2, :width], ref[i, 0:1, :width])

    line_up(0)

    @pl.loop(0, pieces)
    def _(p):
        to_sibling(0, p).wait_recv()

        @pl.loop(0, blocks_piece // 8)
        def _(j):
            for u in range(8):
                i = p * blocks_piece + j * 8 + u
                fine = scores(q_rows(i), fine_blocks(0, i)) * scale
                coarse_top = per_row(c_max, i, 1)
                top = jnp.maximum(coarse_top, jnp.max(fine, axis=1, keepdims=True))
                fine = jnp.exp2(fine - top)
                alpha = jnp.exp2(coarse_top - top)
                total = alpha * per_row(c_sum, i, 1) + jnp.sum(fine, axis=1, keepdims=True)
                share = 1.0 / total
                weights[i] = (fine * share).astype(BF16)
                base[i] = (alpha * share) * per_row(c_val, i, HD)

    line_up(1)

    def to_out(p):
        where = pl.ds(p * blocks_piece, blocks_piece)
        return pltpu.make_async_copy(o_st.at[where], out.at[where], o_sem.at[p])

    @pl.loop(0, pieces)
    def _(p):
        to_sibling(1, p).wait_recv()

        @pl.loop(0, blocks_piece // unroll)
        def _(j):
            for u in range(unroll):
                i = p * blocks_piece + j * unroll + u
                result = jnp.dot(weights[i], fine_blocks(1, i), preferred_element_type=F32)
                o_st[i] = (result + base[i]).astype(BF16)

        to_out(p).start()

    @pl.loop(0, pieces)
    def _(p):
        to_out(p).wait()
        for t in range(2):
            to_sibling(t, p).wait_send()

    for copy in picks[1] + asked:
        copy.wait_send()


def pick(collective_id, cap, rows, own, means, q_first, q_later, tabs, pos):
    smem, hbm = pl.BlockSpec(memory_space=pltpu.SMEM), pl.BlockSpec(memory_space=pl.ANY)
    q_shape = (HEADS, 2 * q_first.shape[1], HD)
    return pl.pallas_call(
        functools.partial(pick_kernel, cap),
        out_shape=jax.ShapeDtypeStruct((BLOCKS, ROWS, HD), BF16),
        in_specs=[smem, smem, hbm, hbm, hbm, hbm, hbm],
        out_specs=hbm,
        scratch_shapes=[
            pltpu.VMEM(rows.shape[1:], BF16),
            pltpu.VMEM(rows.shape[1:], BF16),
            pltpu.VMEM(own.shape, BF16),
            pltpu.VMEM(means.shape, BF16),
            pltpu.VMEM(q_shape, BF16),
            pltpu.VMEM((2, SIDE - 1, cap, HALF, HD), BF16),
            pltpu.VMEM((SIDE, MOST, HALF, HD), BF16),
            pltpu.VMEM((SIDE, MOST, HALF, HD), BF16),
            pltpu.VMEM((2, LISTED, BLK, HD), BF16),
            pltpu.VMEM((BLOCKS, ROWS, (REFINE + 1) * BLK), BF16),
            pltpu.VMEM((BLOCKS, ROWS, HD), F32),
            pltpu.VMEM((BLOCKS, 8, HD), F32),
            pltpu.VMEM((BLOCKS, 8, HD), F32),
            pltpu.VMEM((BLOCKS, 8, HD), F32),
            pltpu.VMEM((BLOCKS, 8, HD), F32),
            pltpu.VMEM((BLOCKS, ROWS, HD), BF16),
            DMA((6,)), DMA((2, 3)), DMA((2, 3)), DMA((2, 4)), DMA((2, 4)),
            DMA((HEADS - 1,)), DMA((HEADS - 1,)), DMA((4,)),
        ],
        compiler_params=pltpu.CompilerParams(
            collective_id=collective_id, has_side_effects=True, vmem_limit_bytes=50 * MIB
        ),
        name="pick",
    )(tabs, pos, rows, own, means, q_first, q_later)


def hand_on_kernel(src, dst, held, in_sem, out_sem):
    parts = in_sem.shape[0]
    per = BLOCKS // parts
    where = [pl.ds(p * per, per) for p in range(parts)]
    inward = [
        pltpu.make_async_copy(src.at[w], held.at[w], in_sem.at[p]) for p, w in enumerate(where)
    ]
    outward = [
        pltpu.make_async_copy(held.at[w], dst.at[w], out_sem.at[p]) for p, w in enumerate(where)
    ]
    start(inward)
    for before, after in zip(inward, outward):
        before.wait()
        after.start()
    for copy in outward:
        copy.wait()


def hand_on(result):
    hbm = pl.BlockSpec(memory_space=pl.ANY)
    return pl.pallas_call(
        hand_on_kernel,
        out_shape=jax.ShapeDtypeStruct(result.shape, result.dtype),
        in_specs=[hbm],
        out_specs=hbm,
        scratch_shapes=[pltpu.VMEM(result.shape, result.dtype), DMA((8,)), DMA((8,))],
        compiler_params=pltpu.CompilerParams(vmem_limit_bytes=24 * MIB),
        name="hand_on",
    )(result)


def blank():
    def kernel(out):
        del out

    return pl.pallas_call(
        kernel,
        out_shape=jax.ShapeDtypeStruct((BLOCKS, ROWS, HD), BF16),
        out_specs=pl.BlockSpec(memory_space=pl.ANY),
        name="blank",
    )()


def on_device(queries, keys, values, refine_owner, refine_local):
    *moved, need = spread(
        keys.reshape(BLOCKS, BLK * KVH, HD),
        values.reshape(BLOCKS, BLK * KVH, HD),
        queries.reshape(-1, HD),
        refine_owner.T,
        refine_local.T,
    )
    caps = (40, 44, 52, MOST)
    most = need[0, 0]
    level = sum((most > cap).astype(I32) for cap in caps[:-1])

    def branch(n):
        return lambda *operands: hand_on(pick(n + 1, caps[n], *operands))

    out = blank()
    for n in range(len(caps)):
        run = branch(n)
        out = lax.fori_loop(0, (level == n).astype(I32), lambda _, kept: run(*moved), out)
    return out.reshape(BLOCKS * BLK, 2, HD)


def solution(mesh):
    return jax.shard_map(
        on_device,
        mesh=mesh,
        in_specs=(
            P(("seq", "head"), None, None),
            P("seq", None, None),
            P("seq", None, None),
            P("seq", None),
            P("seq", None),
        ),
        out_specs=P("seq", "head", None),
        check_vma=False,
    )
```

```python
import functools
import math

import jax
import jax.numpy as jnp
from jax import lax
from jax.experimental import pallas as pl
from jax.experimental.pallas import tpu as pltpu
from jax.sharding import PartitionSpec as P

MESH = pl.DeviceIdType.MESH
BLK = 128
HD = 128
KVH = 4
SIDE = 4
BLOCKS = 32
LISTED = 128
REFINE = 4
HEADS = 8
HALF = BLK // 2
MOST = 64
ROWS = 2 * BLK
MIB = 2**20
F32, BF16, I32 = jnp.float32, jnp.bfloat16, jnp.int32
DMA = pltpu.SemaphoreType.DMA


class Place:
    def __init__(self):
        self.seq, self.head = lax.axis_index("seq"), lax.axis_index("head")
        self.core = self.head % 2
        x, z = self.seq // SIDE, self.seq % SIDE
        self.a, self.b = x + self.core * (z - x), z + self.core * (x - z)
        self.stride_a, self.stride_b = SIDE - 3 * self.core, 1 + 3 * self.core
        self.sibling = (self.seq, self.head + 1 - 2 * self.core)

    def on_a(self, k):
        return (self.a + k) % SIDE

    def on_b(self, k):
        return (self.b + k) % SIDE

    def dev_a(self, k):
        return (self.on_a(k) * self.stride_a + self.b * self.stride_b, self.head)

    def dev_b(self, k):
        return (self.a * self.stride_a + self.on_b(k) * self.stride_b, self.head)

    def dev_head(self, k):
        return (self.seq, (self.head + k) % HEADS)


def remote(src, dst, send, recv, dev):
    return pltpu.make_async_remote_copy(
        src_ref=src, dst_ref=dst, send_sem=send, recv_sem=recv, device_id=dev, device_id_type=MESH
    )


def greet(peers):
    barrier = pltpu.get_barrier_semaphore()
    for dev in peers:
        pl.semaphore_signal(barrier, inc=1, device_id=dev, device_id_type=MESH)


def wait_greeted(peers):
    pl.semaphore_wait(pltpu.get_barrier_semaphore(), len(peers))


def start(copies):
    for copy in copies:
        copy.start()


def spread_kernel(
    keys, values, queries, owner, local,
    rows, own, means, q_out, q_later, tabs, pos, need,
    kv_in, q_in, half, both, q_st, tab_out, tab_in, pos_v, need_a, need_b, mean_a,
    in_sem, a_send, a_recv, q_send, q_recv, t_send, t_recv, n_send, n_recv, m_send, m_recv, x_send, x_recv, l_sem,
):
    at = Place()
    kv = at.head // 2
    parts = 2
    per = BLOCKS // parts
    loads = []
    for t, src in enumerate((keys, values)):
        for p in range(parts):
            where = pl.ds(p * per, per)
            loads.append(
                pltpu.make_async_copy(
                    src.at[where, pl.ds(at.core * (HALF * KVH), HALF * KVH)],
                    kv_in.at[t, where],
                    in_sem.at[t * parts + p],
                )
            )
    loads.append(pltpu.make_async_copy(queries, q_in, in_sem.at[2 * parts]))
    start(loads)
    peers = [at.dev_a(k) for k in range(1, SIDE)]
    peers += [at.dev_b(k) for k in range(1, SIDE)]
    peers += [at.dev_head(k) for k in range(1, HEADS)]
    greet(peers)

    lane = lax.broadcasted_iota(I32, (LISTED, LISTED), 1)
    sub = lax.broadcasted_iota(I32, (LISTED, LISTED), 0)

    def as_row(ref):
        return jnp.concatenate([ref[r : r + 1] for r in range(REFINE)], axis=1)

    def as_column(line):
        spot = jnp.where(lane == sub, line.astype(F32), 0.0)
        return jnp.sum(spot, axis=1, keepdims=True).astype(I32)

    ow_r, lo_r = as_row(owner), as_row(local)
    ow_c, lo_c = as_column(ow_r), as_column(lo_r)
    x_r, z_r = ow_r // SIDE, ow_r % SIDE
    x_c, z_c = ow_c // SIDE, ow_c % SIDE
    id_r, id_c = ow_r * BLOCKS + lo_r, ow_c * BLOCKS + lo_c
    twin = id_r == id_c

    def count(mask, axis):
        ones = jnp.where(mask, 1.0, 0.0).astype(F32)
        return jnp.sum(ones, axis=axis, keepdims=True).astype(I32)

    first_r = count(twin & (sub < lane), 0) == 0
    first_c = count(twin & (lane < sub), 1) == 0
    rank_z = count((z_c == z_r) & (lane < sub) & first_r, 1)
    rank_x = count((x_c == x_r) & (lane < sub) & first_r, 1)
    places = [
        group * LISTED
        + jnp.sum(jnp.where(twin & first_c, rank, 0), axis=0, keepdims=True)
        for group, rank in ((z_r, rank_z), (x_r, rank_x))
    ]
    rank_c = rank_z + at.core * (rank_x - rank_z)
    ac, bc = x_c + at.core * (z_c - x_c), z_c + at.core * (x_c - z_c)
    idx_c = ac * BLOCKS + lo_c
    for g in range(SIDE):
        wanted = first_c & (bc == g) & (rank_c == lane)
        table = jnp.sum(jnp.where(wanted, idx_c, 0), axis=0, keepdims=True)
        tab_out[g] = jnp.broadcast_to(table, (8, LISTED))
    line = lax.broadcasted_iota(I32, (8, LISTED), 0)
    pos_v[...] = jnp.where(line == 0, places[0], jnp.where(line == 1, places[1], id_r))
    most = jnp.zeros((1, 1), F32)
    for group, rank, here in ((x_c, rank_x, at.seq // SIDE), (z_c, rank_z, at.seq % SIDE)):
        wanted = jnp.where(first_c & (group != here), rank + 1, 0).astype(F32)
        most = jnp.maximum(most, jnp.max(wanted, axis=0, keepdims=True))
    need_a[at.a] = jnp.broadcast_to(most, (8, LISTED)).astype(I32)
    out_row = lax.broadcasted_iota(I32, (HALF, HALF * KVH), 0)
    in_row = lax.broadcasted_iota(I32, (HALF, HALF * KVH), 1)
    chooser = jnp.where(in_row == out_row * KVH + kv, 1.0, 0.0).astype(BF16)
    my_half = pl.ds(at.core * HALF, HALF)
    gather, to_x = [], []

    def choose(t, p):
        loads[t * parts + p].wait()

        @pl.loop(p * per // 4, (p + 1) * per // 4)
        def _(i):
            for u in range(4):
                picked = jnp.dot(chooser, kv_in[t, i * 4 + u], preferred_element_type=F32)
                picked = picked.astype(BF16)
                half[t, i * 4 + u] = picked
                both[t, i * 4 + u, my_half] = picked

    for t in range(2):
        for part, k, n in ((0, 1, 0), (1, 3, 2), (1, 1, 1), (0, 3, 3)):
            where = pl.ds(part * per, per)
            gather.append(
                remote(
                    half.at[t, where], rows.at[t, at.a, where],
                    a_send.at[t, n], a_recv.at[t, n], at.dev_a(k),
                )
            )
        to_x.append(
            remote(
                both.at[t, :, my_half], both.at[t, :, my_half],
                x_send.at[t], x_recv.at[t], at.sibling,
            )
        )
    wait_greeted(peers)
    tables = [
        remote(
            tab_out.at[at.on_b(k)], tab_in.at[k], t_send.at[k - 1], t_recv.at[k - 1], at.dev_b(k)
        )
        for k in range(1, SIDE)
    ]
    start(tables)

    need_along_a = [
        remote(
            need_a.at[at.a], need_a.at[at.a], n_send.at[k - 1], n_recv.at[k - 1], at.dev_a(k)
        )
        for k in range(1, SIDE)
    ]
    start(need_along_a)
    tab_in[0] = tab_out[at.b]
    pos_copy = pltpu.make_async_copy(pos_v, pos, l_sem.at[3])
    pos_copy.start()
    choose(0, 0)
    gather[0].start()
    choose(0, 1)
    gather[1].start()
    for copy in need_along_a:
        copy.wait_recv()
    need_b[at.b] = jnp.max(need_a[...], axis=0)
    need_along_b = [
        remote(
            need_b.at[at.b], need_b.at[at.b], n_send.at[k + 2], n_recv.at[k + 2], at.dev_b(k)
        )
        for k in range(1, SIDE)
    ]
    start(need_along_b)
    choose(1, 0)
    gather[4].start()
    choose(1, 1)
    gather[5].start()
    start(gather[2:4] + gather[6:8] + to_x)
    own_row = [pltpu.make_async_copy(half.at[t], rows.at[t, at.a], l_sem.at[t]) for t in range(2)]
    start(own_row)

    loads[-1].wait()
    step = 16
    out_row = lax.broadcasted_iota(I32, (16 * step, 16 * step), 0)
    in_row = lax.broadcasted_iota(I32, (16 * step, 16 * step), 1)
    pair, rest = out_row // (2 * step), out_row % (2 * step)
    order = jnp.where(in_row == (rest // 2) * 16 + pair * 2 + rest % 2, 1.0, 0.0).astype(BF16)
    chunks = q_in.shape[0] // (16 * step)

    def turn(low, high):
        @pl.loop(low // 2, high // 2)
        def _(i):
            for u in range(2):
                first = pl.multiple_of((i * 2 + u) * 16 * step, 16 * step)
                turned = jnp.dot(order, q_in[pl.ds(first, 16 * step)], preferred_element_type=F32)
                turned = turned.astype(BF16)
                place = pl.multiple_of((i * 2 + u) * 2 * step, 2 * step)
                for h in range(HEADS):
                    q_st[h, pl.ds(place, 2 * step)] = turned[h * 2 * step : (h + 1) * 2 * step]

    turn(0, chunks // 2)
    now = pl.ds(0, q_st.shape[1] // 2)
    asked = [
        remote(
            q_st.at[(at.head + k) % HEADS, now], q_out.at[at.head],
            q_send.at[k - 1], q_recv.at[k - 1], at.dev_head(k),
        )
        for k in range(1, HEADS)
    ]
    start(asked)
    own_q = pltpu.make_async_copy(q_st.at[at.head, now], q_out.at[at.head], l_sem.at[2])
    own_q.start()
    passed = []
    lower, upper = pl.ds(0, per), pl.ds(per, per)

    def forward(t):
        gather[4 * t].wait_recv()
        ref = rows.at[t, at.on_a(3), lower]
        passed.append(remote(ref, ref, a_send.at[t, 4], a_recv.at[t, 4], at.dev_a(1)))
        passed[-1].start()
        gather[4 * t + 1].wait_recv()
        ref = rows.at[t, at.on_a(1), upper]
        passed.append(remote(ref, ref, a_send.at[t, 5], a_recv.at[t, 5], at.dev_a(3)))
        passed[-1].start()

    forward(0)

    take = 16
    pick_r = lax.broadcasted_iota(I32, (take, take * BLK), 0)
    pick_c = lax.broadcasted_iota(I32, (take, take * BLK), 1) // BLK
    averager = jnp.where(pick_r == pick_c, 1.0 / BLK, 0.0).astype(BF16)
    for t in range(2):
        to_x[t].wait_recv()
    for t in range(2):
        for i in range(BLOCKS // take):
            where = pl.ds(i * take, take)
            tokens = both[t, where].reshape(take * BLK, HD)
            mean = jnp.dot(averager, tokens, preferred_element_type=F32)
            mean_a[t, where] = mean.astype(BF16)
    own_out = pltpu.make_async_copy(both, own, l_sem.at[4])
    own_out.start()
    along_a = [
        remote(
            mean_a, means.at[at.a], m_send.at[k - 1], m_recv.at[k - 1], at.dev_a(k)
        )
        for k in range(1, SIDE)
    ]
    start(along_a)
    mean_out = pltpu.make_async_copy(mean_a, means.at[at.a], l_sem.at[5])
    mean_out.start()

    forward(1)
    turn(chunks // 2, chunks)
    later = pl.ds(q_st.shape[1] // 2, q_st.shape[1] // 2)
    later_q = pltpu.make_async_copy(q_st.at[:, later], q_later, l_sem.at[6])
    later_q.start()

    for copy in need_along_b:
        copy.wait_recv()
    need[0, 0] = jnp.max(jnp.max(need_b[...], axis=0).astype(F32)).astype(I32)
    for copy in tables:
        copy.wait_recv()
    tab_copy = pltpu.make_async_copy(tab_in, tabs, l_sem.at[7])
    tab_copy.start()
    for copy in along_a:
        copy.wait_recv()

    for t in range(2):
        gather[4 * t + 2].wait_recv()
        gather[4 * t + 3].wait_recv()
        passed[2 * t].wait_recv()
        passed[2 * t + 1].wait_recv()
    for copy in asked:
        copy.wait()
    for copy in own_row + [own_q, later_q, pos_copy, own_out, tab_copy, mean_out]:
        copy.wait()
    for copy in gather + passed + to_x + tables + along_a + need_along_a + need_along_b:
        copy.wait_send()


def spread(keys, values, queries, owner, local):
    vmem, hbm = pl.BlockSpec(memory_space=pltpu.VMEM), pl.BlockSpec(memory_space=pl.ANY)
    q_rows = queries.shape[0] // HEADS
    row_shape = (2, SIDE, BLOCKS, HALF, HD)
    own_shape = (2, BLOCKS, BLK, HD)
    mean_shape = (2, BLOCKS, HD)
    return pl.pallas_call(
        spread_kernel,
        out_shape=(
            jax.ShapeDtypeStruct(row_shape, BF16),
            jax.ShapeDtypeStruct(own_shape, BF16),
            jax.ShapeDtypeStruct((SIDE,) + mean_shape, BF16),
            jax.ShapeDtypeStruct((HEADS, q_rows // 2, HD), BF16),
            jax.ShapeDtypeStruct((HEADS, q_rows // 2, HD), BF16),
            jax.ShapeDtypeStruct((SIDE, 8, LISTED), I32),
            jax.ShapeDtypeStruct((8, LISTED), I32),
            jax.ShapeDtypeStruct((1, 1), I32),
        ),
        in_specs=[hbm, hbm, hbm, vmem, vmem],
        out_specs=(hbm,) * 7 + (pl.BlockSpec(memory_space=pltpu.SMEM),),
        scratch_shapes=[
            pltpu.VMEM((2, BLOCKS, HALF * KVH, HD), BF16),
            pltpu.VMEM(queries.shape, BF16),
            pltpu.VMEM((2, BLOCKS, HALF, HD), BF16),
            pltpu.VMEM(own_shape, BF16),
            pltpu.VMEM((HEADS, q_rows, HD), BF16),
            pltpu.VMEM((SIDE, 8, LISTED), I32),
            pltpu.VMEM((SIDE, 8, LISTED), I32),
            pltpu.VMEM((8, LISTED), I32),
            pltpu.VMEM((SIDE, 8, LISTED), I32),
            pltpu.VMEM((SIDE, 8, LISTED), I32),
            pltpu.VMEM(mean_shape, BF16),
            DMA((5,)), DMA((2, 6)), DMA((2, 6)), DMA((HEADS - 1,)), DMA((HEADS - 1,)),
            DMA((3,)), DMA((3,)), DMA((6,)), DMA((6,)), DMA((3,)), DMA((3,)),
            DMA((2,)), DMA((2,)), DMA((8,)),
        ],
        compiler_params=pltpu.CompilerParams(
            collective_id=0, has_side_effects=True, vmem_limit_bytes=60 * MIB
        ),
        name="spread",
    )(keys, values, queries, owner, local)


def scores(left, right):
    return lax.dot_general(left, right, (((1,), (1,)), ((), ())), preferred_element_type=F32)


def pick_kernel(
    cap, tabs, pos, rows, own, means, q_first, q_later, out,
    row_k, row_v, both, mean, q, sendbuf, recv_k, recv_v, far, weights, base, q_mean, c_max, c_sum, c_val, o_st,
    in_sem, s_send, s_recv, x_send, x_recv, q_send, q_recv, m_send, m_recv, o_sem,
):
    at = Place()
    row, recv = (row_k, row_v), (recv_k, recv_v)
    early, late = pl.ds(0, q.shape[1] // 2), pl.ds(q.shape[1] // 2, q.shape[1] // 2)
    loads = [pltpu.make_async_copy(rows.at[t], row[t], in_sem.at[t]) for t in range(2)]
    loads += [
        pltpu.make_async_copy(q_first, q.at[:, early], in_sem.at[2]),
        pltpu.make_async_copy(means, mean.at[at.b], in_sem.at[3]),
        pltpu.make_async_copy(own, both, in_sem.at[4]),
        pltpu.make_async_copy(q_later.at[at.head], q.at[at.head, late], in_sem.at[5]),
    ]
    start(loads)
    peers = [at.dev_b(k) for k in range(1, SIDE)] + [at.dev_head(k) for k in range(1, HEADS)]
    greet(peers)
    wait_greeted(peers)
    mean_sends = [
        remote(means, mean.at[at.b], m_send.at[k - 1], m_recv.at[k - 1], at.dev_b(k))
        for k in range(1, SIDE)
    ]

    picks = [[], []]
    offsets = (2, 1, 3)

    def collect(t):
        blocks = row[t].reshape(SIDE * BLOCKS, HALF, HD)
        loads[t].wait()
        for n, k in enumerate(offsets):

            @pl.loop(0, cap // 4)
            def _(i, k=k):
                for u in range(4):
                    sendbuf[t, k - 1, i * 4 + u] = blocks[tabs[k, 0, i * 4 + u]]

            picks[t].append(
                remote(
                    sendbuf.at[t, k - 1], recv[t].at[at.b, pl.ds(0, cap)],
                    s_send.at[t, n], s_recv.at[t, n], at.dev_b(-k % SIDE),
                )
            )
            if t == 0:
                picks[t][-1].start()

        @pl.loop(0, MOST // 8)
        def _(i):
            for u in range(8):
                recv[t][at.b, i * 8 + u] = blocks[tabs[0, 0, i * 8 + u]]

    collect(0)
    asked = [
        remote(
            q_later.at[(at.head + k) % HEADS], q.at[at.head, late],
            q_send.at[k - 1], q_recv.at[k - 1], at.dev_head(k),
        )
        for k in range(1, HEADS)
    ]
    start(asked + mean_sends)
    collect(1)

    to_log2 = math.log2(math.e)
    scale = HD**-0.5 * to_log2
    which = lax.broadcasted_iota(I32, (8, ROWS), 0)
    column = lax.broadcasted_iota(I32, (8, ROWS), 1)
    parity = jnp.where(which == column % 2, 1.0 / BLK, 0.0).astype(BF16)
    for n in (2, 3, 5):
        loads[n].wait()
    for copy in asked:
        copy.wait_recv()
    per_owner = q.shape[1] // ROWS

    def q_rows(i):
        first = pl.multiple_of((i % per_owner) * ROWS, ROWS)
        return q[i // per_owner, pl.ds(first, ROWS)]

    @pl.loop(0, BLOCKS // 4)
    def _(i):
        for u in range(4):
            q_mean[i * 4 + u] = jnp.dot(parity, q_rows(i * 4 + u), preferred_element_type=F32)

    for before, after in zip(*picks):
        before.wait_send()
        after.start()
    loads[4].wait()

    my_half = pl.ds(at.core * HALF, HALF)
    pieces, unroll = x_send.shape[1], 4
    piece, blocks_piece = LISTED // pieces, BLOCKS // pieces

    def to_sibling(t, p):
        ref = far.at[t, pl.ds(p * piece, piece), my_half]
        return remote(ref, ref, x_send.at[t, p], x_recv.at[t, p], at.sibling)

    def line_up(t):
        for copy in picks[t]:
            copy.wait_recv()

        @pl.loop(0, pieces)
        def _(p):
            @pl.loop(0, blocks_piece // 2)
            def _(j):
                for u in range(2):
                    for r in range(REFINE):
                        i = p * blocks_piece + j * 2 + u
                        place = pos[at.core, r * BLOCKS + i]
                        far[t, i * REFINE + r, my_half] = recv[t][place // LISTED, place % LISTED]

            to_sibling(t, p).start()

    def fine_blocks(t, i):
        listed = far[t, pl.ds(i * REFINE, REFINE)].reshape(REFINE * BLK, HD)
        return jnp.concatenate([both[t, i], listed], axis=0)

    odd = lax.broadcasted_iota(I32, (ROWS, 1), 0) % 2 == 1

    def per_row(ref, i, width):
        return jnp.where(odd, ref[i, 1:2, :width], ref[i, 0:1, :width])

    line_up(0)
    for copy in mean_sends:
        copy.wait_recv()
    group = 8
    total_blocks = SIDE * SIDE * BLOCKS
    key_means = mean[:, :, 0].reshape(total_blocks, HD)
    value_means = mean[:, :, 1].reshape(total_blocks, HD)
    spot = lax.broadcasted_iota(I32, (8, total_blocks), 1)
    holder = (spot // BLOCKS % SIDE) * at.stride_a + spot // (SIDE * BLOCKS) * at.stride_b
    number = holder * BLOCKS + spot % BLOCKS

    @pl.loop(0, BLOCKS // group)
    def _(i):
        where = pl.ds(i * group, group)
        means_f = q_mean[where].reshape(group * 8, HD)
        high = means_f.astype(BF16)
        rest = means_f - high.astype(F32)
        mid = rest.astype(BF16)
        low = (rest - mid.astype(F32)).astype(BF16)
        coarse = scores(high, key_means) + scores(mid, key_means) + scores(low, key_means)
        coarse = coarse * scale + math.log2(BLK)
        kept = []
        for u in range(group):
            block = i * group + u
            gone = number == at.seq * BLOCKS + block
            for r in range(REFINE):
                gone = gone | (number == pos[2, r * BLOCKS + block])
            kept.append(jnp.where(gone, 0.0, 1.0))
        kept = jnp.concatenate(kept, axis=0) > 0.0
        coarse = jnp.where(kept, coarse, -1e30)
        top = jnp.max(coarse, axis=1, keepdims=True)
        part = jnp.where(kept, jnp.exp2(coarse - top), 0.0)
        c_max[where] = jnp.broadcast_to(top, (group * 8, HD)).reshape(group, 8, HD)
        total = jnp.sum(part, axis=1, keepdims=True)
        c_sum[where] = jnp.broadcast_to(total, (group * 8, HD)).reshape(group, 8, HD)
        value = jnp.dot(part.astype(BF16), value_means, preferred_element_type=F32)
        c_val[where] = value.reshape(group, 8, HD)

    @pl.loop(0, pieces)
    def _(p):
        to_sibling(0, p).wait_recv()

        @pl.loop(0, blocks_piece // 8)
        def _(j):
            for u in range(8):
                i = p * blocks_piece + j * 8 + u
                fine = scores(q_rows(i), fine_blocks(0, i)) * scale
                coarse_top = per_row(c_max, i, 1)
                top = jnp.maximum(coarse_top, jnp.max(fine, axis=1, keepdims=True))
                fine = jnp.exp2(fine - top)
                alpha = jnp.exp2(coarse_top - top)
                total = alpha * per_row(c_sum, i, 1) + jnp.sum(fine, axis=1, keepdims=True)
                share = 1.0 / total
                weights[i] = (fine * share).astype(BF16)
                base[i] = (alpha * share) * per_row(c_val, i, HD)

    line_up(1)

    def to_out(p):
        where = pl.ds(p * blocks_piece, blocks_piece)
        return pltpu.make_async_copy(o_st.at[where], out.at[where], o_sem.at[p])

    @pl.loop(0, pieces)
    def _(p):
        to_sibling(1, p).wait_recv()

        @pl.loop(0, blocks_piece // unroll)
        def _(j):
            for u in range(unroll):
                i = p * blocks_piece + j * unroll + u
                result = jnp.dot(weights[i], fine_blocks(1, i), preferred_element_type=F32)
                o_st[i] = (result + base[i]).astype(BF16)

        to_out(p).start()

    @pl.loop(0, pieces)
    def _(p):
        to_out(p).wait()
        for t in range(2):
            to_sibling(t, p).wait_send()

    for copy in picks[1] + asked + mean_sends:
        copy.wait_send()


def pick(collective_id, cap, rows, own, means, q_first, q_later, tabs, pos):
    smem, hbm = pl.BlockSpec(memory_space=pltpu.SMEM), pl.BlockSpec(memory_space=pl.ANY)
    q_shape = (HEADS, 2 * q_first.shape[1], HD)
    return pl.pallas_call(
        functools.partial(pick_kernel, cap),
        out_shape=jax.ShapeDtypeStruct((BLOCKS, ROWS, HD), BF16),
        in_specs=[smem, smem, hbm, hbm, hbm, hbm, hbm],
        out_specs=hbm,
        scratch_shapes=[
            pltpu.VMEM(rows.shape[1:], BF16),
            pltpu.VMEM(rows.shape[1:], BF16),
            pltpu.VMEM(own.shape, BF16),
            pltpu.VMEM((SIDE,) + means.shape, BF16),
            pltpu.VMEM(q_shape, BF16),
            pltpu.VMEM((2, SIDE - 1, cap, HALF, HD), BF16),
            pltpu.VMEM((SIDE, MOST, HALF, HD), BF16),
            pltpu.VMEM((SIDE, MOST, HALF, HD), BF16),
            pltpu.VMEM((2, LISTED, BLK, HD), BF16),
            pltpu.VMEM((BLOCKS, ROWS, (REFINE + 1) * BLK), BF16),
            pltpu.VMEM((BLOCKS, ROWS, HD), F32),
            pltpu.VMEM((BLOCKS, 8, HD), F32),
            pltpu.VMEM((BLOCKS, 8, HD), F32),
            pltpu.VMEM((BLOCKS, 8, HD), F32),
            pltpu.VMEM((BLOCKS, 8, HD), F32),
            pltpu.VMEM((BLOCKS, ROWS, HD), BF16),
            DMA((6,)), DMA((2, 3)), DMA((2, 3)), DMA((2, 4)), DMA((2, 4)),
            DMA((HEADS - 1,)), DMA((HEADS - 1,)), DMA((3,)), DMA((3,)), DMA((4,)),
        ],
        compiler_params=pltpu.CompilerParams(
            collective_id=collective_id, has_side_effects=True, vmem_limit_bytes=50 * MIB
        ),
        name="pick",
    )(tabs, pos, rows, own, means, q_first, q_later)


def hand_on_kernel(src, dst, held, in_sem, out_sem):
    parts = in_sem.shape[0]
    per = BLOCKS // parts
    where = [pl.ds(p * per, per) for p in range(parts)]
    inward = [
        pltpu.make_async_copy(src.at[w], held.at[w], in_sem.at[p]) for p, w in enumerate(where)
    ]
    outward = [
        pltpu.make_async_copy(held.at[w], dst.at[w], out_sem.at[p]) for p, w in enumerate(where)
    ]
    start(inward)
    for before, after in zip(inward, outward):
        before.wait()
        after.start()
    for copy in outward:
        copy.wait()


def hand_on(result):
    hbm = pl.BlockSpec(memory_space=pl.ANY)
    return pl.pallas_call(
        hand_on_kernel,
        out_shape=jax.ShapeDtypeStruct(result.shape, result.dtype),
        in_specs=[hbm],
        out_specs=hbm,
        scratch_shapes=[pltpu.VMEM(result.shape, result.dtype), DMA((8,)), DMA((8,))],
        compiler_params=pltpu.CompilerParams(vmem_limit_bytes=24 * MIB),
        name="hand_on",
    )(result)


def blank():
    def kernel(out):
        del out

    return pl.pallas_call(
        kernel,
        out_shape=jax.ShapeDtypeStruct((BLOCKS, ROWS, HD), BF16),
        out_specs=pl.BlockSpec(memory_space=pl.ANY),
        name="blank",
    )()


def on_device(queries, keys, values, refine_owner, refine_local):
    *moved, need = spread(
        keys.reshape(BLOCKS, BLK * KVH, HD),
        values.reshape(BLOCKS, BLK * KVH, HD),
        queries.reshape(-1, HD),
        refine_owner.T,
        refine_local.T,
    )
    caps = (40, 44, 52, MOST)
    most = need[0, 0]
    level = sum((most > cap).astype(I32) for cap in caps[:-1])

    def branch(n):
        return lambda *operands: hand_on(pick(n + 1, caps[n], *operands))

    out = blank()
    for n in range(len(caps)):
        run = branch(n)
        out = lax.fori_loop(0, (level == n).astype(I32), lambda _, kept: run(*moved), out)
    return out.reshape(BLOCKS * BLK, 2, HD)


def solution(mesh):
    return jax.shard_map(
        on_device,
        mesh=mesh,
        in_specs=(
            P(("seq", "head"), None, None),
            P("seq", None, None),
            P("seq", None, None),
            P("seq", None),
            P("seq", None),
        ),
        out_specs=P("seq", "head", None),
        check_vma=False,
    )
```

```python
import functools
import math

import jax
import jax.numpy as jnp
from jax import lax
from jax.experimental import pallas as pl
from jax.experimental.pallas import tpu as pltpu
from jax.sharding import PartitionSpec as P

MESH = pl.DeviceIdType.MESH
BLK = 128
HD = 128
KVH = 4
SIDE = 4
BLOCKS = 32
LISTED = 128
REFINE = 4
HEADS = 8
HALF = BLK // 2
MOST = 64
ROWS = 2 * BLK
MIB = 2**20
F32, BF16, I32 = jnp.float32, jnp.bfloat16, jnp.int32
DMA = pltpu.SemaphoreType.DMA


class Place:
    def __init__(self):
        self.seq, self.head = lax.axis_index("seq"), lax.axis_index("head")
        self.core = self.head % 2
        x, z = self.seq // SIDE, self.seq % SIDE
        self.a, self.b = x + self.core * (z - x), z + self.core * (x - z)
        self.stride_a, self.stride_b = SIDE - 3 * self.core, 1 + 3 * self.core
        self.sibling = (self.seq, self.head + 1 - 2 * self.core)

    def on_a(self, k):
        return (self.a + k) % SIDE

    def on_b(self, k):
        return (self.b + k) % SIDE

    def dev_a(self, k):
        return (self.on_a(k) * self.stride_a + self.b * self.stride_b, self.head)

    def dev_b(self, k):
        return (self.a * self.stride_a + self.on_b(k) * self.stride_b, self.head)

    def dev_head(self, k):
        return (self.seq, (self.head + k) % HEADS)


def remote(src, dst, send, recv, dev):
    return pltpu.make_async_remote_copy(
        src_ref=src, dst_ref=dst, send_sem=send, recv_sem=recv, device_id=dev, device_id_type=MESH
    )


def greet(peers):
    barrier = pltpu.get_barrier_semaphore()
    for dev in peers:
        pl.semaphore_signal(barrier, inc=1, device_id=dev, device_id_type=MESH)


def wait_greeted(peers):
    pl.semaphore_wait(pltpu.get_barrier_semaphore(), len(peers))


def start(copies):
    for copy in copies:
        copy.start()


def spread_kernel(
    keys, values, queries, owner, local,
    rows, own, means, q_out, q_later, tabs, pos, need,
    kv_in, q_in, half, both, q_st, tab_out, tab_in, pos_v, need_a, need_b, mean_a,
    in_sem, a_send, a_recv, q_send, q_recv, t_send, t_recv, n_send, n_recv, m_send, m_recv, x_send, x_recv, l_sem,
):
    at = Place()
    kv = at.head // 2
    parts = 2
    per = BLOCKS // parts
    loads = []
    for t, src in enumerate((keys, values)):
        for p in range(parts):
            where = pl.ds(p * per, per)
            loads.append(
                pltpu.make_async_copy(
                    src.at[where, pl.ds(at.core * (HALF * KVH), HALF * KVH)],
                    kv_in.at[t, where],
                    in_sem.at[t * parts + p],
                )
            )
    loads.append(pltpu.make_async_copy(queries, q_in, in_sem.at[2 * parts]))
    start(loads)
    peers = [at.dev_a(k) for k in range(1, SIDE)]
    peers += [at.dev_b(k) for k in range(1, SIDE)]
    peers += [at.dev_head(k) for k in range(1, HEADS)]
    greet(peers)

    lane = lax.broadcasted_iota(I32, (LISTED, LISTED), 1)
    sub = lax.broadcasted_iota(I32, (LISTED, LISTED), 0)

    def as_row(ref):
        return jnp.concatenate([ref[r : r + 1] for r in range(REFINE)], axis=1)

    def as_column(line):
        spot = jnp.where(lane == sub, line.astype(F32), 0.0)
        return jnp.sum(spot, axis=1, keepdims=True).astype(I32)

    ow_r, lo_r = as_row(owner), as_row(local)
    ow_c, lo_c = as_column(ow_r), as_column(lo_r)
    x_r, z_r = ow_r // SIDE, ow_r % SIDE
    x_c, z_c = ow_c // SIDE, ow_c % SIDE
    id_r, id_c = ow_r * BLOCKS + lo_r, ow_c * BLOCKS + lo_c
    twin = id_r == id_c

    def count(mask, axis):
        ones = jnp.where(mask, 1.0, 0.0).astype(F32)
        return jnp.sum(ones, axis=axis, keepdims=True).astype(I32)

    first_r = count(twin & (sub < lane), 0) == 0
    first_c = count(twin & (lane < sub), 1) == 0
    rank_z = count((z_c == z_r) & (lane < sub) & first_r, 1)
    rank_x = count((x_c == x_r) & (lane < sub) & first_r, 1)
    places = [
        group * LISTED
        + jnp.sum(jnp.where(twin & first_c, rank, 0), axis=0, keepdims=True)
        for group, rank in ((z_r, rank_z), (x_r, rank_x))
    ]
    rank_c = rank_z + at.core * (rank_x - rank_z)
    ac, bc = x_c + at.core * (z_c - x_c), z_c + at.core * (x_c - z_c)
    idx_c = ac * BLOCKS + lo_c
    for g in range(SIDE):
        wanted = first_c & (bc == g) & (rank_c == lane)
        table = jnp.sum(jnp.where(wanted, idx_c, 0), axis=0, keepdims=True)
        tab_out[g] = jnp.broadcast_to(table, (8, LISTED))
    line = lax.broadcasted_iota(I32, (8, LISTED), 0)
    pos_v[...] = jnp.where(line == 0, places[0], jnp.where(line == 1, places[1], id_r))
    most = jnp.zeros((1, 1), F32)
    for group, rank, here in ((x_c, rank_x, at.seq // SIDE), (z_c, rank_z, at.seq % SIDE)):
        wanted = jnp.where(first_c & (group != here), rank + 1, 0).astype(F32)
        most = jnp.maximum(most, jnp.max(wanted, axis=0, keepdims=True))
    need_a[at.a] = jnp.broadcast_to(most, (8, LISTED)).astype(I32)
    out_row = lax.broadcasted_iota(I32, (HALF, HALF * KVH), 0)
    in_row = lax.broadcasted_iota(I32, (HALF, HALF * KVH), 1)
    chooser = jnp.where(in_row == out_row * KVH + kv, 1.0, 0.0).astype(BF16)
    my_half = pl.ds(at.core * HALF, HALF)
    gather, to_x = [], []

    def choose(t, p):
        loads[t * parts + p].wait()

        @pl.loop(p * per // 4, (p + 1) * per // 4)
        def _(i):
            for u in range(4):
                picked = jnp.dot(chooser, kv_in[t, i * 4 + u], preferred_element_type=F32)
                picked = picked.astype(BF16)
                half[t, i * 4 + u] = picked
                both[t, i * 4 + u, my_half] = picked

    for t in range(2):
        for part, k, n in ((0, 1, 0), (1, 3, 2), (1, 1, 1), (0, 3, 3)):
            where = pl.ds(part * per, per)
            gather.append(
                remote(
                    half.at[t, where], rows.at[t, at.a, where],
                    a_send.at[t, n], a_recv.at[t, n], at.dev_a(k),
                )
            )
        to_x.append(
            remote(
                both.at[t, :, my_half], both.at[t, :, my_half],
                x_send.at[t], x_recv.at[t], at.sibling,
            )
        )
    wait_greeted(peers)
    tables = [
        remote(
            tab_out.at[at.on_b(k)], tab_in.at[k], t_send.at[k - 1], t_recv.at[k - 1], at.dev_b(k)
        )
        for k in range(1, SIDE)
    ]
    start(tables)

    need_along_a = [
        remote(
            need_a.at[at.a], need_a.at[at.a], n_send.at[k - 1], n_recv.at[k - 1], at.dev_a(k)
        )
        for k in range(1, SIDE)
    ]
    start(need_along_a)
    tab_in[0] = tab_out[at.b]
    pos_copy = pltpu.make_async_copy(pos_v, pos, l_sem.at[3])
    pos_copy.start()
    choose(0, 0)
    gather[0].start()
    choose(0, 1)
    gather[1].start()
    for copy in need_along_a:
        copy.wait_recv()
    need_b[at.b] = jnp.max(need_a[...], axis=0)
    need_along_b = [
        remote(
            need_b.at[at.b], need_b.at[at.b], n_send.at[k + 2], n_recv.at[k + 2], at.dev_b(k)
        )
        for k in range(1, SIDE)
    ]
    start(need_along_b)
    choose(1, 0)
    gather[4].start()
    choose(1, 1)
    gather[5].start()
    start(gather[2:4] + gather[6:8] + to_x)
    own_row = [pltpu.make_async_copy(half.at[t], rows.at[t, at.a], l_sem.at[t]) for t in range(2)]
    start(own_row)

    loads[-1].wait()
    step = 16
    out_row = lax.broadcasted_iota(I32, (16 * step, 16 * step), 0)
    in_row = lax.broadcasted_iota(I32, (16 * step, 16 * step), 1)
    pair, rest = out_row // (2 * step), out_row % (2 * step)
    order = jnp.where(in_row == (rest // 2) * 16 + pair * 2 + rest % 2, 1.0, 0.0).astype(BF16)
    chunks = q_in.shape[0] // (16 * step)

    def turn(low, high):
        @pl.loop(low // 2, high // 2)
        def _(i):
            for u in range(2):
                first = pl.multiple_of((i * 2 + u) * 16 * step, 16 * step)
                turned = jnp.dot(order, q_in[pl.ds(first, 16 * step)], preferred_element_type=F32)
                turned = turned.astype(BF16)
                place = pl.multiple_of((i * 2 + u) * 2 * step, 2 * step)
                for h in range(HEADS):
                    q_st[h, pl.ds(place, 2 * step)] = turned[h * 2 * step : (h + 1) * 2 * step]

    turn(0, chunks // 2)
    now = pl.ds(0, q_st.shape[1] // 2)
    asked = [
        remote(
            q_st.at[(at.head + k) % HEADS, now], q_out.at[at.head],
            q_send.at[k - 1], q_recv.at[k - 1], at.dev_head(k),
        )
        for k in range(1, HEADS)
    ]
    start(asked)
    own_q = pltpu.make_async_copy(q_st.at[at.head, now], q_out.at[at.head], l_sem.at[2])
    own_q.start()
    passed = []
    lower, upper = pl.ds(0, per), pl.ds(per, per)

    def forward(t):
        gather[4 * t].wait_recv()
        ref = rows.at[t, at.on_a(3), lower]
        passed.append(remote(ref, ref, a_send.at[t, 4], a_recv.at[t, 4], at.dev_a(1)))
        passed[-1].start()
        gather[4 * t + 1].wait_recv()
        ref = rows.at[t, at.on_a(1), upper]
        passed.append(remote(ref, ref, a_send.at[t, 5], a_recv.at[t, 5], at.dev_a(3)))
        passed[-1].start()

    forward(0)

    take = 16
    pick_r = lax.broadcasted_iota(I32, (take, take * BLK), 0)
    pick_c = lax.broadcasted_iota(I32, (take, take * BLK), 1) // BLK
    averager = jnp.where(pick_r == pick_c, 1.0 / BLK, 0.0).astype(BF16)
    for t in range(2):
        to_x[t].wait_recv()
    for t in range(2):
        for i in range(BLOCKS // take):
            where = pl.ds(i * take, take)
            tokens = both[t, where].reshape(take * BLK, HD)
            mean = jnp.dot(averager, tokens, preferred_element_type=F32)
            mean_a[t, where] = mean.astype(BF16)
    own_out = pltpu.make_async_copy(both, own, l_sem.at[4])
    own_out.start()
    along_a = [
        remote(
            mean_a, means.at[at.a], m_send.at[k - 1], m_recv.at[k - 1], at.dev_a(k)
        )
        for k in range(1, SIDE)
    ]
    start(along_a)
    mean_out = pltpu.make_async_copy(mean_a, means.at[at.a], l_sem.at[5])
    mean_out.start()

    forward(1)
    turn(chunks // 2, chunks)
    later = pl.ds(q_st.shape[1] // 2, q_st.shape[1] // 2)
    later_q = pltpu.make_async_copy(q_st.at[:, later], q_later, l_sem.at[6])
    later_q.start()

    for copy in need_along_b:
        copy.wait_recv()
    need[0, 0] = jnp.max(jnp.max(need_b[...], axis=0).astype(F32)).astype(I32)
    for copy in tables:
        copy.wait_recv()
    tab_copy = pltpu.make_async_copy(tab_in, tabs, l_sem.at[7])
    tab_copy.start()
    for copy in along_a:
        copy.wait_recv()

    for t in range(2):
        gather[4 * t + 2].wait_recv()
        gather[4 * t + 3].wait_recv()
        passed[2 * t].wait_recv()
        passed[2 * t + 1].wait_recv()
    for copy in asked:
        copy.wait()
    for copy in own_row + [own_q, later_q, pos_copy, own_out, tab_copy, mean_out]:
        copy.wait()
    for copy in gather + passed + to_x + tables + along_a + need_along_a + need_along_b:
        copy.wait_send()


def spread(keys, values, queries, owner, local):
    vmem, hbm = pl.BlockSpec(memory_space=pltpu.VMEM), pl.BlockSpec(memory_space=pl.ANY)
    q_rows = queries.shape[0] // HEADS
    row_shape = (2, SIDE, BLOCKS, HALF, HD)
    own_shape = (2, BLOCKS, BLK, HD)
    mean_shape = (2, BLOCKS, HD)
    return pl.pallas_call(
        spread_kernel,
        out_shape=(
            jax.ShapeDtypeStruct(row_shape, BF16),
            jax.ShapeDtypeStruct(own_shape, BF16),
            jax.ShapeDtypeStruct((SIDE,) + mean_shape, BF16),
            jax.ShapeDtypeStruct((HEADS, q_rows // 2, HD), BF16),
            jax.ShapeDtypeStruct((HEADS, q_rows // 2, HD), BF16),
            jax.ShapeDtypeStruct((SIDE, 8, LISTED), I32),
            jax.ShapeDtypeStruct((8, LISTED), I32),
            jax.ShapeDtypeStruct((1, 1), I32),
        ),
        in_specs=[hbm, hbm, hbm, vmem, vmem],
        out_specs=(hbm,) * 7 + (pl.BlockSpec(memory_space=pltpu.SMEM),),
        scratch_shapes=[
            pltpu.VMEM((2, BLOCKS, HALF * KVH, HD), BF16),
            pltpu.VMEM(queries.shape, BF16),
            pltpu.VMEM((2, BLOCKS, HALF, HD), BF16),
            pltpu.VMEM(own_shape, BF16),
            pltpu.VMEM((HEADS, q_rows, HD), BF16),
            pltpu.VMEM((SIDE, 8, LISTED), I32),
            pltpu.VMEM((SIDE, 8, LISTED), I32),
            pltpu.VMEM((8, LISTED), I32),
            pltpu.VMEM((SIDE, 8, LISTED), I32),
            pltpu.VMEM((SIDE, 8, LISTED), I32),
            pltpu.VMEM(mean_shape, BF16),
            DMA((5,)), DMA((2, 6)), DMA((2, 6)), DMA((HEADS - 1,)), DMA((HEADS - 1,)),
            DMA((3,)), DMA((3,)), DMA((6,)), DMA((6,)), DMA((3,)), DMA((3,)),
            DMA((2,)), DMA((2,)), DMA((8,)),
        ],
        compiler_params=pltpu.CompilerParams(
            collective_id=0, has_side_effects=True, vmem_limit_bytes=60 * MIB
        ),
        name="spread",
    )(keys, values, queries, owner, local)


def scores(left, right):
    return lax.dot_general(left, right, (((1,), (1,)), ((), ())), preferred_element_type=F32)


def pick_kernel(
    cap, tabs, pos, rows, own, means, q_first, q_later, out,
    row_k, row_v, both, mean, q, sendbuf, recv_k, recv_v, far, weights, base, q_mean, c_max, c_sum, c_val, o_st,
    in_sem, s_send, s_recv, x_send, x_recv, q_send, q_recv, m_send, m_recv, o_sem,
):
    at = Place()
    row, recv = (row_k, row_v), (recv_k, recv_v)
    early, late = pl.ds(0, q.shape[1] // 2), pl.ds(q.shape[1] // 2, q.shape[1] // 2)
    loads = [pltpu.make_async_copy(rows.at[t], row[t], in_sem.at[t]) for t in range(2)]
    loads += [
        pltpu.make_async_copy(q_first, q.at[:, early], in_sem.at[2]),
        pltpu.make_async_copy(means, mean.at[at.b], in_sem.at[3]),
        pltpu.make_async_copy(own, both, in_sem.at[4]),
        pltpu.make_async_copy(q_later.at[at.head], q.at[at.head, late], in_sem.at[5]),
    ]
    start(loads)
    peers = [at.dev_b(k) for k in range(1, SIDE)] + [at.dev_head(k) for k in range(1, HEADS)]
    greet(peers)
    wait_greeted(peers)
    mean_sends = [
        remote(means, mean.at[at.b], m_send.at[k - 1], m_recv.at[k - 1], at.dev_b(k))
        for k in range(1, SIDE)
    ]

    picks = [[], []]
    offsets = (2, 1, 3)

    def collect(t):
        blocks = row[t].reshape(SIDE * BLOCKS, HALF, HD)
        loads[t].wait()
        for n, k in enumerate(offsets):

            @pl.loop(0, cap // 2)
            def _(i, k=k):
                for u in range(2):
                    sendbuf[t, k - 1, i * 2 + u] = blocks[tabs[k, 0, i * 2 + u]]

            picks[t].append(
                remote(
                    sendbuf.at[t, k - 1], recv[t].at[at.b, pl.ds(0, cap)],
                    s_send.at[t, n], s_recv.at[t, n], at.dev_b(-k % SIDE),
                )
            )
            if t == 0:
                picks[t][-1].start()

        @pl.loop(0, MOST // 8)
        def _(i):
            for u in range(8):
                recv[t][at.b, i * 8 + u] = blocks[tabs[0, 0, i * 8 + u]]

    collect(0)
    asked = [
        remote(
            q_later.at[(at.head + k) % HEADS], q.at[at.head, late],
            q_send.at[k - 1], q_recv.at[k - 1], at.dev_head(k),
        )
        for k in range(1, HEADS)
    ]
    start(asked + mean_sends)
    collect(1)

    to_log2 = math.log2(math.e)
    scale = HD**-0.5 * to_log2
    which = lax.broadcasted_iota(I32, (8, ROWS), 0)
    column = lax.broadcasted_iota(I32, (8, ROWS), 1)
    parity = jnp.where(which == column % 2, 1.0 / BLK, 0.0).astype(BF16)
    for n in (2, 3, 5):
        loads[n].wait()
    for copy in asked:
        copy.wait_recv()
    per_owner = q.shape[1] // ROWS

    def q_rows(i):
        first = pl.multiple_of((i % per_owner) * ROWS, ROWS)
        return q[i // per_owner, pl.ds(first, ROWS)]

    @pl.loop(0, BLOCKS // 4)
    def _(i):
        for u in range(4):
            q_mean[i * 4 + u] = jnp.dot(parity, q_rows(i * 4 + u), preferred_element_type=F32)

    for before, after in zip(*picks):
        before.wait_send()
        after.start()
    loads[4].wait()

    my_half = pl.ds(at.core * HALF, HALF)
    pieces = x_send.shape[1]
    piece, blocks_piece = LISTED // pieces, BLOCKS // pieces

    def to_sibling(t, p):
        ref = far.at[t, pl.ds(p * piece, piece), my_half]
        return remote(ref, ref, x_send.at[t, p], x_recv.at[t, p], at.sibling)

    def line_up(t):
        for copy in picks[t]:
            copy.wait_recv()

        @pl.loop(0, pieces)
        def _(p):
            @pl.loop(0, blocks_piece // 4)
            def _(j):
                for u in range(4):
                    for r in range(REFINE):
                        i = p * blocks_piece + j * 4 + u
                        place = pos[at.core, r * BLOCKS + i]
                        far[t, i * REFINE + r, my_half] = recv[t][place // LISTED, place % LISTED]

            to_sibling(t, p).start()

    def fine_blocks(t, i):
        listed = far[t, pl.ds(i * REFINE, REFINE)].reshape(REFINE * BLK, HD)
        return jnp.concatenate([both[t, i], listed], axis=0)

    odd = lax.broadcasted_iota(I32, (ROWS, 1), 0) % 2 == 1

    def per_row(ref, i, width):
        return jnp.where(odd, ref[i, 1:2, :width], ref[i, 0:1, :width])

    line_up(0)
    for copy in mean_sends:
        copy.wait_recv()
    group = 8
    total_blocks = SIDE * SIDE * BLOCKS
    key_means = mean[:, :, 0].reshape(total_blocks, HD)
    value_means = mean[:, :, 1].reshape(total_blocks, HD)
    spot = lax.broadcasted_iota(I32, (8, total_blocks), 1)
    holder = (spot // BLOCKS % SIDE) * at.stride_a + spot // (SIDE * BLOCKS) * at.stride_b
    number = holder * BLOCKS + spot % BLOCKS

    @pl.loop(0, BLOCKS // group)
    def _(i):
        where = pl.ds(i * group, group)
        means_f = q_mean[where].reshape(group * 8, HD)
        high = means_f.astype(BF16)
        rest = means_f - high.astype(F32)
        mid = rest.astype(BF16)
        low = (rest - mid.astype(F32)).astype(BF16)
        coarse = scores(high, key_means) + scores(mid, key_means) + scores(low, key_means)
        coarse = coarse * scale + math.log2(BLK)
        kept = []
        for u in range(group):
            block = i * group + u
            gone = number == at.seq * BLOCKS + block
            for r in range(REFINE):
                gone = gone | (number == pos[2, r * BLOCKS + block])
            kept.append(jnp.where(gone, 0.0, 1.0))
        kept = jnp.concatenate(kept, axis=0) > 0.0
        coarse = jnp.where(kept, coarse, -1e30)
        top = jnp.max(coarse, axis=1, keepdims=True)
        part = jnp.where(kept, jnp.exp2(coarse - top), 0.0)
        c_max[where] = jnp.broadcast_to(top, (group * 8, HD)).reshape(group, 8, HD)
        total = jnp.sum(part, axis=1, keepdims=True)
        c_sum[where] = jnp.broadcast_to(total, (group * 8, HD)).reshape(group, 8, HD)
        value = jnp.dot(part.astype(BF16), value_means, preferred_element_type=F32)
        c_val[where] = value.reshape(group, 8, HD)

    @pl.loop(0, pieces)
    def _(p):
        to_sibling(0, p).wait_recv()

        @pl.loop(0, blocks_piece // 8)
        def _(j):
            for u in range(8):
                i = p * blocks_piece + j * 8 + u
                fine = scores(q_rows(i), fine_blocks(0, i)) * scale
                coarse_top = per_row(c_max, i, 1)
                top = jnp.maximum(coarse_top, jnp.max(fine, axis=1, keepdims=True))
                fine = jnp.exp2(fine - top)
                alpha = jnp.exp2(coarse_top - top)
                total = alpha * per_row(c_sum, i, 1) + jnp.sum(fine, axis=1, keepdims=True)
                share = 1.0 / total
                weights[i] = (fine * share).astype(BF16)
                base[i] = (alpha * share) * per_row(c_val, i, HD)

    line_up(1)

    def to_out(p):
        where = pl.ds(p * blocks_piece, blocks_piece)
        return pltpu.make_async_copy(o_st.at[where], out.at[where], o_sem.at[p])

    @pl.loop(0, pieces)
    def _(p):
        to_sibling(1, p).wait_recv()

        @pl.loop(0, blocks_piece // 8)
        def _(j):
            for u in range(8):
                i = p * blocks_piece + j * 8 + u
                result = jnp.dot(weights[i], fine_blocks(1, i), preferred_element_type=F32)
                o_st[i] = (result + base[i]).astype(BF16)

        to_out(p).start()

    @pl.loop(0, pieces)
    def _(p):
        to_out(p).wait()
        for t in range(2):
            to_sibling(t, p).wait_send()

    for copy in picks[1] + asked + mean_sends:
        copy.wait_send()


def pick(collective_id, cap, rows, own, means, q_first, q_later, tabs, pos):
    smem, hbm = pl.BlockSpec(memory_space=pltpu.SMEM), pl.BlockSpec(memory_space=pl.ANY)
    q_shape = (HEADS, 2 * q_first.shape[1], HD)
    return pl.pallas_call(
        functools.partial(pick_kernel, cap),
        out_shape=jax.ShapeDtypeStruct((BLOCKS, ROWS, HD), BF16),
        in_specs=[smem, smem, hbm, hbm, hbm, hbm, hbm],
        out_specs=hbm,
        scratch_shapes=[
            pltpu.VMEM(rows.shape[1:], BF16),
            pltpu.VMEM(rows.shape[1:], BF16),
            pltpu.VMEM(own.shape, BF16),
            pltpu.VMEM((SIDE,) + means.shape, BF16),
            pltpu.VMEM(q_shape, BF16),
            pltpu.VMEM((2, SIDE - 1, cap, HALF, HD), BF16),
            pltpu.VMEM((SIDE, MOST, HALF, HD), BF16),
            pltpu.VMEM((SIDE, MOST, HALF, HD), BF16),
            pltpu.VMEM((2, LISTED, BLK, HD), BF16),
            pltpu.VMEM((BLOCKS, ROWS, (REFINE + 1) * BLK), BF16),
            pltpu.VMEM((BLOCKS, ROWS, HD), F32),
            pltpu.VMEM((BLOCKS, 8, HD), F32),
            pltpu.VMEM((BLOCKS, 8, HD), F32),
            pltpu.VMEM((BLOCKS, 8, HD), F32),
            pltpu.VMEM((BLOCKS, 8, HD), F32),
            pltpu.VMEM((BLOCKS, ROWS, HD), BF16),
            DMA((6,)), DMA((2, 3)), DMA((2, 3)), DMA((2, 4)), DMA((2, 4)),
            DMA((HEADS - 1,)), DMA((HEADS - 1,)), DMA((3,)), DMA((3,)), DMA((4,)),
        ],
        compiler_params=pltpu.CompilerParams(
            collective_id=collective_id, has_side_effects=True, vmem_limit_bytes=50 * MIB
        ),
        name="pick",
    )(tabs, pos, rows, own, means, q_first, q_later)


def hand_on_kernel(src, dst, held, in_sem, out_sem):
    parts = in_sem.shape[0]
    per = BLOCKS // parts
    where = [pl.ds(p * per, per) for p in range(parts)]
    inward = [
        pltpu.make_async_copy(src.at[w], held.at[w], in_sem.at[p]) for p, w in enumerate(where)
    ]
    outward = [
        pltpu.make_async_copy(held.at[w], dst.at[w], out_sem.at[p]) for p, w in enumerate(where)
    ]
    start(inward)
    for before, after in zip(inward, outward):
        before.wait()
        after.start()
    for copy in outward:
        copy.wait()


def hand_on(result):
    hbm = pl.BlockSpec(memory_space=pl.ANY)
    return pl.pallas_call(
        hand_on_kernel,
        out_shape=jax.ShapeDtypeStruct(result.shape, result.dtype),
        in_specs=[hbm],
        out_specs=hbm,
        scratch_shapes=[pltpu.VMEM(result.shape, result.dtype), DMA((8,)), DMA((8,))],
        compiler_params=pltpu.CompilerParams(vmem_limit_bytes=24 * MIB),
        name="hand_on",
    )(result)


def blank():
    def kernel(out):
        del out

    return pl.pallas_call(
        kernel,
        out_shape=jax.ShapeDtypeStruct((BLOCKS, ROWS, HD), BF16),
        out_specs=pl.BlockSpec(memory_space=pl.ANY),
        name="blank",
    )()


def on_device(queries, keys, values, refine_owner, refine_local):
    *moved, need = spread(
        keys.reshape(BLOCKS, BLK * KVH, HD),
        values.reshape(BLOCKS, BLK * KVH, HD),
        queries.reshape(-1, HD),
        refine_owner.T,
        refine_local.T,
    )
    caps = (38, 42, 46, 50, MOST)
    most = need[0, 0]
    level = sum((most > cap).astype(I32) for cap in caps[:-1])

    def branch(n):
        return lambda *operands: hand_on(pick(n + 1, caps[n], *operands))

    out = blank()
    for n in range(len(caps)):
        run = branch(n)
        out = lax.fori_loop(0, (level == n).astype(I32), lambda _, kept: run(*moved), out)
    return out.reshape(BLOCKS * BLK, 2, HD)


def solution(mesh):
    return jax.shard_map(
        on_device,
        mesh=mesh,
        in_specs=(
            P(("seq", "head"), None, None),
            P("seq", None, None),
            P("seq", None, None),
            P("seq", None),
            P("seq", None),
        ),
        out_specs=P("seq", "head", None),
        check_vma=False,
    )
```
